32 devices in a mesh: dp: 16 (over z, x, core), tensor: 2 (over y).
Axes of the slice: x: 2, y: 2, z: 4, core: 2. Of those that a mesh axis runs over, the one named last changes fastest.
Arguments:
- tokens: bfloat16 [6272, 768], P('dp'), may hold values from -6 to 6
- body_mask: int32 [32, 196], P('dp'), may hold values from 0 to 1, as said below
- ln1_gain: float32 [768], replicated, may hold values from 0.5 to 1.5
- ln1_bias: float32 [768], replicated, may hold values from -1.75 to 1.75
- w_qkv: bfloat16 [768, 3, 768], P(None, None, 'tensor'), may hold values from -0.21875 to 0.21875
- b_q: float32 [768], P('tensor'), may hold values from -3 to 3
- b_v: float32 [768], P('tensor'), may hold values from -3 to 3
- w_out: bfloat16 [768, 768], P('tensor'), may hold values from -0.875 to 0.875
- b_out: float32 [768], replicated, may hold values from -3 to 3
- ln2_gain: float32 [768], replicated, may hold values from 0.5 to 1.5
- ln2_bias: float32 [768], replicated, may hold values from -1.75 to 1.75
- w_up: bfloat16 [768, 3072], P(None, 'tensor'), may hold values from -0.21875 to 0.21875
- b_up: float32 [3072], P('tensor'), may hold values from -3 to 3
- w_down: bfloat16 [3072, 768], P('tensor'), may hold values from -0.109375 to 0.109375
- b_down: float32 [768], replicated, may hold values from -3 to 3
- cotangent: bfloat16 [6272, 768], P('dp'), may hold values from -6 to 6
Outputs:
- block_out: float32 [6272, 768], P('dp')
- grad_tokens: float32 [6272, 768], P('dp')
- grad_ln1_gain: float32 [768], replicated
- grad_ln1_bias: float32 [768], replicated
- grad_w_qkv: float32 [768, 3, 768], P('dp', None, 'tensor')
- grad_b_q: float32 [768], P('tensor')
- grad_b_v: float32 [768], P('tensor')
- grad_w_out: float32 [768, 768], P('tensor', 'dp')
- grad_b_out: float32 [768], replicated
- grad_ln2_gain: float32 [768], replicated
- grad_ln2_bias: float32 [768], replicated
- grad_w_up: float32 [768, 3072], P('dp', 'tensor')
- grad_b_up: float32 [3072], P('tensor')
- grad_w_down: float32 [3072, 768], P('tensor', 'dp')
- grad_b_down: float32 [768], replicated
The draws below stay inside these ranges and needn't reach their ends.
Inputs may be any that keep to these rules, and one draw needn't show every extreme that they name: `body_mask`: every slice has at least an eighth of its 196 tokens (rounded down) flagged 1; the number of flagged tokens differs widely from slice to slice.
All inputs are finite; a program needn't handle non-finite values.
Results may differ from the reference program's by a relative error of at most 0.015.
Values may be sent and summed in bfloat16 or wider, within the bound.
No kernel may reach another device: no remote copies, remote signals or barrier semaphores. Data moves between devices by JAX's collectives and lax.ppermute only.
A program may use at most 128 MiB of HBM per device.

```python
import math
import jax
import jax.numpy as jnp
from jax import lax

D = 768
HD = 64
FF = 3072
SEQ = 196
SEQ_DEV = 2
SLICES = 32
TOKENS = 6272


def draw_body_mask(key, part):
    key = jax.random.fold_in(key, 7)
    count_key, order_key = jax.random.split(key)
    valid_counts = jax.random.randint(count_key, (SLICES, 1), SEQ // 8, SEQ + 1)

    def ranked(single_key):
        return jax.random.permutation(single_key, SEQ)
    ranks = jax.vmap(ranked)(jax.random.split(order_key, SLICES))
    return (ranks < valid_counts).astype(jnp.int32)


def strengthened(drawn, stream_key, source, target, shards_of, factor):
    owner, partner = [(jnp.arange(drawn.shape[dim]) // (drawn.shape[dim] // shards_of)).reshape([-1 if axis == dim else 1 for axis in range(drawn.ndim)]) for dim in (source, target)]
    chosen = jax.random.permutation(stream_key, shards_of)[partner]
    strong = (owner == chosen) | (owner == (partner + shards_of // 2) % shards_of)
    return jnp.where(strong, factor * drawn, drawn)


def level_of(own_key, shape, cuts, least, top_value):
    gain, own = 1.0, jax.random.fold_in(own_key, 6)
    for dim, blocks in cuts:
        heights = jnp.exp(jax.random.uniform(jax.random.fold_in(own, dim), (blocks,), jnp.float32, least / len(cuts), top_value / len(cuts)))
        gain = gain * jnp.repeat(heights, shape[dim] // blocks).reshape([-1 if axis == dim else 1 for axis in range(len(shape))])
    return gain


def normal_values(rng, dims, scale, limit, shards=(), held_as=jnp.bfloat16):
    entries = jax.random.normal(rng, dims, jnp.float32) * scale
    if len(shards) > 0:
        entries = level_of(rng, dims, shards, -0.22, 0.18) * entries
    return jnp.clip(entries, min=-limit, max=limit).astype(held_as)


def heavy_noise(stream_key, dims, scale, reach, shards, heavy, held_as=jnp.bfloat16):
    array = scale * jax.random.normal(stream_key, dims, jnp.float32)
    if shards:
        array = array * level_of(stream_key, dims, shards, -0.22, 0.18)
    return jnp.clip(strengthened(array, jax.random.fold_in(stream_key, 3), *heavy), -reach, reach).astype(held_as)


def setup_inputs(seed: int = 0) -> dict:
    seeds = jax.random.split(jax.random.key(seed), 17)
    tokens = heavy_noise(seeds[0], (TOKENS, D), 1.0, 6.0, ((0, 16),), (0, 1, 16, 2.0))
    body_mask = draw_body_mask(jax.random.fold_in(seeds[16], 71), 0)
    ln1_gain = jnp.clip(1.0 + 0.1 * jax.random.normal(seeds[2], (D,), jnp.float32), 0.5, 1.5)
    ln1_bias = normal_values(seeds[3], (D,), 0.3, 1.75, (), jnp.float32)
    w_qkv = normal_values(seeds[4], (D, 3, D), D ** -0.5, 0.21875, ((2, 2),))
    b_q = normal_values(seeds[5], (D,), 0.5, 3.0, ((0, 2),), jnp.float32)
    b_v = normal_values(seeds[6], (D,), 0.5, 3.0, ((0, 2),), jnp.float32)
    w_out = normal_values(seeds[7], (D, D), (D // 16) ** -0.5, 0.875, ((0, 2),))
    b_out = normal_values(seeds[8], (D,), 0.5, 3.0, (), jnp.float32)
    ln2_gain = jnp.clip(1.0 + 0.1 * jax.random.normal(seeds[9], (D,), jnp.float32), 0.5, 1.5)
    ln2_bias = normal_values(seeds[10], (D,), 0.3, 1.75, (), jnp.float32)
    w_up = normal_values(seeds[11], (D, FF), D ** -0.5, 0.21875, ((1, 2),))
    b_up = normal_values(seeds[12], (FF,), 0.5, 3.0, ((0, 2),), jnp.float32)
    w_down = normal_values(seeds[13], (FF, D), FF ** -0.5, 0.109375, ((0, 2),))
    b_down = normal_values(seeds[14], (D,), 0.5, 3.0, (), jnp.float32)
    cotangent = heavy_noise(seeds[15], (TOKENS, D), 1.0, 6.0, ((0, 16),), (0, 1, 16, 2.0))
    return {"tokens": tokens, "body_mask": body_mask, "ln1_gain": ln1_gain, "ln1_bias": ln1_bias, "w_qkv": w_qkv, "b_q": b_q, "b_v": b_v, "w_out": w_out, "b_out": b_out, "ln2_gain": ln2_gain, "ln2_bias": ln2_bias, "w_up": w_up, "b_up": b_up, "w_down": w_down, "b_down": b_down, "cotangent": cotangent}


@jax.custom_vjp
def low(v):
    return lax.optimization_barrier(v.astype(jnp.bfloat16)).astype(jnp.float32)

@jax.custom_vjp
def low_back(v):
    return v

def low_keep(v):
    return (low(v), None)

def low_pass(kept, grad):
    return (grad,)

def back_keep(v):
    return (v, None)

def back_low(kept, grad):
    return (low(grad),)
low.defvjp(low_keep, low_pass)
low_back.defvjp(back_keep, back_low)

def layer_norm(source, gain_vec, bias_vec):
    center = source - lax.optimization_barrier(jnp.mean(source, axis=-1, keepdims=True))
    spread = lax.optimization_barrier(jnp.mean(center * center, axis=-1, keepdims=True))
    return center * lax.rsqrt(spread + 1e-06) * gain_vec + bias_vec

def matmul(left_side, right_side):
    return jnp.dot(left_side, right_side, precision=lax.Precision.HIGHEST)

def block_forward(weights_all, slice_tokens, slice_mask):
    ln1_gain, ln1_bias, w_qkv, b_q, b_v, w_out, b_out, ln2_gain, ln2_bias, w_up, b_up, w_down, b_down = weights_all
    slice_count, seq_length, model_width = slice_tokens.shape
    head_count = model_width // HD
    token_rows = slice_tokens.reshape(slice_count * seq_length, model_width)
    normed = low(layer_norm(token_rows, ln1_gain, ln1_bias))
    queries = low_back(low(matmul(normed, w_qkv[:, 0, :]) + b_q))
    key_rows = low_back(low(matmul(normed, w_qkv[:, 1, :])))
    valued = low_back(low(matmul(normed, w_qkv[:, 2, :]) + b_v))

    def to_heads(flat_rows):
        return flat_rows.reshape(slice_count, seq_length, head_count, HD)
    scores = jnp.einsum('sqhe,skhe->shqk', to_heads(queries), to_heads(key_rows), precision=lax.Precision.HIGHEST) * (1.0 / math.sqrt(HD))
    scores = low_back(scores)
    scores = jnp.where(slice_mask[:, None, None, :] > 0, scores, -1e+30)
    row_max = lax.optimization_barrier(jnp.max(scores, axis=-1, keepdims=True))
    exp_scores = jnp.exp(scores - row_max)
    softmax_rows = low(exp_scores / lax.optimization_barrier(jnp.sum(exp_scores, axis=-1, keepdims=True)))
    mixed_rows = jnp.einsum('shqk,skhe->sqhe', softmax_rows, to_heads(valued), precision=lax.Precision.HIGHEST).reshape(slice_count * seq_length, model_width)
    mixed_rows = low_back(low(mixed_rows))
    hidden = token_rows + low_back(matmul(mixed_rows, w_out)) + b_out
    normed2 = low(layer_norm(hidden, ln2_gain, ln2_bias))
    upper_rows = low_back(matmul(normed2, w_up)) + b_up
    active = low(jax.nn.gelu(upper_rows, approximate=False))
    result = hidden + matmul(active, w_down) + b_down
    return result.reshape(slice_count, seq_length, model_width)

def reference(tokens, body_mask, ln1_gain, ln1_bias, w_qkv, b_q, b_v, w_out, b_out, ln2_gain, ln2_bias, w_up, b_up, w_down, b_down, cotangent):
    weights_all = tuple((item.astype(jnp.float32) for item in (ln1_gain, ln1_bias, w_qkv, b_q, b_v, w_out, b_out, ln2_gain, ln2_bias, w_up, b_up, w_down, b_down)))
    group_size = 4 * SEQ_DEV
    group_steps = SLICES // group_size
    token_groups = tokens.astype(jnp.float32).reshape(group_steps, group_size, SEQ, D)
    mask_groups = body_mask.reshape(group_steps, group_size, SEQ)
    cot_groups = cotangent.astype(jnp.float32).reshape(group_steps, group_size, SEQ, D)

    def one_group(grad_totals, scan_item):
        slice_tokens, slice_mask, slice_cots = scan_item

        def forward_only(weight_set, token_set):
            return block_forward(weight_set, token_set, slice_mask)
        result, pullback = jax.vjp(forward_only, weights_all, slice_tokens)
        weight_grads, token_grads = pullback(slice_cots)
        return (jax.tree.map(jnp.add, grad_totals, weight_grads), (result, token_grads))
    start_totals = jax.tree.map(jnp.zeros_like, weights_all)
    grad_totals, (results, token_grads) = lax.scan(one_group, start_totals, (token_groups, mask_groups, cot_groups))
    return (results.reshape(TOKENS, D), token_grads.reshape(TOKENS, D), grad_totals[0], grad_totals[1], grad_totals[2], grad_totals[3], grad_totals[4], grad_totals[5], grad_totals[6], grad_totals[7], grad_totals[8], grad_totals[9], grad_totals[10], grad_totals[11], grad_totals[12])
```

```python
import math
from functools import partial

import jax
import jax.numpy as jnp
from jax import lax
from jax.experimental import pallas as pl
from jax.experimental.pallas import tpu as pltpu
from jax.sharding import PartitionSpec as P

HD = 64
LANES = 128
ROW_TILE = 16
F32 = jnp.float32
BF16 = jnp.bfloat16
VMEM_LIMIT = 48 * 1024 * 1024

NN = (((1,), (0,)), ((), ()))
NT = (((1,), (1,)), ((), ()))
TN = (((0,), (0,)), ((), ()))


def mm(left, right, dims=NN):
    return lax.dot_general(left, right, dims, preferred_element_type=F32)


def unit_of(source):
    center = source - jnp.mean(source, axis=-1, keepdims=True)
    scaled = lax.rsqrt(jnp.mean(center * center, axis=-1, keepdims=True) + 1e-06)
    return center * scaled, scaled


def norm_back(upstream, unit_rows, scaled, gain_vec):
    inner = upstream * gain_vec
    return scaled * (
        inner
        - jnp.mean(inner, axis=-1, keepdims=True)
        - unit_rows * jnp.mean(inner * unit_rows, axis=-1, keepdims=True)
    )


def column_sums(rows):
    return jnp.sum(rows, axis=0, keepdims=True)


def first_head(width=LANES):
    return lax.broadcasted_iota(jnp.int32, (1, width), 1) < HD


def attend_kernel(
    tok_ref, key_bias_ref, gain_ref, bias_ref, w_qkv_ref, b_q_ref, b_v_ref, w_out_ref,
    part_ref, normed_ref, q_ref, k_ref, v_ref, soft_ref, mixed_ref,
):
    unit, _ = unit_of(tok_ref[...].astype(F32))
    normed = (unit * gain_ref[...] + bias_ref[...]).astype(BF16)
    normed_ref[...] = normed
    q_ref[...] = (mm(normed, w_qkv_ref[0]) + b_q_ref[...]).astype(BF16)
    k_ref[...] = mm(normed, w_qkv_ref[1]).astype(BF16)
    v_ref[...] = (mm(normed, w_qkv_ref[2]) + b_v_ref[...]).astype(BF16)
    key_bias = key_bias_ref[...]
    score_scale = 1.0 / math.sqrt(HD)
    low = first_head()
    for pair in range(q_ref.shape[1] // LANES):
        lanes = slice(pair * LANES, (pair + 1) * LANES)
        q_pair, k_pair, v_pair = q_ref[:, lanes], k_ref[:, lanes], v_ref[:, lanes]
        for side in range(2):
            own = low if side == 0 else jnp.logical_not(low)
            q_own = q_pair * jnp.where(own, score_scale, 0.0).astype(BF16)
            scores = mm(k_pair, q_own, NT) + key_bias
            expo = jnp.exp(scores - jnp.max(scores, axis=0, keepdims=True))
            soft = (expo * (1.0 / jnp.sum(expo, axis=0, keepdims=True))).astype(BF16)
            soft_ref[2 * pair + side] = soft
            mixed = mm(v_pair, soft, TN)
            begin = side * HD
            mixed_ref[pair * LANES + begin : pair * LANES + begin + HD, :] = mixed[
                begin : begin + HD
            ].astype(BF16)
    part_ref[...] = mm(mixed_ref[...], w_out_ref[...], TN).astype(BF16)


def mlp_kernel(
    tok_ref, own_ref, other_ref, b_out_ref, gain_ref, bias_ref, w_up_ref, b_up_ref, w_down_ref,
    cot_ref,
    hidden_ref, normed_ref, active_ref, upper_low_ref, down_ref, back_ref, sum_up_ref, sum_down_ref,
    down_total, back_total,
):
    attended = own_ref[...].astype(F32) + other_ref[...].astype(F32)
    hidden = tok_ref[...].astype(F32) + attended + b_out_ref[...]
    hidden_ref[...] = hidden
    unit, _ = unit_of(hidden)
    normed = (unit * gain_ref[...] + bias_ref[...]).astype(BF16)
    normed_ref[...] = normed
    cot = cot_ref[...]
    sum_down_ref[...] = column_sums(cot.astype(F32))
    width = w_up_ref.shape[1]
    step = 512
    for begin in range(0, width, step):
        units = slice(begin, begin + step)
        upper = mm(normed, w_up_ref[:, units]) + b_up_ref[:, units]
        cdf = 0.5 * (1.0 + lax.erf(upper * math.sqrt(0.5)))
        density = jnp.exp(upper * upper * -0.5) * (1.0 / math.sqrt(2.0 * math.pi))
        active = (upper * cdf).astype(BF16)
        active_ref[:, units] = active
        upper_grad = mm(cot, w_down_ref[units, :], NT) * (cdf + upper * density)
        sum_up_ref[:, units] = column_sums(upper_grad)
        upper_low = upper_grad.astype(BF16)
        upper_low_ref[:, units] = upper_low
        down = mm(active, w_down_ref[units, :])
        back = mm(upper_low, w_up_ref[:, units], NT)
        if begin == 0:
            down_total[...] = down
            back_total[...] = back
        else:
            down_total[...] += down
            back_total[...] += back
    down_ref[...] = down_total[...].astype(BF16)
    back_ref[...] = back_total[...].astype(BF16)


def attend_back_kernel(
    hidden_ref, own_ref, other_ref, cot_ref, gain_ref, w_out_ref, q_ref, k_ref, v_ref, soft_ref,
    w_qkv_ref,
    hidden_grad_ref, hidden_low_ref, grads_ref, back_ref, sums_ref,
    query_t,
):
    unit, scaled = unit_of(hidden_ref[...])
    upstream = own_ref[...].astype(F32) + other_ref[...].astype(F32)
    hidden_grad = cot_ref[...].astype(F32) + norm_back(upstream, unit, scaled, gain_ref[...])
    hidden_grad_ref[...] = hidden_grad
    hidden_low = hidden_grad.astype(BF16)
    hidden_low_ref[...] = hidden_low
    sums_ref[0:1, :] = column_sums(upstream * unit)
    sums_ref[1:2, :] = column_sums(upstream)
    sums_ref[2:3, :] = column_sums(hidden_grad)
    width = q_ref.shape[1]
    score_scale = 1.0 / math.sqrt(HD)
    low = first_head()
    for pair in range(width // LANES):
        lanes = slice(pair * LANES, (pair + 1) * LANES)
        q_pair, k_pair, v_pair = q_ref[:, lanes], k_ref[:, lanes], v_ref[:, lanes]
        mixed_grad = mm(hidden_low, w_out_ref[lanes, :], NT).astype(BF16)
        keys, values = [], []
        for side in range(2):
            own = low if side == 0 else jnp.logical_not(low)
            soft_low = soft_ref[2 * pair + side]
            soft = soft_low.astype(F32)
            own_grad = mixed_grad * jnp.where(own, 1.0, 0.0).astype(BF16)
            prob_grad = mm(v_pair, own_grad, NT)
            inner = jnp.sum(soft * prob_grad, axis=0, keepdims=True)
            score_grad = (soft * (prob_grad - inner)).astype(BF16)
            values.append(mm(soft_low, mixed_grad))
            keys.append(mm(score_grad, q_pair))
            query = mm(k_pair, score_grad, TN)
            begin = side * HD
            query_t[pair * LANES + begin : pair * LANES + begin + HD, :] = query[begin : begin + HD]
        grads_ref[0, :, lanes] = (
            jnp.transpose(query_t[lanes, :]) * score_scale
        ).astype(BF16)
        grads_ref[1, :, lanes] = (jnp.where(low, keys[0], keys[1]) * score_scale).astype(BF16)
        grads_ref[2, :, lanes] = jnp.where(low, values[0], values[1]).astype(BF16)
    sums_ref[3:4, :width] = column_sums(grads_ref[0].astype(F32))
    sums_ref[3:4, width : 2 * width] = column_sums(grads_ref[2].astype(F32))
    back = mm(grads_ref[0], w_qkv_ref[0], NT)
    back += mm(grads_ref[1], w_qkv_ref[1], NT)
    back += mm(grads_ref[2], w_qkv_ref[2], NT)
    back_ref[...] = back.astype(BF16)


def finish_kernel(
    tok_ref, own_ref, other_ref, gain_ref, hidden_grad_ref, out_ref, sums_ref
):
    unit, scaled = unit_of(tok_ref[...].astype(F32))
    upstream = own_ref[...].astype(F32) + other_ref[...].astype(F32)
    out_ref[...] = hidden_grad_ref[...] + norm_back(upstream, unit, scaled, gain_ref[...])
    sums_ref[0:1, :] = column_sums(upstream * unit)
    sums_ref[1:2, :] = column_sums(upstream)


def gram_kernel(count, parity_ref, *refs):
    lefts, rights = refs[:count], refs[count : 2 * count]
    keep_ref, send_ref = refs[2 * count : 2 * count + 2]
    flips = refs[2 * count + 2 :]
    blocks, rows, _ = flips[0].shape
    for left, flip in zip(lefts, flips):
        turned = jnp.transpose(left[...].astype(F32)).astype(BF16)
        for block in range(blocks):
            flip[block] = turned[block * rows : (block + 1) * rows]
    parity = parity_ref[0]
    planes, width = rights[0].shape[0], rights[0].shape[2]
    step = min(width, 512)
    for out_ref, which in ((send_ref, 1 - parity), (keep_ref, parity)):
        halves = [
            jnp.concatenate([flip[2 * block + which] for block in range(blocks // 2)], axis=0)
            for flip in flips
        ]
        for plane in range(planes):
            for begin in range(0, width, step):
                total = mm(halves[0], rights[0][plane, :, begin : begin + step])
                for half, right in zip(halves[1:], rights[1:]):
                    total += mm(half, right[plane, :, begin : begin + step])
                total = total.astype(BF16)
                for block in range(blocks // 2):
                    out_ref[plane, block, :, begin : begin + step] = total[
                        block * rows : (block + 1) * rows
                    ]


def call(kernel, outs, args, scratch=(), flops=0, moved=0, name=None):
    return pl.pallas_call(
        kernel,
        out_shape=[jax.ShapeDtypeStruct(shape, dtype) for shape, dtype in outs],
        scratch_shapes=list(scratch),
        compiler_params=pltpu.CompilerParams(vmem_limit_bytes=VMEM_LIMIT),
        cost_estimate=pl.CostEstimate(flops=flops, bytes_accessed=moved, transcendentals=0),
        name=name,
    )(*args)


def gram(lefts, rights, shares, parity, name):
    width = lefts[0].shape[1]
    rows = width // shares
    planes, _, columns = rights[0].shape
    if rows % ROW_TILE == 0:
        half = ((planes, shares // 2, rows, columns), BF16)
        count = len(lefts)
        return pl.pallas_call(
            partial(gram_kernel, count),
            out_shape=[jax.ShapeDtypeStruct(*half)] * 2,
            in_specs=[pl.BlockSpec(memory_space=pltpu.SMEM)]
            + [pl.BlockSpec(memory_space=pltpu.VMEM)] * (2 * count),
            scratch_shapes=[pltpu.VMEM((shares, rows, left.shape[0]), BF16) for left in lefts],
            compiler_params=pltpu.CompilerParams(vmem_limit_bytes=VMEM_LIMIT),
            name=name,
        )(parity[None], *lefts, *rights)
    total = sum(
        jnp.einsum("rd,prc->pdc", left, right, preferred_element_type=F32)
        for left, right in zip(lefts, rights)
    )
    total = total.astype(BF16).reshape(planes, shares // 2, 2, rows, columns)
    pick = lambda which: lax.dynamic_index_in_dim(total, which, 2, keepdims=False)
    return pick(parity), pick(1 - parity)


def flip_pairs(shares, bit):
    return [(index, index ^ (1 << bit)) for index in range(shares)]


def scatter_shares(kept, sent, shares, index):
    parts = [kept, lax.ppermute(sent, "dp", flip_pairs(shares, 0))]
    for bit in range(1, shares.bit_length() - 1):
        mine = (index >> bit) & 1

        def pick(part, which):
            planes, blocks, rows, columns = part.shape
            view = part.reshape(planes, blocks // 2, 2, rows, columns)
            return lax.dynamic_index_in_dim(view, which, 2, keepdims=False)

        outgoing = sum(pick(part, 1 - mine).astype(F32) for part in parts).astype(BF16)
        incoming = lax.ppermute(outgoing, "dp", flip_pairs(shares, bit))
        parts = [pick(part, mine) for part in parts] + [incoming]
    return sum(part.astype(F32) for part in parts)[:, 0]


def sum_all(vector, shares):
    for bit in range(shares.bit_length() - 1):
        vector = vector + lax.ppermute(vector, "dp", flip_pairs(shares, bit))
    return vector


def swap(rows):
    return lax.ppermute(rows, "tensor", [(0, 1), (1, 0)])


def local(
    shares, tokens, body_mask, ln1_gain, ln1_bias, w_qkv, b_q, b_v, w_out, b_out, ln2_gain, ln2_bias,
    w_up, b_up, w_down, b_down, cotangent,
):
    slices, seq = body_mask.shape
    model = tokens.shape[1]
    padded = -(-seq // ROW_TILE) * ROW_TILE
    width = w_qkv.shape[2]
    heads = width // HD
    units = w_up.shape[1]
    index = lax.axis_index("dp")
    parity = (index & 1).astype(jnp.int32)
    row = lambda vector: vector[None, :]
    spread = lambda rows: jnp.pad(
        rows.reshape(slices, seq, model), ((0, 0), (0, padded - seq), (0, 0))
    )
    token_rows, cot_rows = spread(tokens), spread(cotangent)
    key_bias = jnp.pad(
        jnp.where(body_mask > 0, 0.0, -1e30), ((0, 0), (0, padded - seq)), constant_values=-1e30
    )[:, :, None]
    w_qkv = jnp.transpose(w_qkv, (1, 0, 2))

    each = range(slices)
    wide, narrow = ((padded, model), BF16), ((padded, width), BF16)
    attended = [
        call(
            attend_kernel,
            [wide, wide, narrow, narrow, narrow, ((heads, padded, padded), BF16), ((width, padded), BF16)],
            (token_rows[s], key_bias[s], row(ln1_gain), row(ln1_bias), w_qkv, row(b_q), row(b_v), w_out),
            name="attend",
        )
        for s in each
    ]
    part = [attended[s][0] for s in each]
    part_other = [swap(part[s]) for s in each]
    tall = ((padded, units), BF16)
    mlp = [
        call(
            mlp_kernel,
            [((padded, model), F32), wide, tall, tall, wide, wide, ((1, units), F32), ((1, model), F32)],
            (
                token_rows[s], part[s], part_other[s], row(b_out), row(ln2_gain), row(ln2_bias),
                w_up, row(b_up), w_down, cot_rows[s],
            ),
            scratch=[pltpu.VMEM((padded, model), F32)] * 2,
            name="mlp",
        )
        for s in each
    ]
    hidden, normed2, active, upper_low, down, back, sum_up, sum_down = zip(*mlp)
    back_other = [swap(back[s]) for s in each]
    third = lambda arrays: [array[None] for array in arrays]
    down_halves = gram(cot_rows, third(active), shares, parity, "gram_down")
    up_halves = gram(normed2, third(upper_low), shares, parity, "gram_up")
    behind = [
        call(
            attend_back_kernel,
            [((padded, model), F32), wide, ((3, padded, width), BF16), wide, ((8, model), F32)],
            (
                hidden[s], back[s], back_other[s], cot_rows[s], row(ln2_gain), w_out,
                *attended[s][2:6], w_qkv,
            ),
            scratch=[pltpu.VMEM((width, padded), F32)],
            name="attend_back",
        )
        for s in each
    ]
    hidden_grad, hidden_low, qkv_grads, first_back, sums = zip(*behind)
    first_other = [swap(first_back[s]) for s in each]
    down_other = [swap(down[s]) for s in each]
    qkv_halves = gram([attended[s][1] for s in each], qkv_grads, shares, parity, "gram_qkv")
    mixed = [jnp.transpose(attended[s][6])[None] for s in each]
    out_halves = gram(hidden_low, mixed, shares, parity, "gram_out")

    share_down = scatter_shares(*down_halves, shares, index)[0]
    share_up = scatter_shares(*up_halves, shares, index)[0]
    share_out = scatter_shares(*out_halves, shares, index)[0]
    share_qkv = scatter_shares(*qkv_halves, shares, index)

    finish = [
        call(
            finish_kernel,
            [((padded, model), F32), ((8, model), F32)],
            (token_rows[s], first_back[s], first_other[s], row(ln1_gain), hidden_grad[s]),
            name="finish",
        )
        for s in each
    ]
    gather = lambda arrays: jnp.concatenate([array[:seq] for array in arrays], axis=0)
    grad_tokens = gather([item[0] for item in finish])
    block_out = gather(
        [hidden[s] + (down[s].astype(F32) + down_other[s].astype(F32)) + row(b_down) for s in each]
    )
    small = sum_all(
        jnp.concatenate(
            [
                sum(item[1][:2] for item in finish),
                sum(item[:4] for item in sums),
                sum(sum_up).reshape(-1, model),
                sum(sum_down),
            ],
            axis=0,
        ),
        shares,
    )
    ups = units // model
    return (
        block_out,
        grad_tokens,
        small[0],
        small[1],
        jnp.transpose(share_qkv, (1, 0, 2)),
        small[5, :width],
        small[5, width : 2 * width],
        share_out.T,
        small[4],
        small[2],
        small[3],
        share_up,
        small[6 : 6 + ups].reshape(-1),
        share_down.T,
        small[6 + ups],
    )


def solution(mesh):
    return jax.shard_map(
        partial(local, mesh.shape["dp"]),
        mesh=mesh,
        in_specs=(
            P("dp", None),
            P("dp", None),
            P(),
            P(),
            P(None, None, "tensor"),
            P("tensor"),
            P("tensor"),
            P("tensor", None),
            P(),
            P(),
            P(),
            P(None, "tensor"),
            P("tensor"),
            P("tensor", None),
            P(),
            P("dp", None),
        ),
        out_specs=(
            P("dp", None),
            P("dp", None),
            P(),
            P(),
            P("dp", None, "tensor"),
            P("tensor"),
            P("tensor"),
            P("tensor", "dp"),
            P(),
            P(),
            P(),
            P("dp", "tensor"),
            P("tensor"),
            P("tensor", "dp"),
            P(),
        ),
        check_vma=False,
    )
```

```python
import math
from functools import partial

import jax
import jax.numpy as jnp
from jax import lax
from jax.experimental import pallas as pl
from jax.experimental.pallas import tpu as pltpu
from jax.sharding import PartitionSpec as P

HD = 64
LANES = 128
SUBLANES = 8
ROW_TILE = 16
F32 = jnp.float32
BF16 = jnp.bfloat16
MIB = 1024 * 1024
HEAVY = 20

NN = (((1,), (0,)), ((), ()))
NT = (((1,), (1,)), ((), ()))
TN = (((0,), (0,)), ((), ()))

ROW_DOWN, ROW_GAIN2, ROW_BIAS2, ROW_OUT, ROW_QV, ROW_GAIN1, ROW_BIAS1, ROW_UP = range(8)


def mm(left, right, dims=NN):
    return lax.dot_general(left, right, dims, preferred_element_type=F32)


def unit_of(source):
    center = source - jnp.mean(source, axis=-1, keepdims=True)
    scaled = lax.rsqrt(jnp.mean(center * center, axis=-1, keepdims=True) + 1e-06)
    return center * scaled, scaled


def norm_back(upstream, unit_rows, scaled, gain_vec):
    inner = upstream * gain_vec
    return scaled * (
        inner
        - jnp.mean(inner, axis=-1, keepdims=True)
        - unit_rows * jnp.mean(inner * unit_rows, axis=-1, keepdims=True)
    )


def column_sums(rows):
    return jnp.sum(rows, axis=0, keepdims=True)


def row_of(ref):
    return ref[...].reshape(1, -1)


def share_bit(bit):
    return (lax.axis_index("dp").astype(jnp.int32) >> bit) & 1


def low_head():
    return lax.broadcasted_iota(jnp.int32, (1, LANES), 1) < HD


class Layout:
    def __init__(self, rows, slices, seq):
        self.rows, self.slices, self.seq = rows, slices, seq
        self.padded = -(-seq // ROW_TILE) * ROW_TILE
        self.sent = -(-seq // SUBLANES) * SUBLANES

    def pick(self, values, s):
        start = s * (self.rows - self.padded)
        return values[start : start + self.padded]

    def real(self, s):
        place = lax.broadcasted_iota(jnp.int32, (self.padded, 1), 0)
        return place < self.seq if s == 0 else place >= self.padded - self.seq

    def cut(self, values, s):
        return values[: self.sent] if s == 0 else values[self.padded - self.sent :]

    def fill(self, values, s):
        extra = jnp.zeros((self.padded - self.sent, values.shape[1]), values.dtype)
        return jnp.concatenate([values, extra] if s == 0 else [extra, values], axis=0)

    def join(self, first, second):
        start = self.rows - self.padded
        place = lax.broadcasted_iota(jnp.int32, (self.padded - start, 1), 0) + start
        middle = jnp.where(place < self.seq, first[start:], second[: self.padded - start])
        return jnp.concatenate([first[:start], middle, second[self.padded - start :]], axis=0)


def attend_kernel(
    lay, s, tok_ref, mask_ref, gain_ref, bias_ref, w_qkv_ref, b_q_ref, b_v_ref, w_out_ref,
    part_ref, normed_ref, q_ref, k_ref, v_ref, soft_ref, mixed_ref, bias_row,
):
    unit, _ = unit_of(lay.pick(tok_ref[...].astype(F32), s))
    normed = (unit * row_of(gain_ref) + row_of(bias_ref)).astype(BF16)
    normed_ref[...] = normed
    q_ref[...] = (mm(normed, w_qkv_ref[0]) + row_of(b_q_ref)).astype(BF16)
    k_ref[...] = mm(normed, w_qkv_ref[1]).astype(BF16)
    v_ref[...] = (mm(normed, w_qkv_ref[2]) + row_of(b_v_ref)).astype(BF16)
    bias_row[...] = jnp.full(bias_row.shape, -1e30, F32)
    bias_row[0:1, : lay.seq] = jnp.where(mask_ref[s : s + 1, :] > 0, 0.0, -1e30)
    lanes_bias = bias_row[...]
    if s:
        lanes_bias = pltpu.roll(lanes_bias, lay.padded - lay.seq, 1)
    turned = jnp.transpose(jnp.broadcast_to(lanes_bias[0:1], (LANES, lanes_bias.shape[1])))
    turned = turned[: lay.padded]
    key_bias = jnp.concatenate([turned] * -(-lay.padded // LANES), axis=1)[:, : lay.padded]
    score_scale = 1.0 / math.sqrt(HD)
    low = low_head()
    for pair in range(q_ref.shape[1] // LANES):
        lanes = slice(pair * LANES, (pair + 1) * LANES)
        q_pair, k_pair, v_pair = q_ref[:, lanes], k_ref[:, lanes], v_ref[:, lanes]
        for side in range(2):
            own = low if side == 0 else jnp.logical_not(low)
            q_own = q_pair * jnp.where(own, score_scale, 0.0).astype(BF16)
            scores = mm(k_pair, q_own, NT) + key_bias
            expo = jnp.exp(scores - jnp.max(scores, axis=0, keepdims=True))
            soft = (expo * (1.0 / jnp.sum(expo, axis=0, keepdims=True))).astype(BF16)
            soft_ref[2 * pair + side] = soft
            mixed = mm(v_pair, soft, TN)
            begin = side * HD
            mixed_ref[pair * LANES + begin : pair * LANES + begin + HD, :] = mixed[
                begin : begin + HD
            ].astype(BF16)
    part_ref[...] = lay.cut(mm(mixed_ref[...], w_out_ref[...], TN), s).astype(BF16)


def mlp_kernel(
    lay, s, tok_ref, own_ref, other_ref, b_out_ref, gain_ref, bias_ref, w_up_ref, b_up_ref,
    w_down_ref, cot_ref, *refs,
):
    before_ref = refs[0] if s else None
    (
        hidden_ref, normed_ref, active_ref, upper_low_ref, down_ref, back_ref, sums_ref,
        down_total, back_total,
    ) = refs[1:] if s else refs
    attended = lay.fill(own_ref[...].astype(F32) + other_ref[...].astype(F32), s)
    hidden = lay.pick(tok_ref[...].astype(F32), s) + attended + row_of(b_out_ref)
    hidden_ref[...] = hidden
    unit, _ = unit_of(hidden)
    normed = (unit * row_of(gain_ref) + row_of(bias_ref)).astype(BF16)
    normed_ref[...] = normed
    cot = jnp.where(lay.real(s), lay.pick(cot_ref[...].astype(F32), s), 0.0)
    sums_ref[...] = before_ref[...] if s else jnp.zeros(sums_ref.shape, F32)
    sums_ref[ROW_DOWN : ROW_DOWN + 1, :] += column_sums(cot)
    cot = cot.astype(BF16)
    b_up = row_of(b_up_ref)
    width, model = w_up_ref.shape[1], tok_ref.shape[1]
    step = 768
    for begin in range(0, width, step):
        units = slice(begin, begin + step)
        upper = mm(normed, w_up_ref[:, units]) + b_up[:, units]
        cdf = 0.5 * (1.0 + lax.erf(upper * math.sqrt(0.5)))
        density = jnp.exp(upper * upper * -0.5) * (1.0 / math.sqrt(2.0 * math.pi))
        active = (upper * cdf).astype(BF16)
        active_ref[:, units] = active
        upper_grad = mm(cot, w_down_ref[units, :], NT) * (cdf + upper * density)
        place = ROW_UP + begin // model
        sums_ref[place : place + 1, begin % model : begin % model + step] += column_sums(upper_grad)
        upper_low = upper_grad.astype(BF16)
        upper_low_ref[:, units] = upper_low
        down = mm(active, w_down_ref[units, :])
        back = mm(upper_low, w_up_ref[:, units], NT)
        if begin == 0:
            down_total[...] = down
            back_total[...] = back
        else:
            down_total[...] += down
            back_total[...] += back
    down_ref[...] = lay.cut(down_total[...], s).astype(BF16)
    back_ref[...] = lay.cut(back_total[...], s).astype(BF16)


def attend_back_kernel(
    lay, s, hidden_ref, own_ref, other_ref, cot_ref, gain_ref, w_out_ref, q_ref, k_ref, v_ref,
    soft_ref, w_qkv_ref, tok_ref, down_ref, before_ref,
    hidden_grad_ref, hidden_low_ref, grads_ref, last_ref, sums_ref, query_t,
):
    last_ref[1] = down_ref[...]
    unit, scaled = unit_of(hidden_ref[...])
    upstream = lay.fill(own_ref[...].astype(F32) + other_ref[...].astype(F32), s)
    cot = jnp.where(lay.real(s), lay.pick(cot_ref[...].astype(F32), s), 0.0)
    hidden_grad = cot + norm_back(upstream, unit, scaled, row_of(gain_ref))
    hidden_grad_ref[...] = hidden_grad
    hidden_low = hidden_grad.astype(BF16)
    hidden_low_ref[...] = hidden_low
    sums_ref[...] = before_ref[...]

    def add_row(place, sums, begin=0):
        sums_ref[place : place + 1, begin : begin + sums.shape[1]] += sums

    add_row(ROW_GAIN2, column_sums(upstream * unit))
    add_row(ROW_BIAS2, column_sums(upstream))
    add_row(ROW_OUT, column_sums(hidden_grad))
    width = q_ref.shape[1]
    score_scale = 1.0 / math.sqrt(HD)
    low = low_head()
    for pair in range(width // LANES):
        lanes = slice(pair * LANES, (pair + 1) * LANES)
        q_pair, k_pair, v_pair = q_ref[:, lanes], k_ref[:, lanes], v_ref[:, lanes]
        mixed_grad = mm(hidden_low, w_out_ref[lanes, :], NT).astype(BF16)
        keys, values = [], []
        for side in range(2):
            own = low if side == 0 else jnp.logical_not(low)
            soft_low = soft_ref[2 * pair + side]
            soft = soft_low.astype(F32)
            own_grad = mixed_grad * jnp.where(own, 1.0, 0.0).astype(BF16)
            prob_grad = mm(v_pair, own_grad, NT)
            inner = jnp.sum(soft * prob_grad, axis=0, keepdims=True)
            score_grad = (soft * (prob_grad - inner)).astype(BF16)
            values.append(mm(soft_low, mixed_grad))
            keys.append(mm(score_grad, q_pair))
            query = mm(k_pair, score_grad, TN)
            begin = side * HD
            query_t[pair * LANES + begin : pair * LANES + begin + HD, :] = query[begin : begin + HD]
        grads_ref[0, :, lanes] = (jnp.transpose(query_t[lanes, :]) * score_scale).astype(BF16)
        grads_ref[1, :, lanes] = (jnp.where(low, keys[0], keys[1]) * score_scale).astype(BF16)
        grads_ref[2, :, lanes] = jnp.where(low, values[0], values[1]).astype(BF16)
    add_row(ROW_QV, column_sums(grads_ref[0].astype(F32)))
    add_row(ROW_QV, column_sums(grads_ref[2].astype(F32)), width)
    back = mm(grads_ref[0], w_qkv_ref[0], NT)
    back += mm(grads_ref[1], w_qkv_ref[1], NT)
    back += mm(grads_ref[2], w_qkv_ref[2], NT)
    last_ref[0] = lay.cut(back, s).astype(BF16)
    unit, _ = unit_of(lay.pick(tok_ref[...].astype(F32), s))
    add_row(ROW_GAIN1, column_sums(back * unit))
    add_row(ROW_BIAS1, column_sums(back))


def finish_kernel(lay, *refs):
    count = lay.slices
    tok_ref, gain_ref, bias_ref = refs[:3]
    own, other, hidden_grad, hidden = (refs[3 + k * count : 3 + (k + 1) * count] for k in range(4))
    block_ref, grad_ref = refs[-2:]
    gain, bias = row_of(gain_ref), row_of(bias_ref)
    tokens = tok_ref[...].astype(F32)
    results, blocks = [], []
    for s in range(count):
        both = lambda which: lay.fill(own[s][which].astype(F32) + other[s][which].astype(F32), s)
        unit, scaled = unit_of(lay.pick(tokens, s))
        results.append(hidden_grad[s][...] + norm_back(both(0), unit, scaled, gain))
        blocks.append(hidden[s][...] + both(1) + bias)
    grad_ref[...] = lay.join(*results)
    block_ref[...] = lay.join(*blocks)


def gram_kernel(lay, groups, *refs):
    count = lay.slices
    ins = 2 * count * len(groups)
    keep_ref, send_ref = refs[ins : ins + 2]
    flips = refs[ins + 2 :]
    blocks, rows, _ = flips[0].shape
    parity = share_bit(0)
    plane = 0
    for group, (kind, masked) in enumerate(groups):
        lefts = refs[2 * count * group : 2 * count * group + count]
        rights = refs[2 * count * group + count : 2 * count * (group + 1)]
        for s in range(count):
            left = lefts[s][...].astype(F32)
            if masked:
                left = jnp.where(lay.real(s), lay.pick(left, s), 0.0)
            turned = jnp.transpose(left).astype(BF16)
            for block in range(blocks):
                flips[s][block] = turned[block * rows : (block + 1) * rows]
        planes = rights[0].shape[0] if len(rights[0].shape) == 3 else 1
        width = keep_ref.shape[-1]
        step = min(width, 512)
        for out_ref, which in ((send_ref, 1 - parity), (keep_ref, parity)):
            halves = [
                jnp.concatenate([flip[2 * block + which] for block in range(blocks // 2)], axis=0)
                for flip in flips
            ]
            for own in range(planes):
                for begin in range(0, width, step):
                    columns = slice(begin, begin + step)
                    total = None
                    for half, right in zip(halves, rights):
                        if kind == "turned":
                            term = mm(half, right[...], NT)
                        elif planes > 1:
                            term = mm(half, right[own, :, columns])
                        else:
                            term = mm(half, right[:, columns])
                        total = term if total is None else total + term
                    total = total.astype(BF16)
                    for block in range(blocks // 2):
                        out_ref[plane + own, block, :, columns] = total[
                            block * rows : (block + 1) * rows
                        ]
        plane += planes


def halve_kernel(low_blocks, bit, *refs):
    parts, outs = refs[:2], refs[2:]
    last = low_blocks == 0
    mine = share_bit(bit)
    planes, blocks = parts[0].shape[:2]

    def total(plane, place):
        return sum(part[plane, place].astype(F32) for part in parts)

    for plane in range(planes):
        if last:
            many = outs[0].shape[0]
            outs[plane // many][plane % many] = total(plane, 0)
            continue
        for block in range(blocks // 2):
            base = block // low_blocks * 2 * low_blocks + block % low_blocks
            outs[0][plane, block] = total(plane, base + (1 - mine) * low_blocks).astype(BF16)
            outs[1][plane, block] = total(plane, base + mine * low_blocks)


class Order:
    def __init__(self):
        self.token = ()

    def __call__(self, kernel, outs, args, scratch=(), limit=16, fresh=False, weight=0, name=None):
        first, tokens = len(args), len(self.token)

        def body(*refs):
            kernel(*refs[:first], *refs[first + tokens :])

        place = pltpu.HBM if fresh else pltpu.VMEM
        results = pl.pallas_call(
            body,
            out_shape=[
                (pltpu.HBM if space else pltpu.VMEM)(shape, dtype) for shape, dtype, *space in outs
            ],
            in_specs=[pl.BlockSpec(memory_space=pltpu.VMEM)] * first
            + [pl.BlockSpec(memory_space=pl.ANY)] * tokens,
            out_specs=[pl.BlockSpec(memory_space=pltpu.VMEM)] * len(outs),
            scratch_shapes=list(scratch),
            compiler_params=pltpu.CompilerParams(vmem_limit_bytes=limit * MIB),
            cost_estimate=pl.CostEstimate(
                flops=1 + weight * 10**9, bytes_accessed=1 + weight * MIB, transcendentals=0
            ),
            name=name,
        )(*(pltpu.with_memory_space_constraint(array, place) for array in args), *self.token)
        self.token = (results[-1],)
        return results


def gram(call, lay, groups, shares, name=None):
    model = groups[0][1][0].shape[1]
    rows = model // shares
    kinds = tuple((kind, masked) for kind, _, _, masked in groups)
    columns = (
        groups[0][2][0].shape[0] if groups[0][0] == "turned" else groups[0][2][0].shape[-1]
    )
    planes = sum(r[0].shape[0] if len(r[0].shape) == 3 else 1 for _, _, r, _ in groups)
    args = [array for _, lefts, rights, _ in groups for array in (*lefts, *rights)]
    if rows % ROW_TILE == 0:
        half = ((planes, shares // 2, rows, columns), BF16)
        return call(
            partial(gram_kernel, lay, kinds),
            [half, half],
            args,
            scratch=[pltpu.VMEM((shares, rows, lay.padded), BF16)] * lay.slices,
            name=name,
        )
    sums = []
    for kind, lefts, rights, masked in groups:
        total = 0.0
        for s, (left, right) in enumerate(zip(lefts, rights)):
            if masked:
                left = jnp.where(lay.real(s), lay.pick(left, s), 0)
            if kind == "turned":
                right = right.T
            right = right if len(right.shape) == 3 else right[None]
            total += jnp.einsum("rd,prc->pdc", left, right, preferred_element_type=F32)
        sums.append(total)
    total = jnp.concatenate(sums, axis=0).astype(BF16)
    total = total.reshape(planes, shares // 2, 2, rows, columns)
    pick = lambda which: lax.dynamic_index_in_dim(total, which, 2, keepdims=False)
    return pick(share_bit(0)), pick(1 - share_bit(0))


def flip_pairs(shares, bit):
    return [(index, index ^ (1 << bit)) for index in range(shares)]


def flip(array, shares, bit):
    return lax.ppermute(array, "dp", flip_pairs(shares, bit))


class Scatter:
    def __init__(self, call, halves, shares, order, name):
        self.call, self.name = call, name
        self.shares, self.order = shares, list(order)
        self.left = sorted(order, reverse=True)
        self.kept, self.outgoing = halves
        self.bit = 0

    def send(self):
        self.incoming = flip(self.outgoing, self.shares, self.bit)

    def add(self, weight=0):
        parts = [self.kept, self.incoming]
        planes, blocks, rows, columns = self.kept.shape
        self.bit = self.order.pop(0)
        low_blocks = 1 << (len(self.left) - 1 - self.left.index(self.bit))
        self.left.remove(self.bit)
        if rows % ROW_TILE:
            mine = share_bit(self.bit)

            def pick(which):
                view = (planes, blocks // 2 // low_blocks, 2, low_blocks, rows, columns)
                total = sum(
                    lax.dynamic_index_in_dim(part.reshape(view), which, 2).astype(F32)
                    for part in parts
                )
                return total.reshape(planes, blocks // 2, rows, columns)

            self.outgoing, self.kept = pick(1 - mine).astype(BF16), pick(mine)
            return
        half = (planes, blocks // 2, rows, columns)
        self.outgoing, self.kept = self.call(
            partial(halve_kernel, low_blocks, self.bit),
            [(half, BF16), (half, F32)],
            parts,
            weight=weight,
            name="add_" + self.name,
        )

    def step(self, weight=0):
        if self.order:
            self.add(weight)
            self.send()

    def finish(self, groups):
        parts = [self.kept, self.incoming]
        planes, _, rows, columns = self.kept.shape
        if rows % ROW_TILE:
            total = sum(part.astype(F32) for part in parts)[:, 0]
            return [total[:groups[0]], total[groups[0] :]][: len(groups)]
        return self.call(
            partial(halve_kernel, 0, 0),
            [((group, rows, columns), F32, True) for group in groups],
            parts,
            name="last_" + self.name,
        )


def add_small_kernel(own_ref, other_ref, out_ref):
    out_ref[...] = own_ref[...] + other_ref[...]


def last_small_kernel(own_ref, other_ref, *refs):
    outs, total_ref = refs[:-1], refs[-1]
    other = other_ref[...]
    place = lax.broadcasted_iota(jnp.int32, (other.shape[0], 1), 0)
    split = (place == ROW_GAIN1) | (place == ROW_BIAS1)
    total_ref[...] = own_ref[...] + jnp.where(split, other, 0.0)
    width = outs[2].shape[0]
    model = total_ref.shape[1]
    row = lambda place: total_ref[place : place + 1, :]
    outs[0][...] = row(ROW_GAIN1).reshape(-1)
    outs[1][...] = row(ROW_BIAS1).reshape(-1)
    outs[2][...] = total_ref[ROW_QV : ROW_QV + 1, :width].reshape(-1)
    outs[3][...] = total_ref[ROW_QV : ROW_QV + 1, width : 2 * width].reshape(-1)
    outs[4][...] = row(ROW_OUT).reshape(-1)
    outs[5][...] = row(ROW_GAIN2).reshape(-1)
    outs[6][...] = row(ROW_BIAS2).reshape(-1)
    for step in range(outs[7].shape[0] // model):
        outs[7][step * model : (step + 1) * model] = row(ROW_UP + step).reshape(-1)
    outs[8][...] = row(ROW_DOWN).reshape(-1)


def swap(rows):
    return lax.ppermute(rows, "tensor", [(0, 1), (1, 0)])


def local(
    shares, tokens, body_mask, ln1_gain, ln1_bias, w_qkv, b_q, b_v, w_out, b_out, ln2_gain, ln2_bias,
    w_up, b_up, w_down, b_down, cotangent,
):
    slices, seq = body_mask.shape
    rows, model = tokens.shape
    lay = Layout(rows, slices, seq)
    padded, sent = lay.padded, lay.sent
    width = w_qkv.shape[2]
    heads = width // HD
    units = w_up.shape[1]
    w_qkv = jnp.transpose(w_qkv, (1, 0, 2))
    each = range(slices)
    wide, narrow, tall = ((padded, model), BF16), ((padded, width), BF16), ((padded, units), BF16)
    wide_f, crossing = ((padded, model), F32), ((sent, model), BF16)
    small = ((-(-(ROW_UP + units // model) // SUBLANES) * SUBLANES, model), F32)
    lane_room = -(-padded // LANES) * LANES

    call = Order()
    bits = range(1, shares.bit_length() - 1)
    far_first = [*bits[1:], *bits[:1]]

    attended, part_other = [], []
    for s in each:
        attended.append(
            call(
                partial(attend_kernel, lay, s),
                [crossing, wide, narrow, narrow, narrow, ((heads, padded, padded), BF16), ((width, padded), BF16)],
                (tokens, body_mask, ln1_gain, ln1_bias, w_qkv, b_q, b_v, w_out),
                scratch=[pltpu.VMEM((SUBLANES, lane_room), F32)],
                fresh=s == 0,
                name="attend",
            )
        )
        part_other.append(swap(attended[s][0]))
    mlp, back_other = [], []
    for s in each:
        mlp.append(
            call(
                partial(mlp_kernel, lay, s),
                [wide_f, wide, tall, tall, crossing, crossing, small],
                (
                    tokens, attended[s][0], part_other[s], b_out, ln2_gain, ln2_bias, w_up, b_up, w_down,
                    cotangent, *([mlp[s - 1][6]] if s else []),
                ),
                scratch=[pltpu.VMEM((padded, model), F32)] * 2,
                name="mlp",
            )
        )
        back_other.append(swap(mlp[s][5]))
    hidden, normed2, active, upper_low, down, back, sums = (list(item) for item in zip(*mlp))
    vector = sums[-1]

    def attend_back(s, vector):
        return call(
            partial(attend_back_kernel, lay, s),
            [wide_f, wide, ((3, padded, width), BF16), ((2, sent, model), BF16), small],
            (
                hidden[s], back[s], back_other[s], cotangent, ln2_gain, w_out, *attended[s][2:6],
                w_qkv, tokens, down[s], vector,
            ),
            scratch=[pltpu.VMEM((width, padded), F32)],
            weight=HEAVY,
            name="attend_back",
        )

    down_halves = gram(call, lay, [("plain", [cotangent] * slices, active, True)], shares, "gram_down")
    down_sum = Scatter(call, down_halves, shares, bits, "down")
    down_sum.send()
    up_halves = gram(call, lay, [("plain", normed2, upper_low, False)], shares, "gram_up")
    up_sum = Scatter(call, up_halves, shares, far_first, "up")
    up_sum.send()
    behind, last_other = [attend_back(0, vector)], []
    last_other.append(swap(behind[0][3]))
    down_sum.step()
    up_sum.step()
    for s in each[1:]:
        behind.append(attend_back(s, behind[-1][4]))
        last_other.append(swap(behind[s][3]))
    hidden_grad, hidden_low, qkv_grads, last, sums = (list(item) for item in zip(*behind))
    vector = sums[-1]

    vector_other = flip(vector, shares, 0)
    qkv_halves = gram(
        call,
        lay,
        [
            ("plain", [attended[s][1] for s in each], qkv_grads, False),
            ("turned", hidden_low, [attended[s][6] for s in each], False),
        ],
        shares,
        "gram_qkv",
    )
    qkv_sum = Scatter(call, qkv_halves, shares, bits, "qkv")
    qkv_sum.send()

    def add_small():
        return call(add_small_kernel, [small], [vector, vector_other], name="add_small")[0]

    steps = shares.bit_length() - 1
    down_sum.step()
    up_sum.step(HEAVY)
    qkv_sum.step()
    for bit in range(1, steps):
        vector = add_small()
        vector_other = flip(vector, shares, bit)
        down_sum.step()
        if bit == 1:
            qkv_sum.step()
        up_sum.step()
    vector = add_small()
    vector_other = swap(vector)
    while down_sum.order or up_sum.order or qkv_sum.order:
        for item in (down_sum, qkv_sum, up_sum):
            item.step()
    (share_down,) = down_sum.finish([1])
    (share_up,) = up_sum.finish([1])
    block_out, grad_tokens = call(
        partial(finish_kernel, lay),
        [((rows, model), F32, True)] * 2,
        (tokens, ln1_gain, b_down, *last, *last_other, *hidden_grad, *hidden),
        name="finish",
    )
    vectors = call(
        last_small_kernel,
        [((size,), F32, True) for size in (model, model, width, width, model, model, model, units, model)],
        [vector, vector_other],
        scratch=[pltpu.VMEM(*small)],
        name="last_small",
    )
    (
        sum_ln1_gain, sum_ln1_bias, sum_b_q, sum_b_v, sum_b_out, sum_ln2_gain, sum_ln2_bias, sum_b_up,
        sum_b_down,
    ) = vectors
    share_qkv, share_out = qkv_sum.finish([3, 1])
    return (
        block_out,
        grad_tokens,
        sum_ln1_gain,
        sum_ln1_bias,
        jnp.transpose(share_qkv, (1, 0, 2)),
        sum_b_q,
        sum_b_v,
        share_out[0].T,
        sum_b_out,
        sum_ln2_gain,
        sum_ln2_bias,
        share_up[0],
        sum_b_up,
        share_down[0].T,
        sum_b_down,
    )


def solution(mesh):
    return jax.shard_map(
        partial(local, mesh.shape["dp"]),
        mesh=mesh,
        in_specs=(
            P("dp", None),
            P("dp", None),
            P(),
            P(),
            P(None, None, "tensor"),
            P("tensor"),
            P("tensor"),
            P("tensor", None),
            P(),
            P(),
            P(),
            P(None, "tensor"),
            P("tensor"),
            P("tensor", None),
            P(),
            P("dp", None),
        ),
        out_specs=(
            P("dp", None),
            P("dp", None),
            P(),
            P(),
            P("dp", None, "tensor"),
            P("tensor"),
            P("tensor"),
            P("tensor", "dp"),
            P(),
            P(),
            P(),
            P("dp", "tensor"),
            P("tensor"),
            P("tensor", "dp"),
            P(),
        ),
        check_vma=False,
    )
```

```python
import math
from functools import partial

import jax
import jax.numpy as jnp
from jax import lax
from jax.experimental import pallas as pl
from jax.experimental.pallas import tpu as pltpu
from jax.sharding import PartitionSpec as P

HD = 64
LANES = 128
SUBLANES = 8
ROW_TILE = 16
F32 = jnp.float32
BF16 = jnp.bfloat16
MIB = 1024 * 1024

ORDER = (
    "A0", "A1", "T", "B0", "B1", "GU", "GD", "R1", "X", "Y", "M1", "C0",
    "C1", "GQ", "s1", "L", "M2", "Q1", "M3", "Q2", "Q3", "M4", "F", "Q4",
)
WEIGHT = {"X": 12, "Y": 3, "C0": 4, "C1": 8, "GQ": 4, "M2": 12, "M3": 12, "F": 2}
CUTS = {"U": 1, "D": 1}

ATTENDED = ("part", "normed", "q", "k", "v", "soft", "mixed")
UPPED = ("hidden", "normed2", "active", "upper_low")
RETURNED = ("hidden_grad", "hidden_low", "qkv_grad", "first_back")
OTHERS = ("back", "other", "cot_turned", "turned", "active_grad")

NN = (((1,), (0,)), ((), ()))
NT = (((1,), (1,)), ((), ()))
TN = (((0,), (0,)), ((), ()))

ROW_DOWN, ROW_GAIN2, ROW_BIAS2, ROW_OUT, ROW_QV, ROW_GAIN1, ROW_BIAS1, ROW_UP = range(8)


def mm(left, right, dims=NN):
    return lax.dot_general(left, right, dims, preferred_element_type=F32)


def unit_of(source):
    center = source - jnp.mean(source, axis=-1, keepdims=True)
    scaled = lax.rsqrt(jnp.mean(center * center, axis=-1, keepdims=True) + 1e-06)
    return center * scaled, scaled


def norm_back(upstream, unit_rows, scaled, gain_vec):
    inner = upstream * gain_vec
    return scaled * (
        inner
        - jnp.mean(inner, axis=-1, keepdims=True)
        - unit_rows * jnp.mean(inner * unit_rows, axis=-1, keepdims=True)
    )


def column_sums(rows):
    return jnp.sum(rows, axis=0, keepdims=True)


def add_sums(sums_ref, place, sums):
    width = sums_ref.shape[1]
    for half in range(sums.shape[1] // width):
        row = 2 * place + half
        sums_ref[row : row + 1, :] += sums[:, half * width : (half + 1) * width]


def row_of(ref):
    return ref[...].reshape(1, -1)


def share_bit(bit):
    return (lax.axis_index("dp").astype(jnp.int32) >> bit) & 1


def low_head():
    return lax.broadcasted_iota(jnp.int32, (1, LANES), 1) < HD


class Layout:
    def __init__(self, rows, slices, seq):
        self.rows, self.slices, self.seq = rows, slices, seq
        self.padded = -(-seq // ROW_TILE) * ROW_TILE
        self.sent = -(-seq // SUBLANES) * SUBLANES

    def pick(self, values, s):
        start = s * (self.rows - self.padded)
        return values[start : start + self.padded]

    def real(self, s):
        place = lax.broadcasted_iota(jnp.int32, (self.padded, 1), 0)
        return place < self.seq if s == 0 else place >= self.padded - self.seq

    def cut(self, values, s):
        return values[: self.sent] if s == 0 else values[self.padded - self.sent :]

    def fill(self, values, s):
        extra = jnp.zeros((self.padded - self.sent, values.shape[1]), values.dtype)
        return jnp.concatenate([values, extra] if s == 0 else [extra, values], axis=0)

    def join(self, first, second):
        start = self.rows - self.padded
        place = lax.broadcasted_iota(jnp.int32, (self.padded - start, 1), 0) + start
        middle = jnp.where(place < self.seq, first[start:], second[: self.padded - start])
        return jnp.concatenate([first[:start], middle, second[self.padded - start :]], axis=0)


def first_attend_kernel(lay, *refs):
    sources, outs = refs[:8], refs[8:15]
    w_qkv_ref, w_out_ref, tok_ref = refs[15:18]
    mask_ref, gain_ref, bias_ref, b_q_ref, b_v_ref, bias_row, sems = refs[18:]
    targets = (tok_ref, mask_ref, gain_ref, bias_ref, w_qkv_ref, b_q_ref, b_v_ref, w_out_ref)
    copies = [
        pltpu.make_async_copy(source, target, sems.at[place])
        for place, (source, target) in enumerate(zip(sources, targets))
    ]
    for place in (0, 2, 3, 4, 5, 6, 1, 7):
        copies[place].start()

    def ready(*places):
        for place in places:
            copies[place].wait()

    attend_kernel(lay, 0, *targets, *outs, bias_row, ready)


def attend_kernel(
    lay, s, tok_ref, mask_ref, gain_ref, bias_ref, w_qkv_ref, b_q_ref, b_v_ref, w_out_ref,
    part_ref, normed_ref, q_ref, k_ref, v_ref, soft_ref, mixed_ref, bias_row,
    ready=lambda *places: None,
):
    ready(0, 2, 3)
    unit, _ = unit_of(lay.pick(tok_ref[...].astype(F32), s))
    normed = (unit * row_of(gain_ref) + row_of(bias_ref)).astype(BF16)
    normed_ref[...] = normed
    ready(4, 5, 6, 1)
    q_ref[...] = (mm(normed, w_qkv_ref[0]) + row_of(b_q_ref)).astype(BF16)
    k_ref[...] = mm(normed, w_qkv_ref[1]).astype(BF16)
    v_ref[...] = (mm(normed, w_qkv_ref[2]) + row_of(b_v_ref)).astype(BF16)
    bias_row[...] = jnp.full(bias_row.shape, -1e30, F32)
    bias_row[0:1, : lay.seq] = jnp.where(mask_ref[s : s + 1, :] > 0, 0.0, -1e30)
    lanes_bias = bias_row[...]
    if s:
        lanes_bias = pltpu.roll(lanes_bias, lay.padded - lay.seq, 1)
    turned = jnp.transpose(jnp.broadcast_to(lanes_bias[0:1], (LANES, lanes_bias.shape[1])))
    turned = turned[: lay.padded]
    key_bias = jnp.concatenate([turned] * -(-lay.padded // LANES), axis=1)[:, : lay.padded]
    score_scale = 1.0 / math.sqrt(HD)
    low = low_head()
    for pair in range(q_ref.shape[1] // LANES):
        lanes = slice(pair * LANES, (pair + 1) * LANES)
        q_pair, k_pair, v_pair = q_ref[:, lanes], k_ref[:, lanes], v_ref[:, lanes]
        for side in range(2):
            own = low if side == 0 else jnp.logical_not(low)
            q_own = q_pair * jnp.where(own, score_scale, 0.0).astype(BF16)
            scores = mm(k_pair, q_own, NT) + key_bias
            expo = jnp.exp(scores - jnp.max(scores, axis=0, keepdims=True))
            soft = (expo * (1.0 / jnp.sum(expo, axis=0, keepdims=True))).astype(BF16)
            soft_ref[2 * pair + side] = soft
            mixed = mm(v_pair, soft, TN)
            begin = side * HD
            mixed_ref[pair * LANES + begin : pair * LANES + begin + HD, :] = mixed[
                begin : begin + HD
            ].astype(BF16)
    ready(7)
    part_ref[...] = lay.cut(mm(mixed_ref[...], w_out_ref[...], TN), s).astype(BF16)


def mlp_kernel(
    lay, s, tok_ref, own_ref, other_ref, b_out_ref, gain_ref, bias_ref, w_up_ref, b_up_ref,
    active_grad_ref, before_ref,
    hidden_ref, normed_ref, active_ref, upper_low_ref, sums_ref, *refs,
):
    attended = lay.fill(own_ref[...].astype(F32) + other_ref[...].astype(F32), s)
    hidden = lay.pick(tok_ref[...].astype(F32), s) + attended + row_of(b_out_ref)
    hidden_ref[...] = hidden
    unit, _ = unit_of(hidden)
    normed = (unit * row_of(gain_ref) + row_of(bias_ref)).astype(BF16)
    turn(normed.astype(F32), normed_ref)
    sums_ref[...] = before_ref[...]
    b_up = row_of(b_up_ref)
    width, model = w_up_ref.shape[1], tok_ref.shape[1]
    step = 768
    for begin in range(0, width, step):
        units = slice(begin, begin + step)
        upper = mm(normed, w_up_ref[:, units]) + b_up[:, units]
        cdf = 0.5 * (1.0 + lax.erf(upper * math.sqrt(0.5)))
        density = jnp.exp(upper * upper * -0.5) * (1.0 / math.sqrt(2.0 * math.pi))
        active_ref[:, units] = (upper * cdf).astype(BF16)
        upper_grad = active_grad_ref[:, units] * (cdf + upper * density)
        add_sums(sums_ref, ROW_UP + begin // model, column_sums(upper_grad))
        upper_low_ref[:, units] = upper_grad.astype(BF16)
    if refs:
        back_kernel(lay, s, upper_low_ref, w_up_ref, *refs)


def back_kernel(lay, s, upper_low_ref, w_up_ref, back_ref):
    back_ref[...] = lay.cut(mm(upper_low_ref[...], w_up_ref[...], NT), s).astype(BF16)


def last_kernel(lay, *refs):
    count = lay.slices
    active, first_back = refs[:count], refs[count : 2 * count]
    w_down_ref, last_ref = refs[2 * count :]
    for s in range(count):
        last_ref[2 * s] = first_back[s][...]
        last_ref[2 * s + 1] = lay.cut(mm(active[s][...], w_down_ref[...]), s).astype(BF16)


def attend_back_kernel(
    lay, s, hidden_ref, own_ref, other_ref, cot_ref, gain_ref, w_out_ref, q_ref, k_ref, v_ref,
    soft_ref, w_qkv_ref, tok_ref, before_ref,
    hidden_grad_ref, hidden_low_ref, grads_ref, back_ref, sums_ref, query_t,
):
    unit, scaled = unit_of(hidden_ref[...])
    upstream = lay.fill(own_ref[...].astype(F32) + other_ref[...].astype(F32), s)
    cot = jnp.where(lay.real(s), lay.pick(cot_ref[...].astype(F32), s), 0.0)
    hidden_grad = cot + norm_back(upstream, unit, scaled, row_of(gain_ref))
    hidden_grad_ref[...] = hidden_grad
    hidden_low = hidden_grad.astype(BF16)
    hidden_low_ref[...] = hidden_low
    sums_ref[...] = before_ref[...]
    add_row = partial(add_sums, sums_ref)
    add_row(ROW_GAIN2, column_sums(upstream * unit))
    add_row(ROW_BIAS2, column_sums(upstream))
    add_row(ROW_OUT, column_sums(hidden_grad))
    width = q_ref.shape[1]
    score_scale = 1.0 / math.sqrt(HD)
    low = low_head()
    for pair in range(width // LANES):
        lanes = slice(pair * LANES, (pair + 1) * LANES)
        q_pair, k_pair, v_pair = q_ref[:, lanes], k_ref[:, lanes], v_ref[:, lanes]
        mixed_grad = mm(hidden_low, w_out_ref[lanes, :], NT).astype(BF16)
        keys, values = [], []
        for side in range(2):
            own = low if side == 0 else jnp.logical_not(low)
            soft_low = soft_ref[2 * pair + side]
            soft = soft_low.astype(F32)
            own_grad = mixed_grad * jnp.where(own, 1.0, 0.0).astype(BF16)
            prob_grad = mm(v_pair, own_grad, NT)
            inner = jnp.sum(soft * prob_grad, axis=0, keepdims=True)
            score_grad = (soft * (prob_grad - inner)).astype(BF16)
            values.append(mm(soft_low, mixed_grad))
            keys.append(mm(score_grad, q_pair))
            query = mm(k_pair, score_grad, TN)
            begin = side * HD
            query_t[pair * LANES + begin : pair * LANES + begin + HD, :] = query[begin : begin + HD]
        grads_ref[0, :, lanes] = (jnp.transpose(query_t[lanes, :]) * score_scale).astype(BF16)
        grads_ref[1, :, lanes] = (jnp.where(low, keys[0], keys[1]) * score_scale).astype(BF16)
        grads_ref[2, :, lanes] = jnp.where(low, values[0], values[1]).astype(BF16)
    for half, part in enumerate((0, 2)):
        row = 2 * ROW_QV + half
        sums_ref[row : row + 1, :] += column_sums(grads_ref[part].astype(F32))
    back = mm(grads_ref[0], w_qkv_ref[0], NT)
    back += mm(grads_ref[1], w_qkv_ref[1], NT)
    back += mm(grads_ref[2], w_qkv_ref[2], NT)
    back_ref[...] = lay.cut(back, s).astype(BF16)
    unit, _ = unit_of(lay.pick(tok_ref[...].astype(F32), s))
    add_row(ROW_GAIN1, column_sums(back * unit))
    add_row(ROW_BIAS1, column_sums(back))


def finish_kernel(lay, *refs):
    count = lay.slices
    tok_ref, gain_ref, bias_ref = refs[:3]
    own_ref, other_ref = refs[3:5]
    hidden_grad, hidden = (refs[5 + k * count : 5 + (k + 1) * count] for k in range(2))
    block_ref, grad_ref = refs[-2:]
    gain, bias = row_of(gain_ref), row_of(bias_ref)
    tokens = tok_ref[...].astype(F32)
    results, blocks = [], []
    for s in range(count):
        both = lambda which: lay.fill(
            own_ref[2 * s + which].astype(F32) + other_ref[2 * s + which].astype(F32), s
        )
        unit, scaled = unit_of(lay.pick(tokens, s))
        results.append(hidden_grad[s][...] + norm_back(both(0), unit, scaled, gain))
        blocks.append(hidden[s][...] + both(1) + bias)
    grad_ref[...] = lay.join(*results)
    block_ref[...] = lay.join(*blocks)


def turn(values, target):
    turned = jnp.transpose(values).astype(BF16)
    blocks, rows, _ = target.shape
    for block in range(blocks):
        target[block] = turned[block * rows : (block + 1) * rows]


def early_kernel(lay, cot_ref, w_down_ref, *refs):
    count = lay.slices
    normed, cot_turned, turned, active_grad = (refs[k * count : (k + 1) * count] for k in range(4))
    sums_ref = refs[-1]
    sums_ref[...] = jnp.zeros(sums_ref.shape, F32)
    for s in range(count):
        cot = jnp.where(lay.real(s), lay.pick(cot_ref[...].astype(F32), s), 0.0)
        add_sums(sums_ref, ROW_DOWN, column_sums(cot))
        turn(cot, cot_turned[s])
        turn(normed[s][...].astype(F32), turned[s])
        active_grad[s][...] = mm(cot.astype(BF16), w_down_ref[...], NT)


def wait_kernel(out_ref):
    out_ref[...] = jnp.zeros(out_ref.shape, F32)


def gram_kernel(lay, groups, keeps, *refs):
    count = lay.slices
    ins = 2 * count * len(groups)
    fresh = any(kind == "right" for kind in groups)
    scratch = refs[-count:] if fresh else ()
    keep_refs = refs[ins : ins + keeps]
    send_refs = refs[ins + keeps : len(refs) - len(scratch)]
    tier, _, _, wide = send_refs[0].shape
    each = keep_refs[0].shape[-1] // wide
    held = keep_refs[0].shape[0]
    blocks, rows = 2 * keep_refs[0].shape[1], keep_refs[0].shape[2]
    parity = share_bit(0)
    plane = 0
    for group, kind in enumerate(groups):
        lefts = refs[2 * count * group : 2 * count * group + count]
        rights = refs[2 * count * group + count : 2 * count * (group + 1)]
        flips = lefts
        if kind == "right":
            flips = scratch
            for left, flip in zip(lefts, flips):
                turn(left[...].astype(F32), flip)
        planes = rights[0].shape[0] if len(rights[0].shape) == 3 else 1
        width = keep_refs[0].shape[-1]
        step = min(width, 768)
        for sent, which in ((True, 1 - parity), (False, parity)):
            halves = [
                jnp.concatenate([flip[2 * block + which] for block in range(blocks // 2)], axis=0)
                for flip in flips
            ]
            for own in range(planes):
                for begin in range(0, width, step):
                    columns = slice(begin, begin + step)
                    total = None
                    for half, right in zip(halves, rights):
                        if kind == "right":
                            term = mm(half, right[...], NT)
                        elif planes > 1:
                            term = mm(half, right[own, :, columns])
                        else:
                            term = mm(half, right[:, columns])
                        total = term if total is None else total + term
                    total = total.astype(BF16)
                    for block in range(blocks // 2):
                        values = total[block * rows : (block + 1) * rows]
                        if not sent:
                            keep_refs[(plane + own) // held][
                                (plane + own) % held, block, :, columns
                            ] = values
                            continue
                        for at in range(0, step, min(step, wide)):
                            piece = (plane + own) // tier * each + (begin + at) // wide
                            place = (begin + at) % wide
                            send_refs[piece][
                                (plane + own) % tier, block, :, place : place + min(step, wide)
                            ] = values[:, at : at + wide]
        plane += planes


def pack(sums):
    high = sums.astype(BF16).astype(F32)
    low = (sums - high).astype(BF16).astype(F32)
    return jnp.concatenate([high, low], axis=0).astype(BF16), high + low


def unpack(packed):
    rows = packed.shape[0] // 2
    values = packed.astype(F32)
    return values[:rows] + values[rows:]


def store_small(total_ref, outs):
    rows = lambda place, count=2: [
        total_ref[2 * place + half : 2 * place + half + 1, :].reshape(-1) for half in range(count)
    ]
    width = total_ref.shape[1]
    for place, out in zip((ROW_GAIN1, ROW_BIAS1, ROW_OUT, ROW_GAIN2, ROW_BIAS2, ROW_DOWN, ROW_UP), outs[2:]):
        for half, values in enumerate(rows(place, out.shape[0] // width)):
            out[half * width : (half + 1) * width] = values
    for out, values in zip(outs[:2], rows(ROW_QV)):
        out[...] = values


def stage_kernel(items, merge, small, *refs):
    refs = list(refs)
    kept, came = [], []
    for _, _, pieces, _, _ in items:
        kept.append(refs.pop(0))
        came.append([refs.pop(0) for _ in range(pieces)])
    if small == "first":
        sums = refs.pop(0)[...] + refs.pop(0)[...]
    elif small:
        sums = refs.pop(0)[...] + unpack(came[0][0][came[0][0].shape[0] - 1])
    last = items[0][0] is None
    packed, held = pack(sums) if small and not last else (None, None)

    def total(item, plane, place, at):
        parts, blocks = came[item], items[item][4]
        if len(parts[0].shape) == 4:
            group, _, _, wide = parts[0].shape
            chunk = kept[item].shape[-1] // wide
            inside = slice(at.start % wide, at.start % wide + at.stop - at.start)
            part = parts[plane // group * chunk + at.start // wide][plane % group, place, :, inside]
        else:
            part = parts[0][plane * blocks + place, :, at]
        return kept[item][plane, place, :, at].astype(F32) + part.astype(F32)

    if last:
        count = items[0][3]
        if small:
            sums_ref = refs.pop()
            sums_ref[...] = sums
            store_small(sums_ref, [refs.pop() for _ in range(9)][::-1])
        for plane in range(count):
            at = 0
            while plane >= sum(out.shape[0] for out in refs[: at + 1]):
                at += 1
            before = sum(out.shape[0] for out in refs[:at])
            refs[at][plane - before] = total(0, plane, 0, slice(0, kept[0].shape[-1]))
        return
    base_plane = 0
    for item, (bit, low, pieces, planes, blocks) in enumerate(items):
        mine = share_bit(bit)
        out, keep = (refs[0], refs[1]) if merge else refs[2 * item : 2 * item + 2]
        columns = kept[item].shape[-1]
        wide = came[item][0].shape[-1]
        for plane in range(planes):
            for begin in range(0, columns, wide):
                at = slice(begin, begin + wide)
                for block in range(blocks // 2):
                    base = block // low * 2 * low + block % low
                    place = (base_plane + plane) * (blocks // 2) + block
                    out[place, :, at] = total(item, plane, base + (1 - mine) * low, at).astype(BF16)
                    keep[base_plane + plane, block, :, at] = total(item, plane, base + mine * low, at)
        if merge:
            base_plane += planes
    if small:
        target = refs[0]
        target[target.shape[0] - 1] = packed
        refs[-1][...] = held


class Order:
    def __init__(self):
        self.token = ()
        self.weight = 0

    def __call__(self, kernel, outs, args, scratch=(), limit=16, fresh=False, also=(), name=None):
        waits = (*self.token, *also)
        first, tokens = len(args), len(waits)

        def body(*refs):
            kernel(*refs[:first], *refs[first + tokens :])

        place = pltpu.HBM if fresh else pltpu.VMEM
        spaces = [pltpu.HBM if space else pltpu.VMEM for _, _, *space in outs]
        results = pl.pallas_call(
            body,
            out_shape=[space(item[0], item[1]) for space, item in zip(spaces, outs)],
            in_specs=[pl.BlockSpec(memory_space=pl.ANY if fresh else pltpu.VMEM)] * first
            + [pl.BlockSpec(memory_space=pl.ANY)] * tokens,
            out_specs=[pl.BlockSpec(memory_space=pltpu.VMEM)] * len(outs),
            scratch_shapes=list(scratch),
            compiler_params=pltpu.CompilerParams(vmem_limit_bytes=limit * MIB),
            cost_estimate=pl.CostEstimate(
                flops=1 + self.weight * 10**9, bytes_accessed=1, transcendentals=0
            ),
            name=name,
        )(*(pltpu.with_memory_space_constraint(array, place) for array in args), *waits)
        self.token = (pltpu.with_memory_space_constraint(results[-1], spaces[-1]),)
        return results


def gram(call, lay, groups, shares, keeps, cuts, name):
    first = groups[0][1][0]
    rows = first.shape[1]
    columns = groups[0][2][0].shape[-1]
    planes = sum(r[0].shape[0] if len(r[0].shape) == 3 else 1 for _, _, r in groups)
    kinds = tuple(kind for kind, _, _ in groups)
    results = call(
        partial(gram_kernel, lay, kinds, keeps),
        [((planes // keeps, shares // 2, rows, columns), BF16)] * keeps
        + [((planes // keeps, shares // 2, rows, columns // cuts), BF16)] * (keeps * cuts),
        [array for _, lefts, rights in groups for array in (*lefts, *rights)],
        scratch=[pltpu.VMEM(first.shape, BF16)] * (lay.slices if "right" in kinds else 0),
        name=name,
    )
    return results[:keeps], results[keeps:]


def plain_scatter(groups, shares):
    sums = []
    for kind, lefts, rights in groups:
        total = 0.0
        for left, right in zip(lefts, rights):
            if kind == "left":
                left = left.reshape(-1, left.shape[2]).T
            else:
                right = right.T
            right = right if len(right.shape) == 3 else right[None]
            total += jnp.einsum("rd,prc->pdc", left, right, preferred_element_type=F32)
        sums.append(total)
    kept = jnp.concatenate(sums, axis=0)
    planes, model, columns = kept.shape
    rows = model // shares
    for bit in range(shares.bit_length() - 1):
        view = kept.reshape(planes, -1, 2, rows, columns)
        mine = share_bit(bit)
        pick = lambda which: lax.dynamic_index_in_dim(view, which, 2, keepdims=False)
        kept = pick(mine) + flip(pick(1 - mine).astype(BF16), shares, bit).astype(F32)
    return kept[:, 0]


def plain_small(vector, shares):
    for bit in range(shares.bit_length() - 1):
        vector = vector + flip(vector, shares, bit)
    return vector + jnp.where(first_norm_rows(vector), swap(vector), 0.0)


def flip_pairs(shares, bit):
    return [(index, index ^ (1 << bit)) for index in range(shares)]


def flip(array, shares, bit):
    return lax.ppermute(array, "dp", flip_pairs(shares, bit))


class Sum:
    def __init__(self, kept, sent, shares, order):
        self.order = list(order)
        self.left = sorted(order, reverse=True)
        self.kept, self.shares = kept, shares
        self.send(sent, 0)

    def send(self, sent, bit):
        self.came = [flip(part, self.shares, bit) for part in sent]

    def next(self):
        planes, blocks = self.kept.shape[:2]
        if not self.order:
            return None, 0, len(self.came), planes, blocks
        bit = self.order.pop(0)
        low = 1 << (len(self.left) - 1 - self.left.index(bit))
        self.left.remove(bit)
        return bit, low, len(self.came), planes, blocks


def stage(call, sums, name, merge=False, small=None, small_args=(), last=()):
    items = tuple(item.next() for item in sums)
    args = [array for item in sums for array in (item.kept, *item.came)]
    rows, columns = sums[0].kept.shape[2:]
    extra = 1 if small else 0
    if last:
        scratch = [pltpu.VMEM(small_args[0].shape, F32)] if small else []
        return call(
            partial(stage_kernel, items, merge, small), list(last), [*args, *small_args], scratch, name=name
        )
    sizes = [(planes, blocks // 2) for _, _, _, planes, blocks in items]
    if merge:
        sizes = [(sum(planes for planes, _ in sizes), sizes[0][1])]
    outs = []
    for place, (planes, blocks) in enumerate(sizes):
        count = planes * blocks + (extra if place == 0 else 0)
        outs += [((count, rows, columns), BF16), ((planes, blocks, rows, columns), F32)]
    if small:
        outs.append((small_args[0].shape, F32))
    results = call(partial(stage_kernel, items, merge, small), outs, [*args, *small_args], name=name)
    for place, item in enumerate(sums[: len(sizes)]):
        item.kept = results[2 * place + 1]
        item.send([results[2 * place]], items[place][0])
    return results[-1]


def first_norm_rows(vector):
    place = lax.broadcasted_iota(jnp.int32, (vector.shape[0], 1), 0) // 2
    return (place == ROW_GAIN1) | (place == ROW_BIAS1)


def add_small_kernel(own_ref, other_ref, out_ref):
    own = own_ref[...]
    out_ref[...] = own + jnp.where(first_norm_rows(own), other_ref[...], 0.0)


def small_outputs(vector, units):
    two = lambda place, count=2: vector[2 * place : 2 * place + count].reshape(-1)
    return (
        vector[2 * ROW_QV], vector[2 * ROW_QV + 1], two(ROW_GAIN1), two(ROW_BIAS1), two(ROW_OUT),
        two(ROW_GAIN2), two(ROW_BIAS2), two(ROW_DOWN), two(ROW_UP, units // vector.shape[1]),
    )


def swap(rows):
    return lax.ppermute(rows, "tensor", [(0, 1), (1, 0)])


def local(
    shares, tokens, body_mask, ln1_gain, ln1_bias, w_qkv, b_q, b_v, w_out, b_out, ln2_gain, ln2_bias,
    w_up, b_up, w_down, b_down, cotangent,
):
    slices, seq = body_mask.shape
    rows, model = tokens.shape
    lay = Layout(rows, slices, seq)
    padded, sent = lay.padded, lay.sent
    width = w_qkv.shape[2]
    heads = width // HD
    units = w_up.shape[1]
    steps = shares.bit_length() - 1
    small_rows = 2 * ROW_UP + units // (model // 2)
    small_height = -(-small_rows // SUBLANES) * SUBLANES
    w_qkv = jnp.transpose(w_qkv, (1, 0, 2))
    wide, narrow, tall = ((padded, model), BF16), ((padded, width), BF16), ((padded, units), BF16)
    tuned = steps == 4 and model // shares == 2 * small_height and width == model // 2
    blocks = shares if tuned else 1
    flipped = ((blocks, model // blocks, padded), BF16)
    wide_f, crossing = ((padded, model), F32), ((sent, model), BF16)
    small = ((small_height, model // 2), F32)
    bias_row = pltpu.VMEM((SUBLANES, -(-padded // LANES) * LANES), F32)
    attend_outs = [
        crossing, wide, narrow, narrow, narrow, ((heads, padded, padded), BF16), ((width, padded), BF16)
    ]

    call = Order()
    state = {name: [None] * slices for name in (*ATTENDED, *UPPED, *RETURNED, *OTHERS)}
    held = {}
    sums = {}
    result = {}

    def keep(s, names, values):
        for name, value in zip(names, values):
            state[name][s] = value

    def attend(s):
        if s == 0:
            results = call(
                partial(first_attend_kernel, lay),
                attend_outs + [(w_qkv.shape, BF16), (w_out.shape, BF16), (tokens.shape, BF16)],
                (tokens, body_mask, ln1_gain, ln1_bias, w_qkv, b_q, b_v, w_out),
                scratch=[
                    pltpu.VMEM(body_mask.shape, jnp.int32),
                    *[pltpu.VMEM((size,), F32) for size in (model, model, width, width)],
                    bias_row,
                    pltpu.SemaphoreType.DMA((8,)),
                ],
                fresh=True,
                name="attend",
            )
            held["w_qkv"], held["w_out"], held["tokens"] = results[7:]
        else:
            results = call(
                partial(attend_kernel, lay, s),
                attend_outs,
                (held["tokens"], body_mask, ln1_gain, ln1_bias, held["w_qkv"], b_q, b_v, held["w_out"]),
                scratch=[bias_row],
                name="attend",
            )
        keep(s, ATTENDED, results)
        state["other"][s] = swap(state["part"][s])

    def early():
        results = call(
            partial(early_kernel, lay),
            [flipped] * (2 * slices) + [((padded, units), F32)] * slices + [small],
            (cotangent, w_down, *state["normed"]),
            name="early",
        )
        for name, place in (("cot_turned", 0), ("turned", 1), ("active_grad", 2)):
            state[name] = results[place * slices : (place + 1) * slices]
        held["vector"] = results[-1]

    def mlp(s):
        late = s == slices - 1
        results = call(
            partial(mlp_kernel, lay, s),
            [wide_f, flipped, tall, tall, small] + ([] if late else [crossing]),
            (
                held["tokens"], state["part"][s], state["other"][s], b_out, ln2_gain, ln2_bias, w_up,
                b_up, state["active_grad"][s], held["vector"],
            ),
            name="mlp",
        )
        keep(s, UPPED, results)
        held["vector"] = results[4]
        if not late:
            send_back(s, results[5])

    def send_back(s, back):
        state["back"][s] = back
        state["other"][s] = swap(back)

    def late_back(s):
        args = (state["upper_low"][s], w_up)
        send_back(s, call(partial(back_kernel, lay, s), [crossing], args, name="back")[0])

    def last():
        held["last"] = call(
            partial(last_kernel, lay),
            [((2 * slices, sent, model), BF16)],
            (*state["active"], *state["first_back"], w_down),
            name="last",
        )[0]
        held["last_other"] = swap(held["last"])

    def attend_back(s):
        results = call(
            partial(attend_back_kernel, lay, s),
            [wide_f, wide, ((3, padded, width), BF16), crossing, small],
            (
                *(state[name][s] for name in ("hidden", "back", "other")), cotangent, ln2_gain,
                held["w_out"], *(state[name][s] for name in ("q", "k", "v", "soft")), held["w_qkv"],
                held["tokens"], held["vector"],
            ),
            scratch=[pltpu.VMEM((width, padded), F32)],
            name="attend_back",
        )
        keep(s, RETURNED, results)
        held["vector"] = results[4]
        if s == slices - 1:
            held["vector_other"] = swap(held["vector"])

    def finish():
        result["rows"] = call(
            partial(finish_kernel, lay),
            [((rows, model), F32, True)] * 2,
            (
                held["tokens"], ln1_gain, b_down, held["last"], held["last_other"],
                *state["hidden_grad"], *state["hidden"],
            ),
            name="finish",
        )

    grams = {
        "D": lambda: [("left", state["cot_turned"], state["active"])],
        "U": lambda: [("left", state["normed2"], state["upper_low"])],
        "Q": lambda: [
            ("left", state["turned"], state["qkv_grad"]),
            ("right", state["hidden_low"], state["mixed"]),
        ],
    }
    near, far = (1, 2, 3), (2, 1, 3)
    share = lambda planes, columns: ((planes, model // shares, columns), F32, True)

    def step_mlp(step):
        sums = [held["U"], held["D"]] if step < 4 else [held["U"]]
        last = [share(1, units), share(1, units)] if step == 4 else ()
        done = stage(call, sums, "sum_mlp_" + "abcd"[step - 1], merge=step == 3, last=last)
        if last:
            result["U"], result["D"] = done

    def step_qkv(step):
        sums = held["Q"] if step < 4 else held["Q"][:1]
        small_kind = {1: "first", 4: "last"}.get(step, "next")
        last = ()
        if step == 4:
            last = [share(3, width), share(1, width)] + [
                ((size,), F32, True)
                for size in (width, width, model, model, model, model, model, model, units)
            ]
        args = (held["vector"], held["vector_other"]) if step == 1 else (held["vector"],)
        done = stage(call, sums, "sum_qkv_" + "abcd"[step - 1], step == 3, small_kind, args, last)
        if last:
            result["Q"], result["O"], *result["small"] = done
        else:
            held["vector"] = done

    for item in ORDER:
        kind, place = item[0], item[1:]
        call.weight = WEIGHT.get(item, 0)
        if kind == "A":
            attend(int(place))
        elif kind == "B":
            mlp(int(place))
        elif kind == "C":
            attend_back(int(place))
        elif kind == "F":
            finish()
        elif kind == "T":
            early()
        elif kind == "R":
            late_back(int(place))
        elif kind == "L":
            last()
        elif kind == "X":
            call(wait_kernel, [((SUBLANES, LANES), F32)], (), also=state["other"][:1], name="wait")
        elif not tuned:
            continue
        elif kind == "Y":
            call(wait_kernel, [((SUBLANES, LANES), F32)], (), also=held["U"].came, name="wait")
        elif kind == "s":
            held["vector"] = call(
                add_small_kernel, [small], [held["vector"], held["vector_other"]], name="add_small"
            )[0]
            held["vector_other"] = flip(held["vector"], shares, 0)
        elif kind == "G":
            keeps = 2 if place == "Q" else 1
            cuts = CUTS.get(place, 1)
            kept, pieces = gram(call, lay, grams[place](), shares, keeps, cuts, "gram_" + place.lower())
            if place == "Q":
                held["Q"] = [
                    Sum(kept[0], pieces[:cuts], shares, near),
                    Sum(kept[1], pieces[cuts:], shares, far),
                ]
            else:
                held[place] = Sum(kept[0], pieces, shares, near if place == "U" else far)
        elif kind == "M":
            step_mlp(int(place))
        else:
            step_qkv(int(place))
    if not tuned:
        for name in "DU":
            result[name] = plain_scatter(grams[name](), shares)
        total = plain_scatter(grams["Q"](), shares)
        result["Q"], result["O"] = total[:3], total[3:]
        result["small"] = small_outputs(plain_small(held["vector"], shares), units)

    (
        sum_b_q, sum_b_v, sum_ln1_gain, sum_ln1_bias, sum_b_out, sum_ln2_gain, sum_ln2_bias, sum_b_down,
        sum_b_up,
    ) = result["small"]
    block_out, grad_tokens = result["rows"]
    return (
        block_out,
        grad_tokens,
        sum_ln1_gain,
        sum_ln1_bias,
        jnp.transpose(result["Q"], (1, 0, 2)),
        sum_b_q,
        sum_b_v,
        result["O"][0].T,
        sum_b_out,
        sum_ln2_gain,
        sum_ln2_bias,
        result["U"][0],
        sum_b_up,
        result["D"][0].T,
        sum_b_down,
    )


def solution(mesh):
    return jax.shard_map(
        partial(local, mesh.shape["dp"]),
        mesh=mesh,
        in_specs=(
            P("dp", None),
            P("dp", None),
            P(),
            P(),
            P(None, None, "tensor"),
            P("tensor"),
            P("tensor"),
            P("tensor", None),
            P(),
            P(),
            P(),
            P(None, "tensor"),
            P("tensor"),
            P("tensor", None),
            P(),
            P("dp", None),
        ),
        out_specs=(
            P("dp", None),
            P("dp", None),
            P(),
            P(),
            P("dp", None, "tensor"),
            P("tensor"),
            P("tensor"),
            P("tensor", "dp"),
            P(),
            P(),
            P(),
            P("dp", "tensor"),
            P("tensor"),
            P("tensor", "dp"),
            P(),
        ),
        check_vma=False,
    )
```

```python
import math
from functools import partial

import jax
import jax.numpy as jnp
from jax import lax
from jax.experimental import pallas as pl
from jax.experimental.pallas import tpu as pltpu
from jax.sharding import PartitionSpec as P

HD = 64
LANES = 128
SUBLANES = 8
ROW_TILE = 16
F32 = jnp.float32
BF16 = jnp.bfloat16
MIB = 1024 * 1024

ORDER = (
    "W", "A0", "A1", "T", "B0", "B1", "GU", "GD", "R1", "X", "Y", "M1",
    "C0", "C1", "GQ", "s1", "L", "M2", "Q1", "M3", "Q2", "Q3", "M4", "F",
    "Q4",
)
WEIGHT = {"T": 6, "B1": 8, "X": 12, "Y": 3, "C0": 4, "C1": 8, "GQ": 4, "M2": 12, "M3": 12, "F": 2}
CUTS = {"U": 1, "D": 1}

ATTENDED = ("crossing", "normed", "q", "k", "v", "soft", "mixed")
UPPED = ("hidden", "normed2", "active", "upper_low")
RETURNED = ("hidden_grad", "hidden_low", "qkv_grad", "first_back")
OTHERS = ("back", "other", "cot_turned", "turned", "active_grad")

NN = (((1,), (0,)), ((), ()))
NT = (((1,), (1,)), ((), ()))
TN = (((0,), (0,)), ((), ()))

ROW_DOWN, ROW_GAIN2, ROW_BIAS2, ROW_OUT, ROW_QV, ROW_GAIN1, ROW_BIAS1, ROW_UP = range(8)


def mm(left, right, dims=NN):
    return lax.dot_general(left, right, dims, preferred_element_type=F32)


def unit_of(source):
    center = source - jnp.mean(source, axis=-1, keepdims=True)
    scaled = lax.rsqrt(jnp.mean(center * center, axis=-1, keepdims=True) + 1e-06)
    return center * scaled, scaled


def norm_back(upstream, unit_rows, scaled, gain_vec):
    inner = upstream * gain_vec
    return scaled * (
        inner
        - jnp.mean(inner, axis=-1, keepdims=True)
        - unit_rows * jnp.mean(inner * unit_rows, axis=-1, keepdims=True)
    )


def column_sums(rows):
    return jnp.sum(rows, axis=0, keepdims=True)


def add_sums(sums_ref, place, sums):
    width = sums_ref.shape[1]
    for half in range(sums.shape[1] // width):
        row = 2 * place + half
        sums_ref[row : row + 1, :] += sums[:, half * width : (half + 1) * width]


def row_of(ref):
    return ref[...].reshape(1, -1)


def share_bit(bit):
    return (lax.axis_index("dp").astype(jnp.int32) >> bit) & 1


def low_head():
    return lax.broadcasted_iota(jnp.int32, (1, LANES), 1) < HD


class Layout:
    def __init__(self, rows, slices, seq):
        self.rows, self.slices, self.seq = rows, slices, seq
        self.padded = -(-seq // ROW_TILE) * ROW_TILE
        self.sent = -(-seq // SUBLANES) * SUBLANES

    def pick(self, values, s):
        start = s * (self.rows - self.padded)
        return values[start : start + self.padded]

    def real(self, s):
        place = lax.broadcasted_iota(jnp.int32, (self.padded, 1), 0)
        return place < self.seq if s == 0 else place >= self.padded - self.seq

    def cut(self, values, s):
        return values[: self.sent] if s == 0 else values[self.padded - self.sent :]

    def fill(self, values, s):
        extra = jnp.zeros((self.padded - self.sent, values.shape[1]), values.dtype)
        return jnp.concatenate([values, extra] if s == 0 else [extra, values], axis=0)

    def join(self, first, second):
        start = self.rows - self.padded
        place = lax.broadcasted_iota(jnp.int32, (self.padded - start, 1), 0) + start
        middle = jnp.where(place < self.seq, first[start:], second[: self.padded - start])
        return jnp.concatenate([first[:start], middle, second[self.padded - start :]], axis=0)


def half_kernel(w_ref, out_ref, sem):
    rows = out_ref.shape[0]
    begin = pl.multiple_of(share_bit(0) * rows, ROW_TILE)
    copy = pltpu.make_async_copy(w_ref.at[pl.ds(begin, rows)], out_ref, sem)
    copy.start()
    copy.wait()


def project(mixed, upper_rows, lower_rows):
    cut = upper_rows.shape[0]
    return mm(mixed[:, :cut], upper_rows) + mm(mixed[:, cut:], lower_rows)


def first_attend_kernel(lay, *refs):
    sources, outs = refs[:8], refs[8:15]
    w_qkv_ref, w_out_ref, tok_ref = refs[15:18]
    mask_ref, gain_ref, bias_ref, b_q_ref, b_v_ref, bias_row, sems = refs[18:]
    targets = (tok_ref, mask_ref, gain_ref, bias_ref, w_qkv_ref, b_q_ref, b_v_ref, w_out_ref)
    copies = [
        pltpu.make_async_copy(source, target, sems.at[place])
        for place, (source, target) in enumerate(zip(sources, targets))
    ]
    for place in (0, 2, 3, 4, 5, 6, 1, 7):
        copies[place].start()

    def ready(*places):
        for place in places:
            copies[place].wait()

    attend_kernel(lay, 0, *targets[:7], *outs, bias_row, ready)


def attend_kernel(
    lay, s, tok_ref, mask_ref, gain_ref, bias_ref, w_qkv_ref, b_q_ref, b_v_ref,
    crossing_ref, normed_ref, q_ref, k_ref, v_ref, soft_ref, mixed_ref, bias_row,
    ready=lambda *places: None,
):
    ready(0, 2, 3)
    unit, _ = unit_of(lay.pick(tok_ref[...].astype(F32), s))
    normed = (unit * row_of(gain_ref) + row_of(bias_ref)).astype(BF16)
    normed_ref[...] = normed
    ready(4, 5, 6, 1)
    q_ref[...] = (mm(normed, w_qkv_ref[0]) + row_of(b_q_ref)).astype(BF16)
    k_ref[...] = mm(normed, w_qkv_ref[1]).astype(BF16)
    v_ref[...] = (mm(normed, w_qkv_ref[2]) + row_of(b_v_ref)).astype(BF16)
    bias_row[...] = jnp.full(bias_row.shape, -1e30, F32)
    bias_row[0:1, : lay.seq] = jnp.where(mask_ref[s : s + 1, :] > 0, 0.0, -1e30)
    lanes_bias = bias_row[...]
    if s:
        lanes_bias = pltpu.roll(lanes_bias, lay.padded - lay.seq, 1)
    turned = jnp.transpose(jnp.broadcast_to(lanes_bias[0:1], (LANES, lanes_bias.shape[1])))
    turned = turned[: lay.padded]
    key_bias = jnp.concatenate([turned] * -(-lay.padded // LANES), axis=1)[:, : lay.padded]
    score_scale = 1.0 / math.sqrt(HD)
    low = low_head()
    for pair in range(q_ref.shape[1] // LANES):
        lanes = slice(pair * LANES, (pair + 1) * LANES)
        q_pair, k_pair, v_pair = q_ref[:, lanes], k_ref[:, lanes], v_ref[:, lanes]
        halves = []
        for side in range(2):
            own = low if side == 0 else jnp.logical_not(low)
            q_own = q_pair * jnp.where(own, score_scale, 0.0).astype(BF16)
            scores = mm(k_pair, q_own, NT) + key_bias
            expo = jnp.exp(scores - jnp.max(scores, axis=0, keepdims=True))
            soft = (expo * (1.0 / jnp.sum(expo, axis=0, keepdims=True))).astype(BF16)
            soft_ref[2 * pair + side] = soft
            begin = side * HD
            halves.append(mm(v_pair, soft, TN)[begin : begin + HD])
        mixed = jnp.transpose(jnp.concatenate(halves, axis=0))
        mixed_ref[:, lanes] = mixed.astype(BF16)
        crossing_ref[:, lanes] = lay.cut(mixed, s).astype(BF16)
    ready(7)


def mlp_kernel(
    lay, s, tok_ref, own_ref, other_ref, w_out_ref, near_ref, far_ref, b_out_ref, gain_ref, bias_ref,
    w_up_ref, b_up_ref, active_grad_ref, before_ref,
    hidden_ref, normed_ref, active_ref, upper_low_ref, sums_ref, *refs,
):
    *refs, products = refs
    cut = near_ref.shape[0]
    upper_half = share_bit(0) == 0
    near, far = near_ref[...], far_ref[...]
    products[0] = project(own_ref[...], w_out_ref[:cut], w_out_ref[cut:])
    products[1] = project(
        lay.fill(other_ref[...].astype(F32), s).astype(BF16),
        jnp.where(upper_half, near, far),
        jnp.where(upper_half, far, near),
    )
    attended = products[0] + products[1]
    hidden = lay.pick(tok_ref[...].astype(F32), s) + attended + row_of(b_out_ref)
    hidden_ref[...] = hidden
    unit, _ = unit_of(hidden)
    normed = (unit * row_of(gain_ref) + row_of(bias_ref)).astype(BF16)
    turn(normed.astype(F32), normed_ref)
    sums_ref[...] = before_ref[...]
    b_up = row_of(b_up_ref)
    width, model = w_up_ref.shape[1], tok_ref.shape[1]
    step = 768
    for begin in range(0, width, step):
        units = slice(begin, begin + step)
        upper = mm(normed, w_up_ref[:, units]) + b_up[:, units]
        cdf = 0.5 * (1.0 + lax.erf(upper * math.sqrt(0.5)))
        density = jnp.exp(upper * upper * -0.5) * (1.0 / math.sqrt(2.0 * math.pi))
        active_ref[:, units] = (upper * cdf).astype(BF16)
        upper_grad = active_grad_ref[:, units] * (cdf + upper * density)
        add_sums(sums_ref, ROW_UP + begin // model, column_sums(upper_grad))
        upper_low_ref[:, units] = upper_grad.astype(BF16)
    if refs:
        back_kernel(lay, s, upper_low_ref, w_up_ref, *refs)


def back_kernel(lay, s, upper_low_ref, w_up_ref, back_ref):
    back_ref[...] = lay.cut(mm(upper_low_ref[...], w_up_ref[...], NT), s).astype(BF16)


def last_kernel(lay, *refs):
    count = lay.slices
    active, first_back = refs[:count], refs[count : 2 * count]
    w_down_ref, last_ref = refs[2 * count :]
    for s in range(count):
        last_ref[2 * s] = first_back[s][...]
        last_ref[2 * s + 1] = lay.cut(mm(active[s][...], w_down_ref[...]), s).astype(BF16)


def attend_back_kernel(
    lay, s, hidden_ref, own_ref, other_ref, cot_ref, gain_ref, w_out_ref, q_ref, k_ref, v_ref,
    soft_ref, w_qkv_ref, tok_ref, before_ref,
    hidden_grad_ref, hidden_low_ref, grads_ref, back_ref, sums_ref, query_t,
):
    unit, scaled = unit_of(hidden_ref[...])
    upstream = lay.fill(own_ref[...].astype(F32) + other_ref[...].astype(F32), s)
    cot = jnp.where(lay.real(s), lay.pick(cot_ref[...].astype(F32), s), 0.0)
    hidden_grad = cot + norm_back(upstream, unit, scaled, row_of(gain_ref))
    hidden_grad_ref[...] = hidden_grad
    hidden_low = hidden_grad.astype(BF16)
    hidden_low_ref[...] = hidden_low
    sums_ref[...] = before_ref[...]
    add_row = partial(add_sums, sums_ref)
    add_row(ROW_GAIN2, column_sums(upstream * unit))
    add_row(ROW_BIAS2, column_sums(upstream))
    add_row(ROW_OUT, column_sums(hidden_grad))
    width = q_ref.shape[1]
    score_scale = 1.0 / math.sqrt(HD)
    low = low_head()
    for pair in range(width // LANES):
        lanes = slice(pair * LANES, (pair + 1) * LANES)
        q_pair, k_pair, v_pair = q_ref[:, lanes], k_ref[:, lanes], v_ref[:, lanes]
        mixed_grad = mm(hidden_low, w_out_ref[lanes, :], NT).astype(BF16)
        keys, values = [], []
        for side in range(2):
            own = low if side == 0 else jnp.logical_not(low)
            soft_low = soft_ref[2 * pair + side]
            soft = soft_low.astype(F32)
            own_grad = mixed_grad * jnp.where(own, 1.0, 0.0).astype(BF16)
            prob_grad = mm(v_pair, own_grad, NT)
            inner = jnp.sum(soft * prob_grad, axis=0, keepdims=True)
            score_grad = (soft * (prob_grad - inner)).astype(BF16)
            values.append(mm(soft_low, mixed_grad))
            keys.append(mm(score_grad, q_pair))
            query = mm(k_pair, score_grad, TN)
            begin = side * HD
            query_t[pair * LANES + begin : pair * LANES + begin + HD, :] = query[begin : begin + HD]
        grads_ref[0, :, lanes] = (jnp.transpose(query_t[lanes, :]) * score_scale).astype(BF16)
        grads_ref[1, :, lanes] = (jnp.where(low, keys[0], keys[1]) * score_scale).astype(BF16)
        grads_ref[2, :, lanes] = jnp.where(low, values[0], values[1]).astype(BF16)
    for half, part in enumerate((0, 2)):
        row = 2 * ROW_QV + half
        sums_ref[row : row + 1, :] += column_sums(grads_ref[part].astype(F32))
    back = mm(grads_ref[0], w_qkv_ref[0], NT)
    back += mm(grads_ref[1], w_qkv_ref[1], NT)
    back += mm(grads_ref[2], w_qkv_ref[2], NT)
    back_ref[...] = lay.cut(back, s).astype(BF16)
    unit, _ = unit_of(lay.pick(tok_ref[...].astype(F32), s))
    add_row(ROW_GAIN1, column_sums(back * unit))
    add_row(ROW_BIAS1, column_sums(back))


def finish_kernel(lay, *refs):
    count = lay.slices
    tok_ref, gain_ref, bias_ref = refs[:3]
    own_ref, other_ref = refs[3:5]
    hidden_grad, hidden = (refs[5 + k * count : 5 + (k + 1) * count] for k in range(2))
    block_ref, grad_ref = refs[-2:]
    gain, bias = row_of(gain_ref), row_of(bias_ref)
    tokens = tok_ref[...].astype(F32)
    results, blocks = [], []
    for s in range(count):
        both = lambda which: lay.fill(
            own_ref[2 * s + which].astype(F32) + other_ref[2 * s + which].astype(F32), s
        )
        unit, scaled = unit_of(lay.pick(tokens, s))
        results.append(hidden_grad[s][...] + norm_back(both(0), unit, scaled, gain))
        blocks.append(hidden[s][...] + both(1) + bias)
    grad_ref[...] = lay.join(*results)
    block_ref[...] = lay.join(*blocks)


def turn(values, target):
    turned = jnp.transpose(values).astype(BF16)
    blocks, rows, _ = target.shape
    for block in range(blocks):
        target[block] = turned[block * rows : (block + 1) * rows]


def early_kernel(lay, cot_ref, w_down_ref, *refs):
    count = lay.slices
    normed, cot_turned, turned, active_grad = (refs[k * count : (k + 1) * count] for k in range(4))
    sums_ref = refs[-1]
    sums_ref[...] = jnp.zeros(sums_ref.shape, F32)
    for s in range(count):
        cot = jnp.where(lay.real(s), lay.pick(cot_ref[...].astype(F32), s), 0.0)
        add_sums(sums_ref, ROW_DOWN, column_sums(cot))
        turn(cot, cot_turned[s])
        turn(normed[s][...].astype(F32), turned[s])
        active_grad[s][...] = mm(cot.astype(BF16), w_down_ref[...], NT)


def wait_kernel(out_ref):
    out_ref[...] = jnp.zeros(out_ref.shape, F32)


def gram_kernel(lay, groups, keeps, *refs):
    count = lay.slices
    ins = 2 * count * len(groups)
    fresh = any(kind == "plain" for kind in groups)
    scratch = refs[-count:] if fresh else ()
    keep_refs = refs[ins : ins + keeps]
    send_refs = refs[ins + keeps : len(refs) - len(scratch)]
    tier, _, _, wide = send_refs[0].shape
    each = keep_refs[0].shape[-1] // wide
    held = keep_refs[0].shape[0]
    blocks, rows = 2 * keep_refs[0].shape[1], keep_refs[0].shape[2]
    parity = share_bit(0)
    plane = 0
    for group, kind in enumerate(groups):
        lefts = refs[2 * count * group : 2 * count * group + count]
        rights = refs[2 * count * group + count : 2 * count * (group + 1)]
        flips = lefts
        if kind == "plain":
            flips = scratch
            for left, flip in zip(lefts, flips):
                turn(left[...].astype(F32), flip)
        planes = rights[0].shape[0] if len(rights[0].shape) == 3 else 1
        width = keep_refs[0].shape[-1]
        step = min(width, 768)
        for sent, which in ((True, 1 - parity), (False, parity)):
            halves = [
                jnp.concatenate([flip[2 * block + which] for block in range(blocks // 2)], axis=0)
                for flip in flips
            ]
            for own in range(planes):
                for begin in range(0, width, step):
                    columns = slice(begin, begin + step)
                    total = None
                    for half, right in zip(halves, rights):
                        if planes > 1:
                            term = mm(half, right[own, :, columns])
                        else:
                            term = mm(half, right[:, columns])
                        total = term if total is None else total + term
                    total = total.astype(BF16)
                    for block in range(blocks // 2):
                        values = total[block * rows : (block + 1) * rows]
                        if not sent:
                            keep_refs[(plane + own) // held][
                                (plane + own) % held, block, :, columns
                            ] = values
                            continue
                        for at in range(0, step, min(step, wide)):
                            piece = (plane + own) // tier * each + (begin + at) // wide
                            place = (begin + at) % wide
                            send_refs[piece][
                                (plane + own) % tier, block, :, place : place + min(step, wide)
                            ] = values[:, at : at + wide]
        plane += planes


def pack(sums):
    high = sums.astype(BF16).astype(F32)
    low = (sums - high).astype(BF16).astype(F32)
    return jnp.concatenate([high, low], axis=0).astype(BF16), high + low


def unpack(packed):
    rows = packed.shape[0] // 2
    values = packed.astype(F32)
    return values[:rows] + values[rows:]


def store_small(total_ref, outs):
    rows = lambda place, count=2: [
        total_ref[2 * place + half : 2 * place + half + 1, :].reshape(-1) for half in range(count)
    ]
    width = total_ref.shape[1]
    for place, out in zip((ROW_GAIN1, ROW_BIAS1, ROW_OUT, ROW_GAIN2, ROW_BIAS2, ROW_DOWN, ROW_UP), outs[2:]):
        for half, values in enumerate(rows(place, out.shape[0] // width)):
            out[half * width : (half + 1) * width] = values
    for out, values in zip(outs[:2], rows(ROW_QV)):
        out[...] = values


def stage_kernel(items, merge, small, *refs):
    refs = list(refs)
    kept, came = [], []
    for _, _, pieces, _, _ in items:
        kept.append(refs.pop(0))
        came.append([refs.pop(0) for _ in range(pieces)])
    if small == "first":
        sums = refs.pop(0)[...] + refs.pop(0)[...]
    elif small:
        sums = refs.pop(0)[...] + unpack(came[-1][0][came[-1][0].shape[0] - 1])
    last = items[0][0] is None
    packed, held = pack(sums) if small and not last else (None, None)

    def total(item, plane, place, at):
        parts, blocks = came[item], items[item][4]
        if len(parts[0].shape) == 4:
            group, _, _, wide = parts[0].shape
            chunk = kept[item].shape[-1] // wide
            inside = slice(at.start % wide, at.start % wide + at.stop - at.start)
            part = parts[plane // group * chunk + at.start // wide][plane % group, place, :, inside]
        else:
            part = parts[0][plane * blocks + place, :, at]
        return kept[item][plane, place, :, at].astype(F32) + part.astype(F32)

    if last:
        count = items[0][3]
        if small:
            sums_ref = refs.pop()
            sums_ref[...] = sums
            store_small(sums_ref, [refs.pop() for _ in range(9)][::-1])
        for plane in range(count):
            at = 0
            while plane >= sum(out.shape[0] for out in refs[: at + 1]):
                at += 1
            before = sum(out.shape[0] for out in refs[:at])
            refs[at][plane - before] = total(0, plane, 0, slice(0, kept[0].shape[-1]))
        return
    base_plane = 0
    for item, (bit, low, pieces, planes, blocks) in enumerate(items):
        mine = share_bit(bit)
        out, keep = (refs[0], refs[1]) if merge else refs[2 * item : 2 * item + 2]
        columns = kept[item].shape[-1]
        wide = came[item][0].shape[-1]
        for plane in range(planes):
            for begin in range(0, columns, wide):
                at = slice(begin, begin + wide)
                for block in range(blocks // 2):
                    base = block // low * 2 * low + block % low
                    place = (base_plane + plane) * (blocks // 2) + block
                    out[place, :, at] = total(item, plane, base + (1 - mine) * low, at).astype(BF16)
                    keep[base_plane + plane, block, :, at] = total(item, plane, base + mine * low, at)
        if merge:
            base_plane += planes
    if small:
        target = refs[0 if merge else 2 * len(items) - 2]
        target[target.shape[0] - 1] = packed
        refs[-1][...] = held


class Order:
    def __init__(self):
        self.token = ()
        self.weight = 0

    def __call__(self, kernel, outs, args, scratch=(), limit=16, fresh=False, also=(), name=None):
        waits = (*self.token, *also)
        first, tokens = len(args), len(waits)

        def body(*refs):
            kernel(*refs[:first], *refs[first + tokens :])

        place = pltpu.HBM if fresh else pltpu.VMEM
        spaces = [pltpu.HBM if space else pltpu.VMEM for _, _, *space in outs]
        results = pl.pallas_call(
            body,
            out_shape=[space(item[0], item[1]) for space, item in zip(spaces, outs)],
            in_specs=[pl.BlockSpec(memory_space=pl.ANY if fresh else pltpu.VMEM)] * first
            + [pl.BlockSpec(memory_space=pl.ANY)] * tokens,
            out_specs=[pl.BlockSpec(memory_space=pltpu.VMEM)] * len(outs),
            scratch_shapes=list(scratch),
            compiler_params=pltpu.CompilerParams(vmem_limit_bytes=limit * MIB),
            cost_estimate=pl.CostEstimate(
                flops=1 + self.weight * 10**9, bytes_accessed=1, transcendentals=0
            ),
            name=name,
        )(*(pltpu.with_memory_space_constraint(array, place) for array in args), *waits)
        self.token = (pltpu.with_memory_space_constraint(results[-1], spaces[-1]),)
        return results


def gram(call, lay, groups, shares, keeps, cuts, name):
    first = groups[0][1][0]
    rows = first.shape[1]
    columns = groups[0][2][0].shape[-1]
    planes = sum(r[0].shape[0] if len(r[0].shape) == 3 else 1 for _, _, r in groups)
    kinds = tuple(kind for kind, _, _ in groups)
    results = call(
        partial(gram_kernel, lay, kinds, keeps),
        [((planes // keeps, shares // 2, rows, columns), BF16)] * keeps
        + [((planes // keeps, shares // 2, rows, columns // cuts), BF16)] * (keeps * cuts),
        [array for _, lefts, rights in groups for array in (*lefts, *rights)],
        scratch=[pltpu.VMEM(first.shape, BF16)] * (lay.slices if "plain" in kinds else 0),
        name=name,
    )
    return results[:keeps], results[keeps:]


def plain_scatter(groups, shares):
    sums = []
    for kind, lefts, rights in groups:
        total = 0.0
        for left, right in zip(lefts, rights):
            if kind == "turned":
                left = left.reshape(-1, left.shape[2]).T
            right = right if len(right.shape) == 3 else right[None]
            total += jnp.einsum("rd,prc->pdc", left, right, preferred_element_type=F32)
        sums.append(total)
    kept = jnp.concatenate(sums, axis=0)
    planes, model, columns = kept.shape
    rows = model // shares
    for bit in range(shares.bit_length() - 1):
        view = kept.reshape(planes, -1, 2, rows, columns)
        mine = share_bit(bit)
        pick = lambda which: lax.dynamic_index_in_dim(view, which, 2, keepdims=False)
        kept = pick(mine) + flip(pick(1 - mine).astype(BF16), shares, bit).astype(F32)
    return kept[:, 0]


def plain_small(vector, shares):
    for bit in range(shares.bit_length() - 1):
        vector = vector + flip(vector, shares, bit)
    return vector + jnp.where(first_norm_rows(vector), swap(vector), 0.0)


def flip_pairs(shares, bit):
    return [(index, index ^ (1 << bit)) for index in range(shares)]


def flip(array, shares, bit):
    return lax.ppermute(array, "dp", flip_pairs(shares, bit))


class Sum:
    def __init__(self, kept, sent, shares, order):
        self.order = list(order)
        self.left = sorted(order, reverse=True)
        self.kept, self.shares = kept, shares
        self.send(sent, 0)

    def send(self, sent, bit):
        self.came = [flip(part, self.shares, bit) for part in sent]

    def next(self):
        planes, blocks = self.kept.shape[:2]
        if not self.order:
            return None, 0, len(self.came), planes, blocks
        bit = self.order.pop(0)
        low = 1 << (len(self.left) - 1 - self.left.index(bit))
        self.left.remove(bit)
        return bit, low, len(self.came), planes, blocks


def stage(call, sums, name, merge=False, small=None, small_args=(), last=()):
    items = tuple(item.next() for item in sums)
    args = [array for item in sums for array in (item.kept, *item.came)]
    rows, columns = sums[0].kept.shape[2:]
    extra = 1 if small else 0
    if last:
        scratch = [pltpu.VMEM(small_args[0].shape, F32)] if small else []
        return call(
            partial(stage_kernel, items, merge, small), list(last), [*args, *small_args], scratch, name=name
        )
    sizes = [(planes, blocks // 2) for _, _, _, planes, blocks in items]
    if merge:
        sizes = [(sum(planes for planes, _ in sizes), sizes[0][1])]
    outs = []
    for place, (planes, blocks) in enumerate(sizes):
        count = planes * blocks + (extra if place == len(sizes) - 1 else 0)
        outs += [((count, rows, columns), BF16), ((planes, blocks, rows, columns), F32)]
    if small:
        outs.append((small_args[0].shape, F32))
    results = call(partial(stage_kernel, items, merge, small), outs, [*args, *small_args], name=name)
    for place, item in enumerate(sums[: len(sizes)]):
        item.kept = results[2 * place + 1]
        item.send([results[2 * place]], items[place][0])
    return results[-1]


def first_norm_rows(vector):
    place = lax.broadcasted_iota(jnp.int32, (vector.shape[0], 1), 0) // 2
    return (place == ROW_GAIN1) | (place == ROW_BIAS1)


def add_small_kernel(own_ref, other_ref, out_ref):
    own = own_ref[...]
    out_ref[...] = own + jnp.where(first_norm_rows(own), other_ref[...], 0.0)


def small_outputs(vector, units):
    two = lambda place, count=2: vector[2 * place : 2 * place + count].reshape(-1)
    return (
        vector[2 * ROW_QV], vector[2 * ROW_QV + 1], two(ROW_GAIN1), two(ROW_BIAS1), two(ROW_OUT),
        two(ROW_GAIN2), two(ROW_BIAS2), two(ROW_DOWN), two(ROW_UP, units // vector.shape[1]),
    )


def swap(rows):
    return lax.ppermute(rows, "tensor", [(0, 1), (1, 0)])


def local(
    shares, tokens, body_mask, ln1_gain, ln1_bias, w_qkv, b_q, b_v, w_out, b_out, ln2_gain, ln2_bias,
    w_up, b_up, w_down, b_down, cotangent,
):
    slices, seq = body_mask.shape
    rows, model = tokens.shape
    lay = Layout(rows, slices, seq)
    padded, sent = lay.padded, lay.sent
    width = w_qkv.shape[2]
    heads = width // HD
    units = w_up.shape[1]
    steps = shares.bit_length() - 1
    small_rows = 2 * ROW_UP + units // (model // 2)
    small_height = -(-small_rows // SUBLANES) * SUBLANES
    w_qkv = jnp.transpose(w_qkv, (1, 0, 2))
    wide, narrow, tall = ((padded, model), BF16), ((padded, width), BF16), ((padded, units), BF16)
    tuned = steps == 4 and model // shares == 2 * small_height and width == model // 2
    blocks = shares if tuned else 1
    flipped = ((blocks, model // blocks, padded), BF16)
    wide_f, crossing = ((padded, model), F32), ((sent, model), BF16)
    small = ((small_height, model // 2), F32)
    bias_row = pltpu.VMEM((SUBLANES, -(-padded // LANES) * LANES), F32)
    attend_outs = [
        ((sent, width), BF16), wide, narrow, narrow, narrow, ((heads, padded, padded), BF16), narrow
    ]

    call = Order()
    state = {name: [None] * slices for name in (*ATTENDED, *UPPED, *RETURNED, *OTHERS)}
    held = {}
    sums = {}
    result = {}

    def keep(s, names, values):
        for name, value in zip(names, values):
            state[name][s] = value

    def attend(s):
        if s == 0:
            results = call(
                partial(first_attend_kernel, lay),
                attend_outs + [(w_qkv.shape, BF16), (w_out.shape, BF16), (tokens.shape, BF16)],
                (tokens, body_mask, ln1_gain, ln1_bias, w_qkv, b_q, b_v, w_out),
                scratch=[
                    pltpu.VMEM(body_mask.shape, jnp.int32),
                    *[pltpu.VMEM((size,), F32) for size in (model, model, width, width)],
                    bias_row,
                    pltpu.SemaphoreType.DMA((8,)),
                ],
                fresh=True,
                name="attend",
            )
            held["w_qkv"], held["w_out"], held["tokens"] = results[7:]
        else:
            results = call(
                partial(attend_kernel, lay, s),
                attend_outs,
                (held["tokens"], body_mask, ln1_gain, ln1_bias, held["w_qkv"], b_q, b_v),
                scratch=[bias_row],
                name="attend",
            )
        keep(s, ATTENDED, results)
        state["other"][s] = swap(state["crossing"][s])

    def weights():
        half = call(
            half_kernel,
            [((width // 2, model), BF16)],
            (w_out,),
            scratch=[pltpu.SemaphoreType.DMA],
            fresh=True,
            name="half",
        )[0]
        held["near"] = swap(half)
        held["far"] = flip(held["near"], shares, 0)

    def early():
        results = call(
            partial(early_kernel, lay),
            [flipped] * (2 * slices) + [((padded, units), F32)] * slices + [small],
            (cotangent, w_down, *state["normed"]),
            name="early",
        )
        for name, place in (("cot_turned", 0), ("turned", 1), ("active_grad", 2)):
            state[name] = results[place * slices : (place + 1) * slices]
        held["vector"] = results[-1]

    def mlp(s):
        late = s == slices - 1
        results = call(
            partial(mlp_kernel, lay, s),
            [wide_f, flipped, tall, tall, small] + ([] if late else [crossing]),
            (
                held["tokens"], state["mixed"][s], state["other"][s], held["w_out"], held["near"],
                held["far"], b_out, ln2_gain, ln2_bias, w_up, b_up, state["active_grad"][s],
                held["vector"],
            ),
            scratch=[pltpu.VMEM((2, padded, model), F32)],
            name="mlp",
        )
        keep(s, UPPED, results)
        held["vector"] = results[4]
        if not late:
            send_back(s, results[5])

    def send_back(s, back):
        state["back"][s] = back
        state["other"][s] = swap(back)

    def late_back(s):
        args = (state["upper_low"][s], w_up)
        send_back(s, call(partial(back_kernel, lay, s), [crossing], args, name="back")[0])

    def last():
        held["last"] = call(
            partial(last_kernel, lay),
            [((2 * slices, sent, model), BF16)],
            (*state["active"], *state["first_back"], w_down),
            name="last",
        )[0]
        held["last_other"] = swap(held["last"])

    def attend_back(s):
        results = call(
            partial(attend_back_kernel, lay, s),
            [wide_f, wide, ((3, padded, width), BF16), crossing, small],
            (
                *(state[name][s] for name in ("hidden", "back", "other")), cotangent, ln2_gain,
                held["w_out"], *(state[name][s] for name in ("q", "k", "v", "soft")), held["w_qkv"],
                held["tokens"], held["vector"],
            ),
            scratch=[pltpu.VMEM((width, padded), F32)],
            name="attend_back",
        )
        keep(s, RETURNED, results)
        held["vector"] = results[4]
        if s == slices - 1:
            held["vector_other"] = swap(held["vector"])

    def finish():
        result["rows"] = call(
            partial(finish_kernel, lay),
            [((rows, model), F32, True)] * 2,
            (
                held["tokens"], ln1_gain, b_down, held["last"], held["last_other"],
                *state["hidden_grad"], *state["hidden"],
            ),
            name="finish",
        )

    grams = {
        "D": lambda: [("turned", state["cot_turned"], state["active"])],
        "U": lambda: [("turned", state["normed2"], state["upper_low"])],
        "Q": lambda: [
            ("turned", state["turned"], state["qkv_grad"]),
            ("plain", state["hidden_low"], state["mixed"]),
        ],
    }
    near, far = (1, 2, 3), (2, 1, 3)
    share = lambda planes, columns: ((planes, model // shares, columns), F32, True)

    def step_mlp(step):
        sums = [held["D"], held["U"]] if step < 3 else [held["U"], held["D"]][: 5 - step]
        last = [share(1, units), share(1, units)] if step == 4 else ()
        done = stage(call, sums, "sum_mlp_" + "abcd"[step - 1], merge=step == 3, last=last)
        if last:
            result["U"], result["D"] = done

    def step_qkv(step):
        sums = held["Q"] if step < 4 else held["Q"][:1]
        small_kind = {1: "first", 4: "last"}.get(step, "next")
        last = ()
        if step == 4:
            last = [share(3, width), share(1, width)] + [
                ((size,), F32, True)
                for size in (width, width, model, model, model, model, model, model, units)
            ]
        args = (held["vector"], held["vector_other"]) if step == 1 else (held["vector"],)
        done = stage(call, sums, "sum_qkv_" + "abcd"[step - 1], step == 3, small_kind, args, last)
        if last:
            result["Q"], result["O"], *result["small"] = done
        else:
            held["vector"] = done

    for item in ORDER:
        kind, place = item[0], item[1:]
        call.weight = WEIGHT.get(item, 0)
        if kind == "W":
            weights()
        elif kind == "A":
            attend(int(place))
        elif kind == "B":
            mlp(int(place))
        elif kind == "C":
            attend_back(int(place))
        elif kind == "F":
            finish()
        elif kind == "T":
            early()
        elif kind == "R":
            late_back(int(place))
        elif kind == "L":
            last()
        elif kind == "X":
            call(wait_kernel, [((SUBLANES, LANES), F32)], (), also=state["other"][:1], name="wait")
        elif not tuned:
            continue
        elif kind == "Y":
            call(wait_kernel, [((SUBLANES, LANES), F32)], (), also=held["U"].came, name="wait")
        elif kind == "s":
            held["vector"] = call(
                add_small_kernel, [small], [held["vector"], held["vector_other"]], name="add_small"
            )[0]
            held["vector_other"] = flip(held["vector"], shares, 0)
        elif kind == "G":
            keeps = 2 if place == "Q" else 1
            cuts = CUTS.get(place, 1)
            kept, pieces = gram(call, lay, grams[place](), shares, keeps, cuts, "gram_" + place.lower())
            if place == "Q":
                held["Q"] = [
                    Sum(kept[0], pieces[:cuts], shares, far),
                    Sum(kept[1], pieces[cuts:], shares, near),
                ]
            else:
                held[place] = Sum(kept[0], pieces, shares, near if place == "U" else far)
        elif kind == "M":
            step_mlp(int(place))
        else:
            step_qkv(int(place))
    if not tuned:
        for name in "DU":
            result[name] = plain_scatter(grams[name](), shares)
        total = plain_scatter(grams["Q"](), shares)
        result["Q"], result["O"] = total[:3], total[3:]
        result["small"] = small_outputs(plain_small(held["vector"], shares), units)

    (
        sum_b_q, sum_b_v, sum_ln1_gain, sum_ln1_bias, sum_b_out, sum_ln2_gain, sum_ln2_bias, sum_b_down,
        sum_b_up,
    ) = result["small"]
    block_out, grad_tokens = result["rows"]
    return (
        block_out,
        grad_tokens,
        sum_ln1_gain,
        sum_ln1_bias,
        jnp.transpose(result["Q"], (1, 0, 2)),
        sum_b_q,
        sum_b_v,
        result["O"][0].T,
        sum_b_out,
        sum_ln2_gain,
        sum_ln2_bias,
        result["U"][0],
        sum_b_up,
        result["D"][0].T,
        sum_b_down,
    )


def solution(mesh):
    return jax.shard_map(
        partial(local, mesh.shape["dp"]),
        mesh=mesh,
        in_specs=(
            P("dp", None),
            P("dp", None),
            P(),
            P(),
            P(None, None, "tensor"),
            P("tensor"),
            P("tensor"),
            P("tensor", None),
            P(),
            P(),
            P(),
            P(None, "tensor"),
            P("tensor"),
            P("tensor", None),
            P(),
            P("dp", None),
        ),
        out_specs=(
            P("dp", None),
            P("dp", None),
            P(),
            P(),
            P("dp", None, "tensor"),
            P("tensor"),
            P("tensor"),
            P("tensor", "dp"),
            P(),
            P(),
            P(),
            P("dp", "tensor"),
            P("tensor"),
            P("tensor", "dp"),
            P(),
        ),
        check_vma=False,
    )
```

```python
import math
from functools import partial

import jax
import jax.numpy as jnp
from jax import lax
from jax.experimental import pallas as pl
from jax.experimental.pallas import tpu as pltpu
from jax.sharding import PartitionSpec as P

HD = 64
LANES = 128
SUBLANES = 8
ROW_TILE = 16
F32 = jnp.float32
BF16 = jnp.bfloat16
MIB = 1024 * 1024

ORDER = (
    "W", "A0", "A1", "T", "B0", "B1", "GU", "GD", "R1", "KU", "KD", "X",
    "Y", "M1", "C0", "C1", "GQ", "s1", "M2", "L", "Q1", "M3", "Q2", "Q3",
    "M4", "F", "Q4",
)
WEIGHT = {"T": 6, "B1": 8, "X": 10, "Y": 1, "C0": 4, "C1": 8, "GQ": 4, "M2": 12, "Q1": 6, "M3": 12, "F": 2}

ATTENDED = ("crossing", "normed", "q", "k", "v", "soft", "mixed")
UPPED = ("hidden", "normed2", "active", "upper_low")
RETURNED = ("hidden_grad", "hidden_low", "qkv_grad", "first_back")
OTHERS = ("back", "other", "cot_turned", "turned", "active_grad")

NN = (((1,), (0,)), ((), ()))
NT = (((1,), (1,)), ((), ()))
TN = (((0,), (0,)), ((), ()))

ROW_DOWN, ROW_GAIN2, ROW_BIAS2, ROW_OUT, ROW_QV, ROW_GAIN1, ROW_BIAS1, ROW_UP = range(8)


def mm(left, right, dims=NN):
    return lax.dot_general(left, right, dims, preferred_element_type=F32)


def unit_of(source):
    center = source - jnp.mean(source, axis=-1, keepdims=True)
    scaled = lax.rsqrt(jnp.mean(center * center, axis=-1, keepdims=True) + 1e-06)
    return center * scaled, scaled


def norm_back(upstream, unit_rows, scaled, gain_vec):
    inner = upstream * gain_vec
    return scaled * (
        inner
        - jnp.mean(inner, axis=-1, keepdims=True)
        - unit_rows * jnp.mean(inner * unit_rows, axis=-1, keepdims=True)
    )


def column_sums(rows):
    return jnp.sum(rows, axis=0, keepdims=True)


def add_sums(sums_ref, place, sums):
    width = sums_ref.shape[1]
    for half in range(sums.shape[1] // width):
        row = 2 * place + half
        sums_ref[row : row + 1, :] += sums[:, half * width : (half + 1) * width]


def row_of(ref):
    return ref[...].reshape(1, -1)


def share_bit(bit):
    return (lax.axis_index("dp").astype(jnp.int32) >> bit) & 1


def low_head():
    return lax.broadcasted_iota(jnp.int32, (1, LANES), 1) < HD


class Layout:
    def __init__(self, rows, slices, seq):
        self.rows, self.slices, self.seq = rows, slices, seq
        self.padded = -(-seq // ROW_TILE) * ROW_TILE
        self.sent = -(-seq // SUBLANES) * SUBLANES

    def pick(self, values, s):
        start = s * (self.rows - self.padded)
        return values[start : start + self.padded]

    def real(self, s):
        place = lax.broadcasted_iota(jnp.int32, (self.padded, 1), 0)
        return place < self.seq if s == 0 else place >= self.padded - self.seq

    def cut(self, values, s):
        return values[: self.sent] if s == 0 else values[self.padded - self.sent :]

    def fill(self, values, s):
        extra = jnp.zeros((self.padded - self.sent, values.shape[1]), values.dtype)
        return jnp.concatenate([values, extra] if s == 0 else [extra, values], axis=0)

    def join(self, first, second):
        start = self.rows - self.padded
        place = lax.broadcasted_iota(jnp.int32, (self.padded - start, 1), 0) + start
        middle = jnp.where(place < self.seq, first[start:], second[: self.padded - start])
        return jnp.concatenate([first[:start], middle, second[self.padded - start :]], axis=0)


def half_kernel(w_ref, out_ref, sem):
    rows = out_ref.shape[0]
    begin = pl.multiple_of(share_bit(0) * rows, ROW_TILE)
    copy = pltpu.make_async_copy(w_ref.at[pl.ds(begin, rows)], out_ref, sem)
    copy.start()
    copy.wait()


def project(mixed, upper_rows, lower_rows):
    cut = upper_rows.shape[0]
    return mm(mixed[:, :cut], upper_rows) + mm(mixed[:, cut:], lower_rows)


def first_attend_kernel(lay, *refs):
    sources, outs = refs[:8], refs[8:15]
    w_qkv_ref, w_out_ref, tok_ref = refs[15:18]
    mask_ref, gain_ref, bias_ref, b_q_ref, b_v_ref, bias_row, sems = refs[18:]
    targets = (tok_ref, mask_ref, gain_ref, bias_ref, w_qkv_ref, b_q_ref, b_v_ref, w_out_ref)
    copies = [
        pltpu.make_async_copy(source, target, sems.at[place])
        for place, (source, target) in enumerate(zip(sources, targets))
    ]
    for place in (0, 2, 3, 4, 5, 6, 1, 7):
        copies[place].start()

    def ready(*places):
        for place in places:
            copies[place].wait()

    attend_kernel(lay, 0, *targets[:7], *outs, bias_row, ready)


def attend_kernel(
    lay, s, tok_ref, mask_ref, gain_ref, bias_ref, w_qkv_ref, b_q_ref, b_v_ref,
    crossing_ref, normed_ref, q_ref, k_ref, v_ref, soft_ref, mixed_ref, bias_row,
    ready=lambda *places: None,
):
    ready(0, 2, 3)
    unit, _ = unit_of(lay.pick(tok_ref[...].astype(F32), s))
    normed = (unit * row_of(gain_ref) + row_of(bias_ref)).astype(BF16)
    normed_ref[...] = normed
    ready(4, 5, 6, 1)
    q_ref[...] = (mm(normed, w_qkv_ref[0]) + row_of(b_q_ref)).astype(BF16)
    k_ref[...] = mm(normed, w_qkv_ref[1]).astype(BF16)
    v_ref[...] = (mm(normed, w_qkv_ref[2]) + row_of(b_v_ref)).astype(BF16)
    bias_row[...] = jnp.full(bias_row.shape, -1e30, F32)
    bias_row[0:1, : lay.seq] = jnp.where(mask_ref[s : s + 1, :] > 0, 0.0, -1e30)
    lanes_bias = bias_row[...]
    if s:
        lanes_bias = pltpu.roll(lanes_bias, lay.padded - lay.seq, 1)
    turned = jnp.transpose(jnp.broadcast_to(lanes_bias[0:1], (LANES, lanes_bias.shape[1])))
    turned = turned[: lay.padded]
    key_bias = jnp.concatenate([turned] * -(-lay.padded // LANES), axis=1)[:, : lay.padded]
    score_scale = 1.0 / math.sqrt(HD)
    low = low_head()
    for pair in range(q_ref.shape[1] // LANES):
        lanes = slice(pair * LANES, (pair + 1) * LANES)
        q_pair, k_pair, v_pair = q_ref[:, lanes], k_ref[:, lanes], v_ref[:, lanes]
        halves = []
        for side in range(2):
            own = low if side == 0 else jnp.logical_not(low)
            q_own = q_pair * jnp.where(own, score_scale, 0.0).astype(BF16)
            scores = mm(k_pair, q_own, NT) + key_bias
            expo = jnp.exp(scores - jnp.max(scores, axis=0, keepdims=True))
            soft = (expo * (1.0 / jnp.sum(expo, axis=0, keepdims=True))).astype(BF16)
            soft_ref[2 * pair + side] = soft
            begin = side * HD
            halves.append(mm(v_pair, soft, TN)[begin : begin + HD])
        mixed = jnp.transpose(jnp.concatenate(halves, axis=0))
        mixed_ref[:, lanes] = mixed.astype(BF16)
        crossing_ref[:, lanes] = lay.cut(mixed, s).astype(BF16)
    ready(7)


def mlp_kernel(
    lay, s, tok_ref, own_ref, other_ref, w_out_ref, near_ref, far_ref, b_out_ref, gain_ref, bias_ref,
    w_up_ref, b_up_ref, active_grad_ref, before_ref,
    hidden_ref, normed_ref, active_ref, upper_low_ref, sums_ref, *refs,
):
    *refs, products = refs
    cut = near_ref.shape[0]
    upper_half = share_bit(0) == 0
    near, far = near_ref[...], far_ref[...]
    products[0] = project(own_ref[...], w_out_ref[:cut], w_out_ref[cut:])
    products[1] = project(
        lay.fill(other_ref[...].astype(F32), s).astype(BF16),
        jnp.where(upper_half, near, far),
        jnp.where(upper_half, far, near),
    )
    attended = products[0] + products[1]
    hidden = lay.pick(tok_ref[...].astype(F32), s) + attended + row_of(b_out_ref)
    hidden_ref[...] = hidden
    unit, _ = unit_of(hidden)
    normed = (unit * row_of(gain_ref) + row_of(bias_ref)).astype(BF16)
    turn(normed.astype(F32), normed_ref)
    sums_ref[...] = before_ref[...]
    b_up = row_of(b_up_ref)
    width, model = w_up_ref.shape[1], tok_ref.shape[1]
    step = 768
    for begin in range(0, width, step):
        units = slice(begin, begin + step)
        upper = mm(normed, w_up_ref[:, units]) + b_up[:, units]
        cdf = 0.5 * (1.0 + lax.erf(upper * math.sqrt(0.5)))
        density = jnp.exp(upper * upper * -0.5) * (1.0 / math.sqrt(2.0 * math.pi))
        active_ref[:, units] = (upper * cdf).astype(BF16)
        upper_grad = active_grad_ref[:, units] * (cdf + upper * density)
        add_sums(sums_ref, ROW_UP + begin // model, column_sums(upper_grad))
        upper_low_ref[:, units] = upper_grad.astype(BF16)
    if refs:
        back_kernel(lay, s, upper_low_ref, w_up_ref, *refs)


def back_kernel(lay, s, upper_low_ref, w_up_ref, back_ref):
    back_ref[...] = lay.cut(mm(upper_low_ref[...], w_up_ref[...], NT), s).astype(BF16)


def last_kernel(lay, *refs):
    count = lay.slices
    active, first_back = refs[:count], refs[count : 2 * count]
    w_down_ref, last_ref = refs[2 * count :]
    for s in range(count):
        last_ref[2 * s] = first_back[s][...]
        last_ref[2 * s + 1] = lay.cut(mm(active[s][...], w_down_ref[...]), s).astype(BF16)


def attend_back_kernel(
    lay, s, hidden_ref, own_ref, other_ref, cot_ref, gain_ref, w_out_ref, q_ref, k_ref, v_ref,
    soft_ref, w_qkv_ref, tok_ref, before_ref,
    hidden_grad_ref, hidden_low_ref, grads_ref, back_ref, sums_ref, query_t,
):
    unit, scaled = unit_of(hidden_ref[...])
    upstream = lay.fill(own_ref[...].astype(F32) + other_ref[...].astype(F32), s)
    cot = jnp.where(lay.real(s), lay.pick(cot_ref[...].astype(F32), s), 0.0)
    hidden_grad = cot + norm_back(upstream, unit, scaled, row_of(gain_ref))
    hidden_grad_ref[...] = hidden_grad
    hidden_low = hidden_grad.astype(BF16)
    hidden_low_ref[...] = hidden_low
    sums_ref[...] = before_ref[...]
    add_row = partial(add_sums, sums_ref)
    add_row(ROW_GAIN2, column_sums(upstream * unit))
    add_row(ROW_BIAS2, column_sums(upstream))
    add_row(ROW_OUT, column_sums(hidden_grad))
    width = q_ref.shape[1]
    score_scale = 1.0 / math.sqrt(HD)
    low = low_head()
    for pair in range(width // LANES):
        lanes = slice(pair * LANES, (pair + 1) * LANES)
        q_pair, k_pair, v_pair = q_ref[:, lanes], k_ref[:, lanes], v_ref[:, lanes]
        mixed_grad = mm(hidden_low, w_out_ref[lanes, :], NT).astype(BF16)
        keys, values = [], []
        for side in range(2):
            own = low if side == 0 else jnp.logical_not(low)
            soft_low = soft_ref[2 * pair + side]
            soft = soft_low.astype(F32)
            own_grad = mixed_grad * jnp.where(own, 1.0, 0.0).astype(BF16)
            prob_grad = mm(v_pair, own_grad, NT)
            inner = jnp.sum(soft * prob_grad, axis=0, keepdims=True)
            score_grad = (soft * (prob_grad - inner)).astype(BF16)
            values.append(mm(soft_low, mixed_grad))
            keys.append(mm(score_grad, q_pair))
            query = mm(k_pair, score_grad, TN)
            begin = side * HD
            query_t[pair * LANES + begin : pair * LANES + begin + HD, :] = query[begin : begin + HD]
        grads_ref[0, :, lanes] = (jnp.transpose(query_t[lanes, :]) * score_scale).astype(BF16)
        grads_ref[1, :, lanes] = (jnp.where(low, keys[0], keys[1]) * score_scale).astype(BF16)
        grads_ref[2, :, lanes] = jnp.where(low, values[0], values[1]).astype(BF16)
    for half, part in enumerate((0, 2)):
        row = 2 * ROW_QV + half
        sums_ref[row : row + 1, :] += column_sums(grads_ref[part].astype(F32))
    back = mm(grads_ref[0], w_qkv_ref[0], NT)
    back += mm(grads_ref[1], w_qkv_ref[1], NT)
    back += mm(grads_ref[2], w_qkv_ref[2], NT)
    back_ref[...] = lay.cut(back, s).astype(BF16)
    unit, _ = unit_of(lay.pick(tok_ref[...].astype(F32), s))
    add_row(ROW_GAIN1, column_sums(back * unit))
    add_row(ROW_BIAS1, column_sums(back))


def finish_kernel(lay, *refs):
    count = lay.slices
    tok_ref, gain_ref, bias_ref = refs[:3]
    own_ref, other_ref = refs[3:5]
    hidden_grad, hidden = (refs[5 + k * count : 5 + (k + 1) * count] for k in range(2))
    block_ref, grad_ref = refs[-2:]
    gain, bias = row_of(gain_ref), row_of(bias_ref)
    tokens = tok_ref[...].astype(F32)
    results, blocks = [], []
    for s in range(count):
        both = lambda which: lay.fill(
            own_ref[2 * s + which].astype(F32) + other_ref[2 * s + which].astype(F32), s
        )
        unit, scaled = unit_of(lay.pick(tokens, s))
        results.append(hidden_grad[s][...] + norm_back(both(0), unit, scaled, gain))
        blocks.append(hidden[s][...] + both(1) + bias)
    grad_ref[...] = lay.join(*results)
    block_ref[...] = lay.join(*blocks)


def turn(values, target):
    turned = jnp.transpose(values).astype(BF16)
    blocks, rows, _ = target.shape
    for block in range(blocks):
        target[block] = turned[block * rows : (block + 1) * rows]


def early_kernel(lay, cot_ref, w_down_ref, *refs):
    count = lay.slices
    normed, cot_turned, turned, active_grad = (refs[k * count : (k + 1) * count] for k in range(4))
    sums_ref = refs[-1]
    sums_ref[...] = jnp.zeros(sums_ref.shape, F32)
    for s in range(count):
        cot = jnp.where(lay.real(s), lay.pick(cot_ref[...].astype(F32), s), 0.0)
        add_sums(sums_ref, ROW_DOWN, column_sums(cot))
        turn(cot, cot_turned[s])
        turn(normed[s][...].astype(F32), turned[s])
        active_grad[s][...] = mm(cot.astype(BF16), w_down_ref[...], NT)


def wait_kernel(out_ref):
    out_ref[...] = jnp.zeros(out_ref.shape, F32)


def gram_kernel(lay, groups, sends, halves, *refs):
    count = lay.slices
    ins = 2 * count * len(groups)
    fresh = any(kind == "plain" for kind in groups)
    scratch = refs[-count:] if fresh else ()
    outs = refs[ins : len(refs) - len(scratch)]
    keep_refs, send_refs = outs[: len(outs) - sends], outs[len(outs) - sends :]
    held, blocks, rows, width = outs[0].shape
    parity = share_bit(0)
    plane = 0
    for group, kind in enumerate(groups):
        lefts = refs[2 * count * group : 2 * count * group + count]
        rights = refs[2 * count * group + count : 2 * count * (group + 1)]
        flips = lefts
        if kind == "plain":
            flips = scratch
            for left, flip in zip(lefts, flips):
                turn(left[...].astype(F32), flip)
        planes = rights[0].shape[0] if len(rights[0].shape) == 3 else 1
        step = min(width, 768)
        for sent in halves:
            which = 1 - parity if sent else parity
            turned = [
                jnp.concatenate([flip[2 * block + which] for block in range(blocks)], axis=0)
                for flip in flips
            ]
            for own in range(planes):
                for begin in range(0, width, step):
                    columns = slice(begin, begin + step)
                    total = None
                    for half, right in zip(turned, rights):
                        if planes > 1:
                            term = mm(half, right[own, :, columns])
                        else:
                            term = mm(half, right[:, columns])
                        total = term if total is None else total + term
                    total = total.astype(BF16)
                    out = (send_refs if sent else keep_refs)[(plane + own) // held]
                    for block in range(blocks):
                        out[(plane + own) % held, block, :, columns] = total[
                            block * rows : (block + 1) * rows
                        ]
        plane += planes


def pack(sums):
    high = sums.astype(BF16).astype(F32)
    low = (sums - high).astype(BF16).astype(F32)
    return jnp.concatenate([high, low], axis=0).astype(BF16), high + low


def unpack(packed):
    rows = packed.shape[0] // 2
    values = packed.astype(F32)
    return values[:rows] + values[rows:]


def store_small(total_ref, outs):
    rows = lambda place, count=2: [
        total_ref[2 * place + half : 2 * place + half + 1, :].reshape(-1) for half in range(count)
    ]
    width = total_ref.shape[1]
    for place, out in zip((ROW_GAIN1, ROW_BIAS1, ROW_OUT, ROW_GAIN2, ROW_BIAS2, ROW_DOWN, ROW_UP), outs[2:]):
        for half, values in enumerate(rows(place, out.shape[0] // width)):
            out[half * width : (half + 1) * width] = values
    for out, values in zip(outs[:2], rows(ROW_QV)):
        out[...] = values


def stage_kernel(items, merge, small, *refs):
    refs = list(refs)
    kept, came = [], []
    for _, _, pieces, _, _ in items:
        kept.append(refs.pop(0))
        came.append([refs.pop(0) for _ in range(pieces)])
    if small == "first":
        sums, other = refs.pop(0)[...], refs.pop(0)[...]
        sums += jnp.where(first_norm_rows(sums), other, 0.0)
    elif small:
        sums = refs.pop(0)[...] + unpack(came[-1][0][came[-1][0].shape[0] - 1])
    last = items[0][0] is None
    packed, held = pack(sums) if small and not last else (None, None)

    def total(item, plane, place, at):
        parts, blocks = came[item], items[item][4]
        if len(parts[0].shape) == 4:
            group, _, _, wide = parts[0].shape
            chunk = kept[item].shape[-1] // wide
            inside = slice(at.start % wide, at.start % wide + at.stop - at.start)
            part = parts[plane // group * chunk + at.start // wide][plane % group, place, :, inside]
        else:
            part = parts[0][plane * blocks + place, :, at]
        return kept[item][plane, place, :, at].astype(F32) + part.astype(F32)

    if last:
        count = items[0][3]
        if small:
            sums_ref = refs.pop()
            sums_ref[...] = sums
            store_small(sums_ref, [refs.pop() for _ in range(9)][::-1])
        for plane in range(count):
            at = 0
            while plane >= sum(out.shape[0] for out in refs[: at + 1]):
                at += 1
            before = sum(out.shape[0] for out in refs[:at])
            refs[at][plane - before] = total(0, plane, 0, slice(0, kept[0].shape[-1]))
        return
    base_plane = 0
    for item, (bit, low, pieces, planes, blocks) in enumerate(items):
        mine = share_bit(bit)
        out, keep = (refs[0], refs[1]) if merge else refs[2 * item : 2 * item + 2]
        columns = kept[item].shape[-1]
        wide = came[item][0].shape[-1]
        for plane in range(planes):
            for begin in range(0, columns, wide):
                at = slice(begin, begin + wide)
                for block in range(blocks // 2):
                    base = block // low * 2 * low + block % low
                    place = (base_plane + plane) * (blocks // 2) + block
                    out[place, :, at] = total(item, plane, base + (1 - mine) * low, at).astype(BF16)
                    keep[base_plane + plane, block, :, at] = total(item, plane, base + mine * low, at)
        if merge:
            base_plane += planes
    if small:
        target = refs[0 if merge else 2 * len(items) - 2]
        target[target.shape[0] - 1] = packed
        refs[-1][...] = held


class Order:
    def __init__(self):
        self.token = ()
        self.weight = 0

    def __call__(self, kernel, outs, args, scratch=(), limit=16, fresh=False, also=(), name=None):
        waits = (*self.token, *also)
        first, tokens = len(args), len(waits)

        def body(*refs):
            kernel(*refs[:first], *refs[first + tokens :])

        place = pltpu.HBM if fresh else pltpu.VMEM
        spaces = [pltpu.HBM if space else pltpu.VMEM for _, _, *space in outs]
        results = pl.pallas_call(
            body,
            out_shape=[space(item[0], item[1]) for space, item in zip(spaces, outs)],
            in_specs=[pl.BlockSpec(memory_space=pl.ANY if fresh else pltpu.VMEM)] * first
            + [pl.BlockSpec(memory_space=pl.ANY)] * tokens,
            out_specs=[pl.BlockSpec(memory_space=pltpu.VMEM)] * len(outs),
            scratch_shapes=list(scratch),
            compiler_params=pltpu.CompilerParams(vmem_limit_bytes=limit * MIB),
            cost_estimate=pl.CostEstimate(
                flops=1 + self.weight * 10**9, bytes_accessed=1, transcendentals=0
            ),
            name=name,
        )(*(pltpu.with_memory_space_constraint(array, place) for array in args), *waits)
        self.token = (pltpu.with_memory_space_constraint(results[-1], spaces[-1]),)
        return results


def gram(call, lay, groups, shares, keeps, name, halves=(True, False)):
    first = groups[0][1][0]
    rows = first.shape[1]
    columns = groups[0][2][0].shape[-1]
    planes = sum(r[0].shape[0] if len(r[0].shape) == 3 else 1 for _, _, r in groups)
    kinds = tuple(kind for kind, _, _ in groups)
    sends = keeps if True in halves else 0
    outs = [((planes // keeps, shares // 2, rows, columns), BF16)] * (keeps * len(halves))
    results = call(
        partial(gram_kernel, lay, kinds, sends, halves),
        outs,
        [array for _, lefts, rights in groups for array in (*lefts, *rights)],
        scratch=[pltpu.VMEM(first.shape, BF16)] * (lay.slices if "plain" in kinds else 0),
        name=name,
    )
    return results[: len(outs) - sends], results[len(outs) - sends :]


def plain_scatter(groups, shares):
    sums = []
    for kind, lefts, rights in groups:
        total = 0.0
        for left, right in zip(lefts, rights):
            if kind == "turned":
                left = left.reshape(-1, left.shape[2]).T
            right = right if len(right.shape) == 3 else right[None]
            total += jnp.einsum("rd,prc->pdc", left, right, preferred_element_type=F32)
        sums.append(total)
    kept = jnp.concatenate(sums, axis=0)
    planes, model, columns = kept.shape
    rows = model // shares
    for bit in range(shares.bit_length() - 1):
        view = kept.reshape(planes, -1, 2, rows, columns)
        mine = share_bit(bit)
        pick = lambda which: lax.dynamic_index_in_dim(view, which, 2, keepdims=False)
        kept = pick(mine) + flip(pick(1 - mine).astype(BF16), shares, bit).astype(F32)
    return kept[:, 0]


def plain_small(vector, shares):
    for bit in range(shares.bit_length() - 1):
        vector = vector + flip(vector, shares, bit)
    return vector + jnp.where(first_norm_rows(vector), swap(vector), 0.0)


def flip_pairs(shares, bit):
    return [(index, index ^ (1 << bit)) for index in range(shares)]


def flip(array, shares, bit):
    return lax.ppermute(array, "dp", flip_pairs(shares, bit))


class Sum:
    def __init__(self, kept, sent, shares, order):
        self.order = list(order)
        self.left = sorted(order, reverse=True)
        self.kept, self.shares = kept, shares
        self.send(sent, 0)

    def send(self, sent, bit):
        self.came = [flip(part, self.shares, bit) for part in sent]

    def next(self):
        planes, blocks = self.kept.shape[:2]
        if not self.order:
            return None, 0, len(self.came), planes, blocks
        bit = self.order.pop(0)
        low = 1 << (len(self.left) - 1 - self.left.index(bit))
        self.left.remove(bit)
        return bit, low, len(self.came), planes, blocks


def stage(call, sums, name, merge=False, small=None, small_args=(), last=()):
    items = tuple(item.next() for item in sums)
    args = [array for item in sums for array in (item.kept, *item.came)]
    rows, columns = sums[0].kept.shape[2:]
    extra = 1 if small else 0
    if last:
        scratch = [pltpu.VMEM(small_args[0].shape, F32)] if small else []
        return call(
            partial(stage_kernel, items, merge, small), list(last), [*args, *small_args], scratch, name=name
        )
    sizes = [(planes, blocks // 2) for _, _, _, planes, blocks in items]
    if merge:
        sizes = [(sum(planes for planes, _ in sizes), sizes[0][1])]
    outs = []
    for place, (planes, blocks) in enumerate(sizes):
        count = planes * blocks + (extra if place == len(sizes) - 1 else 0)
        outs += [((count, rows, columns), BF16), ((planes, blocks, rows, columns), F32)]
    if small:
        outs.append((small_args[0].shape, F32))
    results = call(partial(stage_kernel, items, merge, small), outs, [*args, *small_args], name=name)
    for place, item in enumerate(sums[: len(sizes)]):
        item.kept = results[2 * place + 1]
        item.send([results[2 * place]], items[place][0])
    return results[-1]


def first_norm_rows(vector):
    place = lax.broadcasted_iota(jnp.int32, (vector.shape[0], 1), 0) // 2
    return (place == ROW_GAIN1) | (place == ROW_BIAS1)


def add_small_kernel(own_ref, other_ref, out_ref):
    out_ref[...] = own_ref[...] + other_ref[...]


def small_outputs(vector, units):
    two = lambda place, count=2: vector[2 * place : 2 * place + count].reshape(-1)
    return (
        vector[2 * ROW_QV], vector[2 * ROW_QV + 1], two(ROW_GAIN1), two(ROW_BIAS1), two(ROW_OUT),
        two(ROW_GAIN2), two(ROW_BIAS2), two(ROW_DOWN), two(ROW_UP, units // vector.shape[1]),
    )


def swap(rows):
    return lax.ppermute(rows, "tensor", [(0, 1), (1, 0)])


def local(
    shares, tokens, body_mask, ln1_gain, ln1_bias, w_qkv, b_q, b_v, w_out, b_out, ln2_gain, ln2_bias,
    w_up, b_up, w_down, b_down, cotangent,
):
    slices, seq = body_mask.shape
    rows, model = tokens.shape
    lay = Layout(rows, slices, seq)
    padded, sent = lay.padded, lay.sent
    width = w_qkv.shape[2]
    heads = width // HD
    units = w_up.shape[1]
    steps = shares.bit_length() - 1
    small_rows = 2 * ROW_UP + units // (model // 2)
    small_height = -(-small_rows // SUBLANES) * SUBLANES
    w_qkv = jnp.transpose(w_qkv, (1, 0, 2))
    wide, narrow, tall = ((padded, model), BF16), ((padded, width), BF16), ((padded, units), BF16)
    tuned = steps == 4 and model // shares == 2 * small_height and width == model // 2
    blocks = shares if tuned else 1
    flipped = ((blocks, model // blocks, padded), BF16)
    wide_f, crossing = ((padded, model), F32), ((sent, model), BF16)
    small = ((small_height, model // 2), F32)
    bias_row = pltpu.VMEM((SUBLANES, -(-padded // LANES) * LANES), F32)
    attend_outs = [
        ((sent, width), BF16), wide, narrow, narrow, narrow, ((heads, padded, padded), BF16), narrow
    ]

    call = Order()
    state = {name: [None] * slices for name in (*ATTENDED, *UPPED, *RETURNED, *OTHERS)}
    held = {}
    sums = {}
    result = {}

    def keep(s, names, values):
        for name, value in zip(names, values):
            state[name][s] = value

    def attend(s):
        if s == 0:
            results = call(
                partial(first_attend_kernel, lay),
                attend_outs + [(w_qkv.shape, BF16), (w_out.shape, BF16), (tokens.shape, BF16)],
                (tokens, body_mask, ln1_gain, ln1_bias, w_qkv, b_q, b_v, w_out),
                scratch=[
                    pltpu.VMEM(body_mask.shape, jnp.int32),
                    *[pltpu.VMEM((size,), F32) for size in (model, model, width, width)],
                    bias_row,
                    pltpu.SemaphoreType.DMA((8,)),
                ],
                fresh=True,
                name="attend",
            )
            held["w_qkv"], held["w_out"], held["tokens"] = results[7:]
        else:
            results = call(
                partial(attend_kernel, lay, s),
                attend_outs,
                (held["tokens"], body_mask, ln1_gain, ln1_bias, held["w_qkv"], b_q, b_v),
                scratch=[bias_row],
                name="attend",
            )
        keep(s, ATTENDED, results)
        state["other"][s] = swap(state["crossing"][s])

    def weights():
        half = call(
            half_kernel,
            [((width // 2, model), BF16)],
            (w_out,),
            scratch=[pltpu.SemaphoreType.DMA],
            fresh=True,
            name="half",
        )[0]
        held["near"] = swap(half)
        held["far"] = flip(held["near"], shares, 0)

    def early():
        results = call(
            partial(early_kernel, lay),
            [flipped] * (2 * slices) + [((padded, units), F32)] * slices + [small],
            (cotangent, w_down, *state["normed"]),
            name="early",
        )
        for name, place in (("cot_turned", 0), ("turned", 1), ("active_grad", 2)):
            state[name] = results[place * slices : (place + 1) * slices]
        held["vector"] = results[-1]

    def mlp(s):
        late = s == slices - 1
        results = call(
            partial(mlp_kernel, lay, s),
            [wide_f, flipped, tall, tall, small] + ([] if late else [crossing]),
            (
                held["tokens"], state["mixed"][s], state["other"][s], held["w_out"], held["near"],
                held["far"], b_out, ln2_gain, ln2_bias, w_up, b_up, state["active_grad"][s],
                held["vector"],
            ),
            scratch=[pltpu.VMEM((2, padded, model), F32)],
            name="mlp",
        )
        keep(s, UPPED, results)
        held["vector"] = results[4]
        if not late:
            send_back(s, results[5])

    def send_back(s, back):
        state["back"][s] = back
        state["other"][s] = swap(back)

    def late_back(s):
        args = (state["upper_low"][s], w_up)
        send_back(s, call(partial(back_kernel, lay, s), [crossing], args, name="back")[0])

    def last():
        held["last"] = call(
            partial(last_kernel, lay),
            [((2 * slices, sent, model), BF16)],
            (*state["active"], *state["first_back"], w_down),
            name="last",
        )[0]
        held["last_other"] = swap(held["last"])

    def attend_back(s):
        results = call(
            partial(attend_back_kernel, lay, s),
            [wide_f, wide, ((3, padded, width), BF16), crossing, small],
            (
                *(state[name][s] for name in ("hidden", "back", "other")), cotangent, ln2_gain,
                held["w_out"], *(state[name][s] for name in ("q", "k", "v", "soft")), held["w_qkv"],
                held["tokens"], held["vector"],
            ),
            scratch=[pltpu.VMEM((width, padded), F32)],
            name="attend_back",
        )
        keep(s, RETURNED, results)
        held["vector"] = results[4]
        if s == slices - 1:
            held["vector_other"] = flip(held["vector"], shares, 0)

    def finish():
        result["rows"] = call(
            partial(finish_kernel, lay),
            [((rows, model), F32, True)] * 2,
            (
                held["tokens"], ln1_gain, b_down, held["last"], held["last_other"],
                *state["hidden_grad"], *state["hidden"],
            ),
            name="finish",
        )

    grams = {
        "D": lambda: [("turned", state["cot_turned"], state["active"])],
        "U": lambda: [("turned", state["normed2"], state["upper_low"])],
        "Q": lambda: [
            ("turned", state["turned"], state["qkv_grad"]),
            ("plain", state["hidden_low"], state["mixed"]),
        ],
    }
    near, far = (1, 2, 3), (2, 1, 3)
    share = lambda planes, columns: ((planes, model // shares, columns), F32, True)

    def step_mlp(step):
        sums = [held["D"], held["U"]] if step < 3 else [held["U"], held["D"]][: 5 - step]
        last = [share(1, units), share(1, units)] if step == 4 else ()
        done = stage(call, sums, "sum_mlp_" + "abcd"[step - 1], merge=step == 3, last=last)
        if last:
            result["U"], result["D"] = done

    def step_qkv(step):
        sums = held["Q"] if step < 4 else held["Q"][:1]
        small_kind = {1: "first", 4: "last"}.get(step, "next")
        last = ()
        if step == 4:
            last = [share(3, width), share(1, width)] + [
                ((size,), F32, True)
                for size in (width, width, model, model, model, model, model, model, units)
            ]
        args = (held["vector"], held["vector_other"]) if step == 1 else (held["vector"],)
        done = stage(call, sums, "sum_qkv_" + "abcd"[step - 1], step == 3, small_kind, args, last)
        if last:
            result["Q"], result["O"], *result["small"] = done
        else:
            held["vector"] = done

    for item in ORDER:
        kind, place = item[0], item[1:]
        call.weight = WEIGHT.get(item, 0)
        if kind == "W":
            weights()
        elif kind == "A":
            attend(int(place))
        elif kind == "B":
            mlp(int(place))
        elif kind == "C":
            attend_back(int(place))
        elif kind == "F":
            finish()
        elif kind == "T":
            early()
        elif kind == "R":
            late_back(int(place))
        elif kind == "L":
            last()
        elif kind == "X":
            call(wait_kernel, [((SUBLANES, LANES), F32)], (), also=state["other"][:1], name="wait")
        elif not tuned:
            continue
        elif kind == "Y":
            call(wait_kernel, [((SUBLANES, LANES), F32)], (), also=held["U"].came, name="wait")
        elif kind == "s":
            held["vector"] = call(
                add_small_kernel, [small], [held["vector"], held["vector_other"]], name="add_small"
            )[0]
            held["vector_other"] = swap(held["vector"])
        elif item == "GQ":
            kept, pieces = gram(call, lay, grams["Q"](), shares, 2, "gram_q")
            held["Q"] = [Sum(kept[0], pieces[:1], shares, far), Sum(kept[1], pieces[1:], shares, near)]
        elif kind in "GK":
            halves, name = ((kind == "G",), ("gram_" if kind == "G" else "keep_") + place.lower())
            kept, pieces = gram(call, lay, grams[place](), shares, 1, name, halves)
            if pieces:
                held[place] = Sum(None, pieces, shares, near if place == "U" else far)
            else:
                held[place].kept = kept[0]
        elif kind == "M":
            step_mlp(int(place))
        else:
            step_qkv(int(place))
    if not tuned:
        for name in "DU":
            result[name] = plain_scatter(grams[name](), shares)
        total = plain_scatter(grams["Q"](), shares)
        result["Q"], result["O"] = total[:3], total[3:]
        result["small"] = small_outputs(plain_small(held["vector"], shares), units)

    (
        sum_b_q, sum_b_v, sum_ln1_gain, sum_ln1_bias, sum_b_out, sum_ln2_gain, sum_ln2_bias, sum_b_down,
        sum_b_up,
    ) = result["small"]
    block_out, grad_tokens = result["rows"]
    return (
        block_out,
        grad_tokens,
        sum_ln1_gain,
        sum_ln1_bias,
        jnp.transpose(result["Q"], (1, 0, 2)),
        sum_b_q,
        sum_b_v,
        result["O"][0].T,
        sum_b_out,
        sum_ln2_gain,
        sum_ln2_bias,
        result["U"][0],
        sum_b_up,
        result["D"][0].T,
        sum_b_down,
    )


def solution(mesh):
    return jax.shard_map(
        partial(local, mesh.shape["dp"]),
        mesh=mesh,
        in_specs=(
            P("dp", None),
            P("dp", None),
            P(),
            P(),
            P(None, None, "tensor"),
            P("tensor"),
            P("tensor"),
            P("tensor", None),
            P(),
            P(),
            P(),
            P(None, "tensor"),
            P("tensor"),
            P("tensor", None),
            P(),
            P("dp", None),
        ),
        out_specs=(
            P("dp", None),
            P("dp", None),
            P(),
            P(),
            P("dp", None, "tensor"),
            P("tensor"),
            P("tensor"),
            P("tensor", "dp"),
            P(),
            P(),
            P(),
            P("dp", "tensor"),
            P("tensor"),
            P("tensor", "dp"),
            P(),
        ),
        check_vma=False,
    )
```

```python
import math
from functools import partial

import jax
import jax.numpy as jnp
from jax import lax
from jax.experimental import pallas as pl
from jax.experimental.pallas import tpu as pltpu
from jax.sharding import PartitionSpec as P

HD = 64
LANES = 128
SUBLANES = 8
ROW_TILE = 16
F32 = jnp.float32
BF16 = jnp.bfloat16
MIB = 1024 * 1024

ORDER = (
    "W", "A0", "A1", "T", "B0", "B1", "GU", "GD", "R1", "KU", "KD", "X",
    "Y", "M1", "C0", "C1", "GQ", "s1", "M2", "Q1", "L", "M3", "Q2", "Q3",
    "M4", "F", "Q4",
)
WEIGHT = {"T": 6, "B1": 8, "X": 10, "Y": 1, "C0": 4, "C1": 8, "GQ": 4, "M2": 12, "Q1": 6, "M3": 12, "F": 2}

ATTENDED = ("crossing", "normed", "q", "k", "v", "soft", "mixed")
UPPED = ("hidden", "normed2", "active", "upper_low")
RETURNED = ("hidden_grad", "hidden_low", "qkv_grad", "first_back")
OTHERS = ("back", "other", "cot_turned", "turned", "active_grad")

NN = (((1,), (0,)), ((), ()))
NT = (((1,), (1,)), ((), ()))
TN = (((0,), (0,)), ((), ()))

ROW_DOWN, ROW_GAIN2, ROW_BIAS2, ROW_OUT, ROW_QV, ROW_GAIN1, ROW_BIAS1, ROW_UP = range(8)


def mm(left, right, dims=NN):
    return lax.dot_general(left, right, dims, preferred_element_type=F32)


def unit_of(source):
    center = source - jnp.mean(source, axis=-1, keepdims=True)
    scaled = lax.rsqrt(jnp.mean(center * center, axis=-1, keepdims=True) + 1e-06)
    return center * scaled, scaled


def norm_back(upstream, unit_rows, scaled, gain_vec):
    inner = upstream * gain_vec
    return scaled * (
        inner
        - jnp.mean(inner, axis=-1, keepdims=True)
        - unit_rows * jnp.mean(inner * unit_rows, axis=-1, keepdims=True)
    )


def column_sums(rows):
    return jnp.sum(rows, axis=0, keepdims=True)


def add_sums(sums_ref, place, sums):
    width = sums_ref.shape[1]
    for half in range(sums.shape[1] // width):
        row = 2 * place + half
        sums_ref[row : row + 1, :] += sums[:, half * width : (half + 1) * width]


def row_of(ref):
    return ref[...].reshape(1, -1)


def share_bit(bit):
    return (lax.axis_index("dp").astype(jnp.int32) >> bit) & 1


def low_head():
    return lax.broadcasted_iota(jnp.int32, (1, LANES), 1) < HD


class Layout:
    def __init__(self, rows, slices, seq):
        self.rows, self.slices, self.seq = rows, slices, seq
        self.padded = -(-seq // ROW_TILE) * ROW_TILE
        self.sent = -(-seq // SUBLANES) * SUBLANES

    def pick(self, values, s):
        start = s * (self.rows - self.padded)
        return values[start : start + self.padded]

    def real(self, s):
        place = lax.broadcasted_iota(jnp.int32, (self.padded, 1), 0)
        return place < self.seq if s == 0 else place >= self.padded - self.seq

    def cut(self, values, s):
        return values[: self.sent] if s == 0 else values[self.padded - self.sent :]

    def fill(self, values, s):
        extra = jnp.zeros((self.padded - self.sent, values.shape[1]), values.dtype)
        return jnp.concatenate([values, extra] if s == 0 else [extra, values], axis=0)

    def join(self, first, second):
        start = self.rows - self.padded
        place = lax.broadcasted_iota(jnp.int32, (self.padded - start, 1), 0) + start
        middle = jnp.where(place < self.seq, first[start:], second[: self.padded - start])
        return jnp.concatenate([first[:start], middle, second[self.padded - start :]], axis=0)


def half_kernel(w_ref, out_ref, sem):
    rows = out_ref.shape[0]
    begin = pl.multiple_of(share_bit(0) * rows, ROW_TILE)
    copy = pltpu.make_async_copy(w_ref.at[pl.ds(begin, rows)], out_ref, sem)
    copy.start()
    copy.wait()


def project(mixed, upper_rows, lower_rows):
    cut = upper_rows.shape[0]
    return mm(mixed[:, :cut], upper_rows) + mm(mixed[:, cut:], lower_rows)


def first_attend_kernel(lay, *refs):
    sources, outs = refs[:8], refs[8:15]
    w_qkv_ref, w_out_ref, tok_ref = refs[15:18]
    mask_ref, gain_ref, bias_ref, b_q_ref, b_v_ref, bias_row, sems = refs[18:]
    targets = (tok_ref, mask_ref, gain_ref, bias_ref, w_qkv_ref, b_q_ref, b_v_ref, w_out_ref)
    copies = [
        pltpu.make_async_copy(source, target, sems.at[place])
        for place, (source, target) in enumerate(zip(sources, targets))
    ]
    for place in (0, 2, 3, 4, 5, 6, 1, 7):
        copies[place].start()

    def ready(*places):
        for place in places:
            copies[place].wait()

    attend_kernel(lay, 0, *targets[:7], *outs, bias_row, ready)


def attend_kernel(
    lay, s, tok_ref, mask_ref, gain_ref, bias_ref, w_qkv_ref, b_q_ref, b_v_ref,
    crossing_ref, normed_ref, q_ref, k_ref, v_ref, soft_ref, mixed_ref, bias_row,
    ready=lambda *places: None,
):
    ready(0, 2, 3)
    unit, _ = unit_of(lay.pick(tok_ref[...].astype(F32), s))
    normed = (unit * row_of(gain_ref) + row_of(bias_ref)).astype(BF16)
    normed_ref[...] = normed
    ready(4, 5, 6, 1)
    q_ref[...] = (mm(normed, w_qkv_ref[0]) + row_of(b_q_ref)).astype(BF16)
    k_ref[...] = mm(normed, w_qkv_ref[1]).astype(BF16)
    v_ref[...] = (mm(normed, w_qkv_ref[2]) + row_of(b_v_ref)).astype(BF16)
    bias_row[...] = jnp.full(bias_row.shape, -1e30, F32)
    bias_row[0:1, : lay.seq] = jnp.where(mask_ref[s : s + 1, :] > 0, 0.0, -1e30)
    lanes_bias = bias_row[...]
    if s:
        lanes_bias = pltpu.roll(lanes_bias, lay.padded - lay.seq, 1)
    turned = jnp.transpose(jnp.broadcast_to(lanes_bias[0:1], (LANES, lanes_bias.shape[1])))
    turned = turned[: lay.padded]
    key_bias = jnp.concatenate([turned] * -(-lay.padded // LANES), axis=1)[:, : lay.padded]
    score_scale = 1.0 / math.sqrt(HD)
    low = low_head()
    for pair in range(q_ref.shape[1] // LANES):
        lanes = slice(pair * LANES, (pair + 1) * LANES)
        q_pair, k_pair, v_pair = q_ref[:, lanes], k_ref[:, lanes], v_ref[:, lanes]
        halves = []
        for side in range(2):
            own = low if side == 0 else jnp.logical_not(low)
            q_own = q_pair * jnp.where(own, score_scale, 0.0).astype(BF16)
            scores = mm(k_pair, q_own, NT) + key_bias
            expo = jnp.exp(scores - jnp.max(scores, axis=0, keepdims=True))
            soft = (expo * (1.0 / jnp.sum(expo, axis=0, keepdims=True))).astype(BF16)
            soft_ref[2 * pair + side] = soft
            begin = side * HD
            halves.append(mm(v_pair, soft, TN)[begin : begin + HD])
        mixed = jnp.transpose(jnp.concatenate(halves, axis=0))
        mixed_ref[:, lanes] = mixed.astype(BF16)
        crossing_ref[:, lanes] = lay.cut(mixed, s).astype(BF16)
    ready(7)


def mlp_kernel(
    lay, s, tok_ref, own_ref, other_ref, w_out_ref, near_ref, far_ref, b_out_ref, gain_ref, bias_ref,
    w_up_ref, b_up_ref, active_grad_ref, before_ref,
    hidden_ref, normed_ref, active_ref, upper_low_ref, sums_ref, *refs,
):
    *refs, products = refs
    cut = near_ref.shape[0]
    upper_half = share_bit(0) == 0
    near, far = near_ref[...], far_ref[...]
    products[0] = project(own_ref[...], w_out_ref[:cut], w_out_ref[cut:])
    products[1] = project(
        lay.fill(other_ref[...].astype(F32), s).astype(BF16),
        jnp.where(upper_half, near, far),
        jnp.where(upper_half, far, near),
    )
    attended = products[0] + products[1]
    hidden = lay.pick(tok_ref[...].astype(F32), s) + attended + row_of(b_out_ref)
    hidden_ref[...] = hidden
    unit, _ = unit_of(hidden)
    normed = (unit * row_of(gain_ref) + row_of(bias_ref)).astype(BF16)
    turn(normed.astype(F32), normed_ref)
    sums_ref[...] = before_ref[...]
    b_up = row_of(b_up_ref)
    width, model = w_up_ref.shape[1], tok_ref.shape[1]
    step = 768
    for begin in range(0, width, step):
        units = slice(begin, begin + step)
        upper = mm(normed, w_up_ref[:, units]) + b_up[:, units]
        cdf = 0.5 * (1.0 + lax.erf(upper * math.sqrt(0.5)))
        density = jnp.exp(upper * upper * -0.5) * (1.0 / math.sqrt(2.0 * math.pi))
        active_ref[:, units] = (upper * cdf).astype(BF16)
        upper_grad = active_grad_ref[:, units] * (cdf + upper * density)
        add_sums(sums_ref, ROW_UP + begin // model, column_sums(upper_grad))
        upper_low_ref[:, units] = upper_grad.astype(BF16)
    if refs:
        back_kernel(lay, s, upper_low_ref, w_up_ref, *refs)


def back_kernel(lay, s, upper_low_ref, w_up_ref, back_ref):
    back_ref[...] = lay.cut(mm(upper_low_ref[...], w_up_ref[...], NT), s).astype(BF16)


def last_kernel(lay, *refs):
    count = lay.slices
    active, first_back = refs[:count], refs[count : 2 * count]
    w_down_ref, last_ref = refs[2 * count :]
    for s in range(count):
        last_ref[2 * s] = first_back[s][...]
        last_ref[2 * s + 1] = lay.cut(mm(active[s][...], w_down_ref[...]), s).astype(BF16)


def attend_back_kernel(
    lay, s, hidden_ref, own_ref, other_ref, cot_ref, gain_ref, w_out_ref, q_ref, k_ref, v_ref,
    soft_ref, w_qkv_ref, tok_ref, before_ref,
    hidden_grad_ref, hidden_low_ref, grads_ref, back_ref, sums_ref, query_t,
):
    unit, scaled = unit_of(hidden_ref[...])
    upstream = lay.fill(own_ref[...].astype(F32) + other_ref[...].astype(F32), s)
    cot = jnp.where(lay.real(s), lay.pick(cot_ref[...].astype(F32), s), 0.0)
    hidden_grad = cot + norm_back(upstream, unit, scaled, row_of(gain_ref))
    hidden_grad_ref[...] = hidden_grad
    hidden_low = hidden_grad.astype(BF16)
    hidden_low_ref[...] = hidden_low
    sums_ref[...] = before_ref[...]
    add_row = partial(add_sums, sums_ref)
    add_row(ROW_GAIN2, column_sums(upstream * unit))
    add_row(ROW_BIAS2, column_sums(upstream))
    add_row(ROW_OUT, column_sums(hidden_grad))
    width = q_ref.shape[1]
    score_scale = 1.0 / math.sqrt(HD)
    low = low_head()
    for pair in range(width // LANES):
        lanes = slice(pair * LANES, (pair + 1) * LANES)
        q_pair, k_pair, v_pair = q_ref[:, lanes], k_ref[:, lanes], v_ref[:, lanes]
        mixed_grad = mm(hidden_low, w_out_ref[lanes, :], NT).astype(BF16)
        keys, values = [], []
        for side in range(2):
            own = low if side == 0 else jnp.logical_not(low)
            soft_low = soft_ref[2 * pair + side]
            soft = soft_low.astype(F32)
            own_grad = mixed_grad * jnp.where(own, 1.0, 0.0).astype(BF16)
            prob_grad = mm(v_pair, own_grad, NT)
            inner = jnp.sum(soft * prob_grad, axis=0, keepdims=True)
            score_grad = (soft * (prob_grad - inner)).astype(BF16)
            values.append(mm(soft_low, mixed_grad))
            keys.append(mm(score_grad, q_pair))
            query = mm(k_pair, score_grad, TN)
            begin = side * HD
            query_t[pair * LANES + begin : pair * LANES + begin + HD, :] = query[begin : begin + HD]
        grads_ref[0, :, lanes] = (jnp.transpose(query_t[lanes, :]) * score_scale).astype(BF16)
        grads_ref[1, :, lanes] = (jnp.where(low, keys[0], keys[1]) * score_scale).astype(BF16)
        grads_ref[2, :, lanes] = jnp.where(low, values[0], values[1]).astype(BF16)
    for half, part in enumerate((0, 2)):
        row = 2 * ROW_QV + half
        sums_ref[row : row + 1, :] += column_sums(grads_ref[part].astype(F32))
    back = mm(grads_ref[0], w_qkv_ref[0], NT)
    back += mm(grads_ref[1], w_qkv_ref[1], NT)
    back += mm(grads_ref[2], w_qkv_ref[2], NT)
    back_ref[...] = lay.cut(back, s).astype(BF16)
    unit, _ = unit_of(lay.pick(tok_ref[...].astype(F32), s))
    add_row(ROW_GAIN1, column_sums(back * unit))
    add_row(ROW_BIAS1, column_sums(back))


def finish_kernel(lay, *refs):
    count = lay.slices
    tok_ref, gain_ref, bias_ref = refs[:3]
    own_ref, other_ref = refs[3:5]
    hidden_grad, hidden = (refs[5 + k * count : 5 + (k + 1) * count] for k in range(2))
    block_ref, grad_ref = refs[-2:]
    gain, bias = row_of(gain_ref), row_of(bias_ref)
    tokens = tok_ref[...].astype(F32)
    results, blocks = [], []
    for s in range(count):
        both = lambda which: lay.fill(
            own_ref[2 * s + which].astype(F32) + other_ref[2 * s + which].astype(F32), s
        )
        unit, scaled = unit_of(lay.pick(tokens, s))
        results.append(hidden_grad[s][...] + norm_back(both(0), unit, scaled, gain))
        blocks.append(hidden[s][...] + both(1) + bias)
    grad_ref[...] = lay.join(*results)
    block_ref[...] = lay.join(*blocks)


def turn(values, target):
    turned = jnp.transpose(values).astype(BF16)
    blocks, rows, _ = target.shape
    for block in range(blocks):
        target[block] = turned[block * rows : (block + 1) * rows]


def early_kernel(lay, cot_ref, w_down_ref, *refs):
    count = lay.slices
    normed, cot_turned, turned, active_grad = (refs[k * count : (k + 1) * count] for k in range(4))
    sums_ref = refs[-1]
    sums_ref[...] = jnp.zeros(sums_ref.shape, F32)
    for s in range(count):
        cot = jnp.where(lay.real(s), lay.pick(cot_ref[...].astype(F32), s), 0.0)
        add_sums(sums_ref, ROW_DOWN, column_sums(cot))
        turn(cot, cot_turned[s])
        turn(normed[s][...].astype(F32), turned[s])
        active_grad[s][...] = mm(cot.astype(BF16), w_down_ref[...], NT)


def wait_kernel(out_ref):
    out_ref[...] = jnp.zeros(out_ref.shape, F32)


def gram_kernel(lay, groups, sends, halves, *refs):
    count = lay.slices
    ins = 2 * count * len(groups)
    fresh = any(kind == "plain" for kind in groups)
    scratch = refs[-count:] if fresh else ()
    outs = refs[ins : len(refs) - len(scratch)]
    keep_refs, send_refs = outs[: len(outs) - sends], outs[len(outs) - sends :]
    held, blocks, rows, width = outs[0].shape
    parity = share_bit(0)
    plane = 0
    for group, kind in enumerate(groups):
        lefts = refs[2 * count * group : 2 * count * group + count]
        rights = refs[2 * count * group + count : 2 * count * (group + 1)]
        flips = lefts
        if kind == "plain":
            flips = scratch
            for left, flip in zip(lefts, flips):
                turn(left[...].astype(F32), flip)
        planes = rights[0].shape[0] if len(rights[0].shape) == 3 else 1
        step = min(width, 768)
        for sent in halves:
            which = 1 - parity if sent else parity
            turned = [
                jnp.concatenate([flip[2 * block + which] for block in range(blocks)], axis=0)
                for flip in flips
            ]
            for own in range(planes):
                for begin in range(0, width, step):
                    columns = slice(begin, begin + step)
                    total = None
                    for half, right in zip(turned, rights):
                        if planes > 1:
                            term = mm(half, right[own, :, columns])
                        else:
                            term = mm(half, right[:, columns])
                        total = term if total is None else total + term
                    total = total.astype(BF16)
                    out = (send_refs if sent else keep_refs)[(plane + own) // held]
                    for block in range(blocks):
                        out[(plane + own) % held, block, :, columns] = total[
                            block * rows : (block + 1) * rows
                        ]
        plane += planes


def pack(sums):
    high = sums.astype(BF16).astype(F32)
    low = (sums - high).astype(BF16).astype(F32)
    return jnp.concatenate([high, low], axis=0).astype(BF16), high + low


def unpack(packed):
    rows = packed.shape[0] // 2
    values = packed.astype(F32)
    return values[:rows] + values[rows:]


def store_small(total_ref, outs):
    rows = lambda place, count=2: [
        total_ref[2 * place + half : 2 * place + half + 1, :].reshape(-1) for half in range(count)
    ]
    width = total_ref.shape[1]
    for place, out in zip((ROW_GAIN1, ROW_BIAS1, ROW_OUT, ROW_GAIN2, ROW_BIAS2, ROW_DOWN, ROW_UP), outs[2:]):
        for half, values in enumerate(rows(place, out.shape[0] // width)):
            out[half * width : (half + 1) * width] = values
    for out, values in zip(outs[:2], rows(ROW_QV)):
        out[...] = values


def stage_kernel(items, merge, small, *refs):
    refs = list(refs)
    kept, came = [], []
    for _, _, pieces, _, _ in items:
        kept.append(refs.pop(0))
        came.append([refs.pop(0) for _ in range(pieces)])
    if small == "first":
        sums, other = refs.pop(0)[...], refs.pop(0)[...]
        sums += jnp.where(first_norm_rows(sums), other, 0.0)
    elif small:
        sums = refs.pop(0)[...] + unpack(came[-1][0][came[-1][0].shape[0] - 1])
    last = items[0][0] is None
    packed, held = pack(sums) if small and not last else (None, None)

    def total(item, plane, place, at):
        parts, blocks = came[item], items[item][4]
        if len(parts[0].shape) == 4:
            group, _, _, wide = parts[0].shape
            chunk = kept[item].shape[-1] // wide
            inside = slice(at.start % wide, at.start % wide + at.stop - at.start)
            part = parts[plane // group * chunk + at.start // wide][plane % group, place, :, inside]
        else:
            part = parts[0][plane * blocks + place, :, at]
        return kept[item][plane, place, :, at].astype(F32) + part.astype(F32)

    if last:
        count = items[0][3]
        if small:
            sums_ref = refs.pop()
            sums_ref[...] = sums
            store_small(sums_ref, [refs.pop() for _ in range(9)][::-1])
        for plane in range(count):
            at = 0
            while plane >= sum(out.shape[0] for out in refs[: at + 1]):
                at += 1
            before = sum(out.shape[0] for out in refs[:at])
            refs[at][plane - before] = total(0, plane, 0, slice(0, kept[0].shape[-1]))
        return
    base_plane = 0
    for item, (bit, low, pieces, planes, blocks) in enumerate(items):
        mine = share_bit(bit)
        out, keep = (refs[0], refs[1]) if merge else refs[2 * item : 2 * item + 2]
        columns = kept[item].shape[-1]
        wide = came[item][0].shape[-1]
        for plane in range(planes):
            for begin in range(0, columns, wide):
                at = slice(begin, begin + wide)
                for block in range(blocks // 2):
                    base = block // low * 2 * low + block % low
                    place = (base_plane + plane) * (blocks // 2) + block
                    out[place, :, at] = total(item, plane, base + (1 - mine) * low, at).astype(BF16)
                    keep[base_plane + plane, block, :, at] = total(item, plane, base + mine * low, at)
        if merge:
            base_plane += planes
    if small:
        target = refs[0 if merge else 2 * len(items) - 2]
        target[target.shape[0] - 1] = packed
        refs[-1][...] = held


class Order:
    def __init__(self):
        self.token = ()
        self.weight = 0

    def __call__(self, kernel, outs, args, scratch=(), limit=16, fresh=False, also=(), name=None):
        waits = (*self.token, *also)
        first, tokens = len(args), len(waits)

        def body(*refs):
            kernel(*refs[:first], *refs[first + tokens :])

        place = pltpu.HBM if fresh else pltpu.VMEM
        spaces = [pltpu.HBM if space else pltpu.VMEM for _, _, *space in outs]
        results = pl.pallas_call(
            body,
            out_shape=[space(item[0], item[1]) for space, item in zip(spaces, outs)],
            in_specs=[pl.BlockSpec(memory_space=pl.ANY if fresh else pltpu.VMEM)] * first
            + [pl.BlockSpec(memory_space=pl.ANY)] * tokens,
            out_specs=[pl.BlockSpec(memory_space=pltpu.VMEM)] * len(outs),
            scratch_shapes=list(scratch),
            compiler_params=pltpu.CompilerParams(vmem_limit_bytes=limit * MIB),
            cost_estimate=pl.CostEstimate(
                flops=1 + self.weight * 10**9, bytes_accessed=1, transcendentals=0
            ),
            name=name,
        )(*(pltpu.with_memory_space_constraint(array, place) for array in args), *waits)
        self.token = (pltpu.with_memory_space_constraint(results[-1], spaces[-1]),)
        return results


def gram(call, lay, groups, shares, keeps, name, halves=(True, False)):
    first = groups[0][1][0]
    rows = first.shape[1]
    columns = groups[0][2][0].shape[-1]
    planes = sum(r[0].shape[0] if len(r[0].shape) == 3 else 1 for _, _, r in groups)
    kinds = tuple(kind for kind, _, _ in groups)
    sends = keeps if True in halves else 0
    outs = [((planes // keeps, shares // 2, rows, columns), BF16)] * (keeps * len(halves))
    results = call(
        partial(gram_kernel, lay, kinds, sends, halves),
        outs,
        [array for _, lefts, rights in groups for array in (*lefts, *rights)],
        scratch=[pltpu.VMEM(first.shape, BF16)] * (lay.slices if "plain" in kinds else 0),
        name=name,
    )
    return results[: len(outs) - sends], results[len(outs) - sends :]


def plain_scatter(groups, shares):
    sums = []
    for kind, lefts, rights in groups:
        total = 0.0
        for left, right in zip(lefts, rights):
            if kind == "turned":
                left = left.reshape(-1, left.shape[2]).T
            right = right if len(right.shape) == 3 else right[None]
            total += jnp.einsum("rd,prc->pdc", left, right, preferred_element_type=F32)
        sums.append(total)
    kept = jnp.concatenate(sums, axis=0)
    planes, model, columns = kept.shape
    rows = model // shares
    for bit in range(shares.bit_length() - 1):
        view = kept.reshape(planes, -1, 2, rows, columns)
        mine = share_bit(bit)
        pick = lambda which: lax.dynamic_index_in_dim(view, which, 2, keepdims=False)
        kept = pick(mine) + flip(pick(1 - mine).astype(BF16), shares, bit).astype(F32)
    return kept[:, 0]


def plain_small(vector, shares):
    for bit in range(shares.bit_length() - 1):
        vector = vector + flip(vector, shares, bit)
    return vector + jnp.where(first_norm_rows(vector), swap(vector), 0.0)


def flip_pairs(shares, bit):
    return [(index, index ^ (1 << bit)) for index in range(shares)]


def flip(array, shares, bit):
    return lax.ppermute(array, "dp", flip_pairs(shares, bit))


class Sum:
    def __init__(self, kept, sent, shares, order):
        self.order = list(order)
        self.left = sorted(order, reverse=True)
        self.kept, self.shares = kept, shares
        self.send(sent, 0)

    def send(self, sent, bit):
        self.came = [flip(part, self.shares, bit) for part in sent]

    def next(self):
        planes, blocks = self.kept.shape[:2]
        if not self.order:
            return None, 0, len(self.came), planes, blocks
        bit = self.order.pop(0)
        low = 1 << (len(self.left) - 1 - self.left.index(bit))
        self.left.remove(bit)
        return bit, low, len(self.came), planes, blocks


def stage(call, sums, name, merge=False, small=None, small_args=(), last=()):
    items = tuple(item.next() for item in sums)
    args = [array for item in sums for array in (item.kept, *item.came)]
    rows, columns = sums[0].kept.shape[2:]
    extra = 1 if small else 0
    if last:
        scratch = [pltpu.VMEM(small_args[0].shape, F32)] if small else []
        return call(
            partial(stage_kernel, items, merge, small), list(last), [*args, *small_args], scratch, name=name
        )
    sizes = [(planes, blocks // 2) for _, _, _, planes, blocks in items]
    if merge:
        sizes = [(sum(planes for planes, _ in sizes), sizes[0][1])]
    outs = []
    for place, (planes, blocks) in enumerate(sizes):
        count = planes * blocks + (extra if place == len(sizes) - 1 else 0)
        outs += [((count, rows, columns), BF16), ((planes, blocks, rows, columns), F32)]
    if small:
        outs.append((small_args[0].shape, F32))
    results = call(partial(stage_kernel, items, merge, small), outs, [*args, *small_args], name=name)
    for place, item in enumerate(sums[: len(sizes)]):
        item.kept = results[2 * place + 1]
        item.send([results[2 * place]], items[place][0])
    return results[-1]


def first_norm_rows(vector):
    place = lax.broadcasted_iota(jnp.int32, (vector.shape[0], 1), 0) // 2
    return (place == ROW_GAIN1) | (place == ROW_BIAS1)


def add_small_kernel(own_ref, other_ref, out_ref):
    out_ref[...] = own_ref[...] + other_ref[...]


def small_outputs(vector, units):
    two = lambda place, count=2: vector[2 * place : 2 * place + count].reshape(-1)
    return (
        vector[2 * ROW_QV], vector[2 * ROW_QV + 1], two(ROW_GAIN1), two(ROW_BIAS1), two(ROW_OUT),
        two(ROW_GAIN2), two(ROW_BIAS2), two(ROW_DOWN), two(ROW_UP, units // vector.shape[1]),
    )


def swap(rows):
    return lax.ppermute(rows, "tensor", [(0, 1), (1, 0)])


def local(
    shares, tokens, body_mask, ln1_gain, ln1_bias, w_qkv, b_q, b_v, w_out, b_out, ln2_gain, ln2_bias,
    w_up, b_up, w_down, b_down, cotangent,
):
    slices, seq = body_mask.shape
    rows, model = tokens.shape
    lay = Layout(rows, slices, seq)
    padded, sent = lay.padded, lay.sent
    width = w_qkv.shape[2]
    heads = width // HD
    units = w_up.shape[1]
    steps = shares.bit_length() - 1
    small_rows = 2 * ROW_UP + units // (model // 2)
    small_height = -(-small_rows // SUBLANES) * SUBLANES
    w_qkv = jnp.transpose(w_qkv, (1, 0, 2))
    wide, narrow, tall = ((padded, model), BF16), ((padded, width), BF16), ((padded, units), BF16)
    tuned = steps == 4 and model // shares == 2 * small_height and width == model // 2
    blocks = shares if tuned else 1
    flipped = ((blocks, model // blocks, padded), BF16)
    wide_f, crossing = ((padded, model), F32), ((sent, model), BF16)
    small = ((small_height, model // 2), F32)
    bias_row = pltpu.VMEM((SUBLANES, -(-padded // LANES) * LANES), F32)
    attend_outs = [
        ((sent, width), BF16), wide, narrow, narrow, narrow, ((heads, padded, padded), BF16), narrow
    ]

    call = Order()
    state = {name: [None] * slices for name in (*ATTENDED, *UPPED, *RETURNED, *OTHERS)}
    held = {}
    sums = {}
    result = {}

    def keep(s, names, values):
        for name, value in zip(names, values):
            state[name][s] = value

    def attend(s):
        if s == 0:
            results = call(
                partial(first_attend_kernel, lay),
                attend_outs + [(w_qkv.shape, BF16), (w_out.shape, BF16), (tokens.shape, BF16)],
                (tokens, body_mask, ln1_gain, ln1_bias, w_qkv, b_q, b_v, w_out),
                scratch=[
                    pltpu.VMEM(body_mask.shape, jnp.int32),
                    *[pltpu.VMEM((size,), F32) for size in (model, model, width, width)],
                    bias_row,
                    pltpu.SemaphoreType.DMA((8,)),
                ],
                fresh=True,
                name="attend",
            )
            held["w_qkv"], held["w_out"], held["tokens"] = results[7:]
        else:
            results = call(
                partial(attend_kernel, lay, s),
                attend_outs,
                (held["tokens"], body_mask, ln1_gain, ln1_bias, held["w_qkv"], b_q, b_v),
                scratch=[bias_row],
                name="attend",
            )
        keep(s, ATTENDED, results)
        state["other"][s] = swap(state["crossing"][s])

    def weights():
        half = call(
            half_kernel,
            [((width // 2, model), BF16)],
            (w_out,),
            scratch=[pltpu.SemaphoreType.DMA],
            fresh=True,
            name="half",
        )[0]
        held["near"] = swap(half)
        held["far"] = flip(held["near"], shares, 0)

    def early():
        results = call(
            partial(early_kernel, lay),
            [flipped] * (2 * slices) + [((padded, units), F32)] * slices + [small],
            (cotangent, w_down, *state["normed"]),
            name="early",
        )
        for name, place in (("cot_turned", 0), ("turned", 1), ("active_grad", 2)):
            state[name] = results[place * slices : (place + 1) * slices]
        held["vector"] = results[-1]

    def mlp(s):
        late = s == slices - 1
        results = call(
            partial(mlp_kernel, lay, s),
            [wide_f, flipped, tall, tall, small] + ([] if late else [crossing]),
            (
                held["tokens"], state["mixed"][s], state["other"][s], held["w_out"], held["near"],
                held["far"], b_out, ln2_gain, ln2_bias, w_up, b_up, state["active_grad"][s],
                held["vector"],
            ),
            scratch=[pltpu.VMEM((2, padded, model), F32)],
            name="mlp",
        )
        keep(s, UPPED, results)
        held["vector"] = results[4]
        if not late:
            send_back(s, results[5])

    def send_back(s, back):
        state["back"][s] = back
        state["other"][s] = swap(back)

    def late_back(s):
        args = (state["upper_low"][s], w_up)
        send_back(s, call(partial(back_kernel, lay, s), [crossing], args, name="back")[0])

    def last():
        held["last"] = call(
            partial(last_kernel, lay),
            [((2 * slices, sent, model), BF16)],
            (*state["active"], *state["first_back"], w_down),
            name="last",
        )[0]
        held["last_other"] = swap(held["last"])

    def attend_back(s):
        results = call(
            partial(attend_back_kernel, lay, s),
            [wide_f, wide, ((3, padded, width), BF16), crossing, small],
            (
                *(state[name][s] for name in ("hidden", "back", "other")), cotangent, ln2_gain,
                held["w_out"], *(state[name][s] for name in ("q", "k", "v", "soft")), held["w_qkv"],
                held["tokens"], held["vector"],
            ),
            scratch=[pltpu.VMEM((width, padded), F32)],
            name="attend_back",
        )
        keep(s, RETURNED, results)
        held["vector"] = results[4]
        if s == slices - 1:
            held["vector_other"] = flip(held["vector"], shares, 0)

    def finish():
        result["rows"] = call(
            partial(finish_kernel, lay),
            [((rows, model), F32, True)] * 2,
            (
                held["tokens"], ln1_gain, b_down, held["last"], held["last_other"],
                *state["hidden_grad"], *state["hidden"],
            ),
            name="finish",
        )

    grams = {
        "D": lambda: [("turned", state["cot_turned"], state["active"])],
        "U": lambda: [("turned", state["normed2"], state["upper_low"])],
        "Q": lambda: [
            ("turned", state["turned"], state["qkv_grad"]),
            ("plain", state["hidden_low"], state["mixed"]),
        ],
    }
    near, far = (1, 2, 3), (2, 1, 3)
    share = lambda planes, columns: ((planes, model // shares, columns), F32, True)

    def step_mlp(step):
        sums = [held["D"], held["U"]] if step < 3 else [held["U"], held["D"]][: 5 - step]
        last = [share(1, units), share(1, units)] if step == 4 else ()
        done = stage(call, sums, "sum_mlp_" + "abcd"[step - 1], merge=step == 3, last=last)
        if last:
            result["U"], result["D"] = done

    def step_qkv(step):
        sums = held["Q"] if step < 4 else held["Q"][:1]
        small_kind = {1: "first", 4: "last"}.get(step, "next")
        last = ()
        if step == 4:
            last = [share(3, width), share(1, width)] + [
                ((size,), F32, True)
                for size in (width, width, model, model, model, model, model, model, units)
            ]
        args = (held["vector"], held["vector_other"]) if step == 1 else (held["vector"],)
        done = stage(call, sums, "sum_qkv_" + "abcd"[step - 1], step == 3, small_kind, args, last)
        if last:
            result["Q"], result["O"], *result["small"] = done
        else:
            held["vector"] = done

    for item in ORDER:
        kind, place = item[0], item[1:]
        call.weight = WEIGHT.get(item, 0)
        if kind == "W":
            weights()
        elif kind == "A":
            attend(int(place))
        elif kind == "B":
            mlp(int(place))
        elif kind == "C":
            attend_back(int(place))
        elif kind == "F":
            finish()
        elif kind == "T":
            early()
        elif kind == "R":
            late_back(int(place))
        elif kind == "L":
            last()
        elif kind == "X":
            call(wait_kernel, [((SUBLANES, LANES), F32)], (), also=state["other"][:1], name="wait")
        elif not tuned:
            continue
        elif kind == "Y":
            call(wait_kernel, [((SUBLANES, LANES), F32)], (), also=held["U"].came, name="wait")
        elif kind == "s":
            held["vector"] = call(
                add_small_kernel, [small], [held["vector"], held["vector_other"]], name="add_small"
            )[0]
            held["vector_other"] = swap(held["vector"])
        elif item == "GQ":
            kept, pieces = gram(call, lay, grams["Q"](), shares, 2, "gram_q")
            held["Q"] = [Sum(kept[0], pieces[:1], shares, far), Sum(kept[1], pieces[1:], shares, near)]
        elif kind in "GK":
            halves, name = ((kind == "G",), ("gram_" if kind == "G" else "keep_") + place.lower())
            kept, pieces = gram(call, lay, grams[place](), shares, 1, name, halves)
            if pieces:
                held[place] = Sum(None, pieces, shares, near if place == "U" else far)
            else:
                held[place].kept = kept[0]
        elif kind == "M":
            step_mlp(int(place))
        else:
            step_qkv(int(place))
    if not tuned:
        for name in "DU":
            result[name] = plain_scatter(grams[name](), shares)
        total = plain_scatter(grams["Q"](), shares)
        result["Q"], result["O"] = total[:3], total[3:]
        result["small"] = small_outputs(plain_small(held["vector"], shares), units)

    (
        sum_b_q, sum_b_v, sum_ln1_gain, sum_ln1_bias, sum_b_out, sum_ln2_gain, sum_ln2_bias, sum_b_down,
        sum_b_up,
    ) = result["small"]
    block_out, grad_tokens = result["rows"]
    return (
        block_out,
        grad_tokens,
        sum_ln1_gain,
        sum_ln1_bias,
        jnp.transpose(result["Q"], (1, 0, 2)),
        sum_b_q,
        sum_b_v,
        result["O"][0].T,
        sum_b_out,
        sum_ln2_gain,
        sum_ln2_bias,
        result["U"][0],
        sum_b_up,
        result["D"][0].T,
        sum_b_down,
    )


def solution(mesh):
    return jax.shard_map(
        partial(local, mesh.shape["dp"]),
        mesh=mesh,
        in_specs=(
            P("dp", None),
            P("dp", None),
            P(),
            P(),
            P(None, None, "tensor"),
            P("tensor"),
            P("tensor"),
            P("tensor", None),
            P(),
            P(),
            P(),
            P(None, "tensor"),
            P("tensor"),
            P("tensor", None),
            P(),
            P("dp", None),
        ),
        out_specs=(
            P("dp", None),
            P("dp", None),
            P(),
            P(),
            P("dp", None, "tensor"),
            P("tensor"),
            P("tensor"),
            P("tensor", "dp"),
            P(),
            P(),
            P(),
            P("dp", "tensor"),
            P("tensor"),
            P("tensor", "dp"),
            P(),
        ),
        check_vma=False,
    )
```
